32 devices in a mesh: groups: 2 (over x), seq: 16 (over z, y, core).
Axes of the slice: x: 2, y: 2, z: 4, core: 2. Of those that a mesh axis runs over, the one named last changes fastest.
Arguments:
- mixer_input: bfloat16 [4096, 6144], P(('groups', 'seq')), parts along dimension 0, may hold values from -6 to 6
- gate_input: bfloat16 [4096, 4096], P(('groups', 'seq')), parts along dimension 0, may hold values from -6 to 6
- step_raw: bfloat16 [4096, 64], P(('groups', 'seq')), parts along dimension 0, may hold values from -4 to 12, as said below
- conv_weight: bfloat16 [4, 6144], replicated, may hold values from -3 to 3
- conv_bias: float32 [6144], replicated, may hold values from -0.7 to -0.3
- step_bias: float32 [128], P('groups'), parts along dimension 0, may hold values from -13 to -2
- decay_log: float32 [128], P('groups'), parts along dimension 0, may hold values from -0.4 to 0.4
- skip_gain: float32 [64], replicated, may hold values from 0.5 to 1.5
- norm_gain: float32 [4096], replicated, may hold values from 0.5 to 1.5
Outputs:
- mixer_out: bfloat16 [4096, 4096], P(('groups', 'seq')), parts along dimension 0
The draws below stay inside these ranges and needn't reach their ends.
There are 2 independent parts, one for each index of `groups`. The reference program is written for one: setup_inputs(seed, part) draws one part's arguments, and reference() takes and returns one part's arrays. A program takes and returns all parts, laid end to end along the dimension named above; an argument that names none is the same for every part. Nothing has to cross between parts.
Inputs may be any that keep to these rules, and one draw needn't show every extreme that they name: `step_raw`: raw step sizes; each head's step sizes change by bounded factors between positions.
All inputs are finite; a program needn't handle non-finite values.
Results may differ from the reference program's by a relative error of at most 0.006.
Values may be sent and summed in bfloat16 or wider, within the bound.
No kernel may reach another device: no remote copies, remote signals or barrier semaphores. Data moves between devices by JAX's collectives and lax.ppermute only.
A program may use at most 64 MiB of HBM per device.

```python
import jax
import jax.numpy as jnp
from jax import lax

HEADS = 64
HEAD_DIM = 64
STATE = 128
HEAD_GROUPS = 8
CONV = 4
SPAN = 128
TOK_DEV = 128
TOKENS = 2048
HI = 4096
CH = 6144


def head_laws(key, fast_share):
    picker = jax.random.uniform(jax.random.fold_in(key, 11), (HEADS,), jnp.float32)
    fast_heads = picker < fast_share
    decay_magnitude = jnp.exp(jax.random.uniform(jax.random.fold_in(key, 12), (HEADS,), jnp.float32, jnp.log(0.7), jnp.log(1.4)))
    slow_rate = jnp.exp(jax.random.uniform(jax.random.fold_in(key, 13), (HEADS,), jnp.float32, jnp.log(0.6), jnp.log(2.0))) / TOKENS
    fast_rate = jnp.exp(jax.random.uniform(jax.random.fold_in(key, 14), (HEADS,), jnp.float32, jnp.log(0.02), jnp.log(0.035)))
    typical = jnp.where(fast_heads, fast_rate, slow_rate) / decay_magnitude
    return (decay_magnitude, typical)


def draw_decay_log(key, part):
    decay_magnitude, typical = head_laws(key, 0.5)
    return jnp.log(decay_magnitude)


def draw_step_bias(key, part):
    decay_magnitude, typical = head_laws(key, 0.5)
    return jnp.log(jnp.expm1(typical))


def draw_step_raw(key, part):
    decay_magnitude, typical = head_laws(key, 0.5)
    key = jax.random.fold_in(key, 5)
    per_head_bias = jnp.log(jnp.expm1(typical))
    noise = 0.4 * jax.random.normal(jax.random.fold_in(key, 1), (TOKENS, HEADS), jnp.float32)
    offsets = jax.random.uniform(jax.random.fold_in(key, 2), (TOKENS // TOK_DEV, HEADS), jnp.float32, -0.7, 0.7)
    mixer_result = noise + jnp.repeat(offsets, TOK_DEV, axis=0)
    token_slots = jax.random.randint(jax.random.fold_in(key, 3), (3,), 0, TOKENS)
    decayed_fraction = jax.random.uniform(jax.random.fold_in(key, 4), (3, HEADS), jnp.float32, 0.2, 0.5)
    step_width_bias = -jnp.log1p(-decayed_fraction) / decay_magnitude[None, :]
    step_width_logit = jnp.log(jnp.expm1(step_width_bias)) - per_head_bias[None, :]
    token_position = jnp.arange(TOKENS)[:, None]
    for step_width in range(3):
        mixer_result = jnp.where(token_position == token_slots[step_width], step_width_logit[step_width][None, :], mixer_result)
    return mixer_result.astype(jnp.bfloat16)


def shard_levels(key, shape, shards, smallest, top_value):
    def one(axis_at, shards_of):
        steps = jax.random.uniform(jax.random.fold_in(jax.random.fold_in(key, 6), axis_at), (shards_of,), jnp.float32, smallest / len(shards), top_value / len(shards))
        return jnp.repeat(jnp.exp(steps), shape[axis_at] // shards_of).reshape((-1,) + (1,) * (len(shape) - axis_at - 1))

    factor_of = one(*shards[0])
    for cut in shards[1:]:
        factor_of = factor_of * one(*cut)
    return factor_of


def bell_draw(stream_key, shape, scale, reach, cuts=(), kind=jnp.bfloat16):
    drawn = scale * jax.random.normal(stream_key, shape, jnp.float32)
    if cuts:
        drawn = drawn * shard_levels(stream_key, shape, cuts, -0.22, 0.18)
    return jnp.clip(drawn, -reach, reach).astype(kind)


def setup_inputs(seed: int = 0, part: int = 0) -> dict:
    seeds = jax.random.split(jax.random.key(seed), 10)
    own_keys = jax.random.split(jax.random.fold_in(seeds[9], part), 10)
    mixer_input = bell_draw(own_keys[0], (TOKENS, CH), 1.0, 6.0, ((0, 16),))
    gate_input = bell_draw(own_keys[1], (TOKENS, HI), 1.0, 6.0, ((0, 16),))
    step_raw = draw_step_raw(jax.random.fold_in(jax.random.fold_in(seeds[9], part), 71), part)
    conv_weight = bell_draw(seeds[3], (CONV, CH), CONV ** -0.5, 3.0)
    conv_bias = jnp.clip(jax.random.uniform(seeds[4], (CH,), jnp.float32, -0.7, -0.3), -0.7, -0.3)
    step_bias = draw_step_bias(jax.random.fold_in(jax.random.fold_in(seeds[9], part), 71), part)
    decay_log = draw_decay_log(jax.random.fold_in(jax.random.fold_in(seeds[9], part), 71), part)
    skip_gain = jnp.clip(jax.random.uniform(seeds[7], (HEADS,), jnp.float32, 0.5, 1.5), 0.5, 1.5)
    norm_gain = jnp.clip(1.0 + 0.1 * jax.random.normal(seeds[8], (HI,), jnp.float32), 0.5, 1.5)
    return dict(mixer_input=mixer_input, gate_input=gate_input, step_raw=step_raw, conv_weight=conv_weight, conv_bias=conv_bias, step_bias=step_bias, decay_log=decay_log, skip_gain=skip_gain, norm_gain=norm_gain)


def rounded(tensor):
    return lax.optimization_barrier(tensor.astype(jnp.bfloat16)).astype(jnp.float32)

def reference(mixer_input, gate_input, step_raw, conv_weight, conv_bias, step_bias, decay_log, skip_gain, norm_gain):
    inner_width = HEADS * HEAD_DIM
    per_group = HEADS // HEAD_GROUPS
    span_count = TOKENS // SPAN
    channels = mixer_input.shape[1]
    padded = jnp.concatenate([jnp.zeros((CONV - 1, channels), mixer_input.dtype), mixer_input], axis=0)
    activation = jnp.zeros((TOKENS, channels), jnp.float32) + conv_bias[None, :].astype(jnp.float32)
    for offset in range(CONV):
        activation = activation + conv_weight[offset][None, :].astype(jnp.float32) * padded[offset:offset + TOKENS].astype(jnp.float32)
    convolved = jax.nn.silu(activation).astype(jnp.bfloat16)
    values = convolved[:, :inner_width].reshape(span_count, SPAN, HEAD_GROUPS, per_group, HEAD_DIM)
    write_keys = convolved[:, inner_width:inner_width + HEAD_GROUPS * STATE].reshape(span_count, SPAN, HEAD_GROUPS, STATE)
    read_keys = convolved[:, inner_width + HEAD_GROUPS * STATE:].reshape(span_count, SPAN, HEAD_GROUPS, STATE)
    step_sizes = jax.nn.softplus(step_raw.astype(jnp.float32) + step_bias[None, :]).reshape(span_count, SPAN, HEAD_GROUPS, per_group)
    decay_rates = -jnp.exp(decay_log).reshape(HEAD_GROUPS, per_group)
    skip_terms = skip_gain.reshape(HEAD_GROUPS, per_group)
    gate_blocks = gate_input.reshape(span_count, SPAN, inner_width)
    causal = lax.broadcasted_iota(jnp.int32, (SPAN, SPAN), 0) >= lax.broadcasted_iota(jnp.int32, (SPAN, SPAN), 1)

    def advance(carry_state, pieces):
        block_values, block_writes, block_reads, block_steps, block_gate = pieces
        cumulative = jnp.cumsum(block_steps * decay_rates[None], axis=0)
        totals = cumulative[-1]
        scores = jnp.einsum('qgk,sgk->gqs', block_reads.astype(jnp.float32), block_writes.astype(jnp.float32))
        along_time = jnp.transpose(cumulative, (1, 2, 0))
        log_gap = along_time[:, :, :, None] - along_time[:, :, None, :]
        decays = jnp.exp(jnp.where(causal, log_gap, 0.0))
        steps_last = jnp.transpose(block_steps, (1, 2, 0))
        weights = jnp.where(causal, scores[:, None] * decays * steps_last[:, :, None, :], 0.0)
        inside = jnp.einsum('ghqs,sghp->qghp', rounded(weights), block_values.astype(jnp.float32))
        tail_weights = jnp.exp(totals[None] - cumulative) * block_steps
        written = rounded(block_writes[:, :, None, :].astype(jnp.float32) * tail_weights[..., None])
        increment = jnp.einsum('sghp,sghk->ghpk', block_values.astype(jnp.float32), written)
        carried_part = jnp.einsum('qgk,ghpk->qghp', block_reads.astype(jnp.float32), rounded(carry_state))
        mixed = inside + carried_part * jnp.exp(cumulative)[..., None] + skip_terms[None, :, :, None] * block_values.astype(jnp.float32)
        gated_rows = mixed.reshape(SPAN, inner_width) * jax.nn.silu(block_gate.astype(jnp.float32))
        grouped = gated_rows.reshape(SPAN, HEAD_GROUPS, inner_width // HEAD_GROUPS)
        inverse_rms = lax.rsqrt(lax.optimization_barrier(jnp.mean(grouped * grouped, axis=-1, keepdims=True)) + 1e-05)
        normed = (grouped * inverse_rms).reshape(SPAN, inner_width) * norm_gain[None, :]
        next_state = jnp.exp(totals)[:, :, None, None] * carry_state + increment
        return (next_state, normed.astype(jnp.bfloat16))
    initial = jnp.zeros((HEAD_GROUPS, per_group, HEAD_DIM, STATE), jnp.float32)
    _, blocks = lax.scan(advance, initial, (values, write_keys, read_keys, step_sizes, gate_blocks))
    return blocks.reshape(TOKENS, inner_width)
```

```python
import functools

import jax
import jax.numpy as jnp
from jax import lax
from jax.experimental import pallas as pl
from jax.experimental.pallas import tpu as pltpu
from jax.sharding import PartitionSpec as P

HEADS = 64
HEAD_DIM = 64
STATE = 128
GROUPS = 8
PER_GROUP = HEADS // GROUPS
GROUP_COLS = PER_GROUP * HEAD_DIM
INNER = HEADS * HEAD_DIM
KEYS = GROUPS * STATE
CONV_COLS = INNER + 2 * KEYS
SPAN = 128
LANES = 128
TILES = GROUP_COLS // LANES
PARTS = 2
PART_GROUPS = GROUPS // PARTS
HALF_GROUPS = PART_GROUPS // 2
QUARTER_GROUPS = HALF_GROUPS // 2
HALF_TILES = HALF_GROUPS * TILES
QUARTER_TILES = QUARTER_GROUPS * TILES
HALF_ROWS = HALF_TILES * STATE
QUARTER_ROWS = QUARTER_TILES * STATE
F32 = jnp.float32
BF16 = jnp.bfloat16
VMEM_LIMIT = 24 * 1024 * 1024


def extra_rows(tiles):
    return -(-2 * tiles // 16) * 16


def decay_rows(tiles):
    return -(-tiles // 8) * 8


def call(body, outs, *args, scratch=(), cost=None):
    specs = [pl.BlockSpec(memory_space=pltpu.VMEM) for _ in args]
    flops, transcendentals = cost or (100000, 0)
    moved = sum(a.size * a.dtype.itemsize for a in args) + sum(
        o[0][0] * o[0][1] * jnp.dtype(o[1]).itemsize for o in outs
    )
    return pl.pallas_call(
        body,
        out_shape=[jax.ShapeDtypeStruct(shape, kind) for shape, kind in outs],
        in_specs=specs,
        out_specs=[pl.BlockSpec(memory_space=pltpu.VMEM) for _ in outs],
        scratch_shapes=list(scratch),
        compiler_params=pltpu.CompilerParams(vmem_limit_bytes=VMEM_LIMIT),
        cost_estimate=pl.CostEstimate(
            flops=flops, bytes_accessed=moved, transcendentals=transcendentals
        ),
    )(*args)


def dot(a, b, dims=((1,), (0,))):
    return lax.dot_general(a, b, (dims, ((), ())), preferred_element_type=F32)


def silu(v):
    return v / (1.0 + jnp.exp(-v))


def pieces(v, count):
    found = []
    for _ in range(count):
        piece = v.astype(BF16)
        found.append(piece)
        v = v - piece.astype(F32)
    return found


def spread(group):
    row = lax.broadcasted_iota(jnp.int32, (2 * HEADS, GROUP_COLS), 0)
    lane = lax.broadcasted_iota(jnp.int32, (2 * HEADS, GROUP_COLS), 1)
    head = group * PER_GROUP + lane // HEAD_DIM
    return ((row == head) | (row == head + HEADS)).astype(BF16)


def columns(group, width, start=0):
    return pl.ds(pl.multiple_of(start + group * width, LANES), width)


def convolve_into(rows, padded, weight_ref, bias_ref, cols):
    total = bias_ref[:, cols]
    for tap in range(4):
        total = total + weight_ref[tap : tap + 1, cols].astype(F32) * padded[5 + tap : 5 + tap + rows, :]
    return silu(total).astype(BF16)


def prepare(x, step, decay_log, weight, bias, conv, both, both_t, tail_pair, carry_pair, total_pair, padded):
    @pl.loop(0, CONV_COLS // 512)
    def _(i):
        cols = columns(i, 512)
        padded[0:8, :] = jnp.zeros((8, 512), F32)
        padded[8 : 8 + SPAN, :] = x[:, cols].astype(F32)
        conv[:, cols] = convolve_into(SPAN, padded, weight, bias, cols)

    sizes = step[...]
    log_decay = sizes * -jnp.exp(decay_log[...])
    row = lax.broadcasted_iota(jnp.int32, (SPAN, SPAN), 0)
    lane = lax.broadcasted_iota(jnp.int32, (SPAN, SPAN), 1)
    lower = (row >= lane).astype(BF16)
    cumulative = sum(dot(lower, piece) for piece in pieces(log_decay, 3))
    total = cumulative[SPAN - 1 : SPAN, :]
    tail = jnp.exp(total - cumulative) * sizes
    joined = jnp.concatenate([cumulative, sizes], axis=1)
    both[...] = joined
    both_t[...] = joined.T
    tail_pair[...] = jnp.concatenate(pieces(tail, 2), axis=1)
    carry_pair[...] = jnp.concatenate(pieces(jnp.exp(cumulative), 2), axis=1)
    total_pair[...] = jnp.concatenate(
        pieces(jnp.broadcast_to(jnp.exp(total), (16, HEADS)), 2), axis=1
    )


def load_fixed(conv, fix, cols):
    return jnp.concatenate([fix[:, cols], conv[16:, cols]], axis=0)


def put_decays(send, tiles, decays):
    high = [d.astype(BF16).astype(F32) for d in decays]
    low = [d - h for d, h in zip(decays, high)]
    rows = high + low
    spare = extra_rows(tiles) - len(rows)
    block = jnp.concatenate(rows + [jnp.zeros((spare, LANES), F32)] * (spare > 0), axis=0)
    send[tiles * STATE : tiles * STATE + extra_rows(tiles), :] = block.astype(BF16)


def increments(part, *refs):
    first = part == 0
    if first:
        (x, halo, weight, bias, conv, tail_pair, total_pair, send, keep, keep_decay, fix, padded) = refs

        @pl.loop(0, CONV_COLS // 512)
        def _(i):
            cols = columns(i, 512)
            padded[0:8, :] = jnp.zeros((8, 512), F32)
            padded[5:8, :] = halo[:, cols].astype(F32)
            padded[8:24, :] = x[0:16, cols].astype(F32)
            fix[:, cols] = convolve_into(16, padded, weight, bias, cols)
    else:
        conv, fix, tail_pair, total_pair, send, keep, keep_decay = refs
    core = lax.axis_index("seq") & 1
    for target, side in ((send, 1 - core), (keep, core)):
        decays = []
        for j in range(HALF_GROUPS):
            group = part * PART_GROUPS + side * HALF_GROUPS + j
            to_channels = spread(group)
            scale = dot(tail_pair[...], to_channels)
            values = load_fixed(conv, fix, columns(group, GROUP_COLS)).astype(F32)
            keys = load_fixed(conv, fix, columns(group, STATE, INNER))
            grown = dot(keys, (values * scale).astype(BF16), ((0,), (0,)))
            decay = dot(total_pair[...], to_channels)
            for t in range(TILES):
                at = (j * TILES + t) * STATE
                target[at : at + STATE, :] = grown[:, t * LANES : (t + 1) * LANES].astype(target.dtype)
                decays.append(decay[0:1, t * LANES : (t + 1) * LANES])
        if target is send:
            put_decays(send, HALF_TILES, decays)
        else:
            for t, d in enumerate(decays):
                keep_decay[t : t + 1, :] = d


def tile_rows(t):
    return pl.ds(pl.multiple_of(t * STATE, STATE), STATE)


def received_decays(recv, tiles, scratch):
    rows = recv[tiles * STATE : tiles * STATE + extra_rows(tiles), :].astype(F32)
    scratch[0:tiles, :] = rows[0:tiles] + rows[tiles : 2 * tiles]


def join_cores(keep, keep_decay, recv, send, own, own_decay, other):
    me = lax.axis_index("seq")
    first = (me & 1) == 0
    y = (me >> 1) & 1
    received_decays(recv, HALF_TILES, other)

    def joined(t):
        mine, theirs = keep[tile_rows(t), :], recv[tile_rows(t), :].astype(F32)
        decay_mine, decay_theirs = keep_decay[pl.ds(t, 1), :], other[pl.ds(t, 1), :]
        early, late = jnp.where(first, mine, theirs), jnp.where(first, theirs, mine)
        return jnp.where(first, decay_theirs, decay_mine) * early + late, decay_mine * decay_theirs

    decays = []
    for t in range(QUARTER_TILES):
        state, decay = joined((1 - y) * QUARTER_TILES + t)
        send[t * STATE : (t + 1) * STATE, :] = state.astype(BF16)
        decays.append(decay)
    put_decays(send, QUARTER_TILES, decays)
    for t in range(QUARTER_TILES):
        state, decay = joined(y * QUARTER_TILES + t)
        own[t * STATE : (t + 1) * STATE, :] = state
        own_decay[t : t + 1, :] = decay


def join_pair(bit, carried, last, *refs):
    state, decay, recv = refs[:3]
    refs = refs[3:]
    if carried:
        before, before_decay = refs[:2]
        refs = refs[2:]
    send, new_state, new_decay = refs[:3]
    refs = refs[3:]
    if bit >= 2:
        new_before, new_before_decay = refs[:2]
        refs = refs[2:]
    (other,) = refs
    upper = ((lax.axis_index("seq") >> bit) & 1) == 1
    received_decays(recv, QUARTER_TILES, other)
    decays = []
    for t in range(QUARTER_TILES):
        rows = slice(t * STATE, (t + 1) * STATE)
        mine, theirs = state[rows, :], recv[rows, :].astype(F32)
        d_mine, d_theirs = decay[t : t + 1, :], other[t : t + 1, :]
        early, late = jnp.where(upper, theirs, mine), jnp.where(upper, mine, theirs)
        total = jnp.where(upper, d_mine, d_theirs) * early + late
        new_state[rows, :] = total
        send[rows, :] = total.astype(BF16)
        new_decay[t : t + 1, :] = d_mine * d_theirs
        decays.append(d_mine * d_theirs)
        if bit >= 2:
            if carried:
                b, bd = before[rows, :], before_decay[t : t + 1, :]
                new_before[rows, :] = jnp.where(upper, b + bd * theirs, b)
                new_before_decay[t : t + 1, :] = jnp.where(upper, bd * d_theirs, bd)
            else:
                new_before[rows, :] = jnp.where(upper, theirs, 0.0)
                new_before_decay[t : t + 1, :] = jnp.where(upper, d_theirs, 1.0)
    put_decays(send, QUARTER_TILES, decays)


def to_planes(bit, carried, *refs):
    recv = refs[0]
    refs = refs[1:]
    if carried:
        before, before_decay = refs[:2]
        refs = refs[2:]
    own, own_decay, recv_pair, send, start, other = refs
    me = lax.axis_index("seq")
    upper = ((me >> bit) & 1) == 1
    y = ((me >> 1) & 1) == 1
    received_decays(recv_pair, QUARTER_TILES, other)
    for t in range(QUARTER_TILES):
        rows = slice(t * STATE, (t + 1) * STATE)
        theirs = recv[rows, :].astype(F32)
        if carried:
            b = before[rows, :]
            plane = jnp.where(upper, b + before_decay[t : t + 1, :] * theirs, b)
        else:
            plane = jnp.where(upper, theirs, 0.0)
        d = jnp.where(y, other[t : t + 1, :], own_decay[t : t + 1, :])
        grown = jnp.where(y, recv_pair[rows, :].astype(F32), own[rows, :])
        later = d * plane + grown
        send[rows, :] = jnp.where(y, plane, later).astype(BF16)
        start[rows, :] = jnp.where(y, later, plane)


def to_cores(start, recv_start, keep, keep_decay, recv, send, own, other):
    me = lax.axis_index("seq")
    first = (me & 1) == 0
    y = (me >> 1) & 1
    received_decays(recv, HALF_TILES, other)
    for side in range(2):
        for t in range(QUARTER_TILES):
            rows = slice(t * STATE, (t + 1) * STATE)
            at = (y if side == 0 else 1 - y) * QUARTER_TILES + t
            chip = start[rows, :] if side == 0 else recv_start[rows, :].astype(F32)
            d = jnp.where(first, keep_decay[pl.ds(at, 1), :], other[pl.ds(at, 1), :])
            grown = jnp.where(first, keep[tile_rows(at), :], recv[tile_rows(at), :].astype(F32))
            later = d * chip + grown
            send[tile_rows(at), :] = jnp.where(first, later, chip).astype(BF16)
            own[tile_rows(at), :] = jnp.where(first, chip, later).astype(BF16)


def inside(conv, fix, both, both_t, carry_pair, gate, skip, base, slope):
    row = lax.broadcasted_iota(jnp.int32, (SPAN, SPAN), 0)
    lane = lax.broadcasted_iota(jnp.int32, (SPAN, SPAN), 1)
    causal = row >= lane
    for group in range(GROUPS):
        cols = slice(group * GROUP_COLS, (group + 1) * GROUP_COLS)
        values = load_fixed(conv, fix, cols)
        writes = load_fixed(conv, fix, slice(INNER + group * STATE, INNER + (group + 1) * STATE))
        reads = load_fixed(
            conv, fix, slice(INNER + KEYS + group * STATE, INNER + KEYS + (group + 1) * STATE)
        )
        scores = dot(reads, writes, ((1,), (1,)))
        found = []
        for h in range(group * PER_GROUP, (group + 1) * PER_GROUP):
            gap = both[:, h : h + 1] - both_t[h : h + 1, :]
            weights = scores * jnp.exp(jnp.where(causal, gap, -jnp.inf)) * both_t[HEADS + h : HEADS + h + 1, :]
            at = (h - group * PER_GROUP) * HEAD_DIM
            found.append(dot(weights.astype(BF16), values[:, at : at + HEAD_DIM]))
        within = jnp.concatenate(found, axis=1)
        opened = silu(gate[:, cols].astype(F32))
        base[:, cols] = (within + skip[:, cols] * values.astype(F32)) * opened
        slope[:, cols] = dot(carry_pair[...], spread(group)) * opened


def finish(part, *refs):
    conv, fix, own, recv, base, slope, gain = refs[:7]
    out = refs[-1]
    core = lax.axis_index("seq") & 1
    for source, side in ((own, core), (recv, 1 - core)):
        for j in range(HALF_GROUPS):
            group = part * PART_GROUPS + side * HALF_GROUPS + j
            cols = columns(group, GROUP_COLS)
            reads = load_fixed(conv, fix, columns(group, STATE, INNER + KEYS))
            starts = jnp.concatenate(
                [source[(j * TILES + t) * STATE : (j * TILES + t + 1) * STATE, :] for t in range(TILES)], axis=1
            )
            gated = base[:, cols] + slope[:, cols] * dot(reads, starts)
            mean = jnp.mean(gated * gated, axis=1, keepdims=True)
            local = columns(side * HALF_GROUPS + j, GROUP_COLS)
            out[:, local] = (gated * lax.rsqrt(mean + 1e-5) * gain[:, cols]).astype(BF16)


def shards(mixer_input, gate_input, step_raw, conv_weight, conv_bias, step_bias, decay_log, skip_gain, norm_gain):
    devices = lax.axis_size("seq")
    bits = devices.bit_length() - 1

    def across(value, bit):
        return lax.ppermute(value, "seq", [(i, i ^ (1 << bit)) for i in range(devices)])

    halo = lax.ppermute(mixer_input[SPAN - 3 :], "seq", [(i, i + 1) for i in range(devices - 1)])
    step = jax.nn.softplus(step_raw.astype(F32) + step_bias[None, :])
    bias = conv_bias[None, :]
    skip = jnp.broadcast_to(skip_gain[:, None], (HEADS, HEAD_DIM)).reshape(1, INNER)
    conv, both, both_t, tail_pair, carry_pair, total_pair = call(
        prepare,
        [
            ((SPAN, CONV_COLS), BF16),
            ((SPAN, 2 * HEADS), F32),
            ((2 * HEADS, SPAN), F32),
            ((SPAN, 2 * HEADS), BF16),
            ((SPAN, 2 * HEADS), BF16),
            ((16, 2 * HEADS), BF16),
        ],
        mixer_input, step, decay_log[None, :], conv_weight, bias,
        scratch=[pltpu.VMEM((8 + SPAN, 512), F32)],
    )
    half_send = ((HALF_ROWS + extra_rows(HALF_TILES), LANES), BF16)
    quarter_send = ((QUARTER_ROWS + extra_rows(QUARTER_TILES), LANES), BF16)
    quarter = ((QUARTER_ROWS, LANES), F32)
    quarter_decay = ((decay_rows(QUARTER_TILES), LANES), F32)
    half_keep = [half_send, ((HALF_ROWS, LANES), F32), ((decay_rows(HALF_TILES), LANES), F32)]
    half_scratch = [pltpu.VMEM((decay_rows(HALF_TILES), LANES), F32)]
    quarter_scratch = [pltpu.VMEM((decay_rows(QUARTER_TILES), LANES), F32)]
    grown = []
    fix = None
    for part in range(PARTS):
        if part == 0:
            send, keep, keep_decay, fix = call(
                functools.partial(increments, part), half_keep + [((16, CONV_COLS), BF16)],
                mixer_input, halo, conv_weight, bias, conv, tail_pair, total_pair,
                scratch=[pltpu.VMEM((24, 512), F32)],
            )
        else:
            send, keep, keep_decay = call(
                functools.partial(increments, part), half_keep, conv, fix, tail_pair, total_pair
            )
        grown.append((send, keep, keep_decay))
    starts = []
    for send, keep, keep_decay in grown:
        recv = across(send, 0)
        send_pair, own, own_decay = call(
            join_cores, [quarter_send, quarter, quarter_decay], keep, keep_decay, recv, scratch=half_scratch
        )
        recv_pair = across(send_pair, 1)
        send_plane, state, decay = call(
            functools.partial(join_pair, 1, False, False), [quarter_send, quarter, quarter_decay],
            own, own_decay, recv_pair, scratch=quarter_scratch,
        )
        carried = ()
        for bit in range(2, bits - 1):
            outs = call(
                functools.partial(join_pair, bit, bool(carried), False),
                [quarter_send, quarter, quarter_decay, quarter, quarter_decay],
                state, decay, across(send_plane, bit), *carried, scratch=quarter_scratch,
            )
            send_plane, state, decay = outs[:3]
            carried = tuple(outs[3:])
        send_start, start = call(
            functools.partial(to_planes, bits - 1, bool(carried)), [((QUARTER_ROWS, LANES), BF16), quarter],
            across(send_plane, bits - 1), *carried, own, own_decay, recv_pair, scratch=quarter_scratch,
        )
        send_core, own_start = call(
            to_cores, [((HALF_ROWS, LANES), BF16)] * 2,
            start, across(send_start, 1), keep, keep_decay, recv, scratch=half_scratch,
        )
        starts.append((own_start, across(send_core, 0)))
    base, slope = call(
        inside, [((SPAN, INNER), F32)] * 2,
        conv, fix, both, both_t, carry_pair, gate_input, skip,
        cost=(2 * 64 * 128 * 128 * 64, 64 * 128 * 128),
    )
    gain = norm_gain[None, :]
    finished = [
        call(
            functools.partial(finish, part), [((SPAN, INNER // PARTS), BF16)],
            conv, fix, own_start, recv_start, base, slope, gain,
        )[0]
        for part, (own_start, recv_start) in enumerate(starts)
    ]
    return jnp.concatenate(finished, axis=1)


def solution(mesh):
    in_specs = (
        P(("groups", "seq"), None),
        P(("groups", "seq"), None),
        P(("groups", "seq"), None),
        P(),
        P(),
        P("groups"),
        P("groups"),
        P(),
        P(),
    )
    return jax.shard_map(
        shards, mesh=mesh, in_specs=in_specs, out_specs=P(("groups", "seq"), None), check_vma=False
    )
```

```python
import functools

import jax
import jax.numpy as jnp
from jax import lax
from jax.experimental import pallas as pl
from jax.experimental.pallas import tpu as pltpu
from jax.sharding import PartitionSpec as P

HEADS = 64
HEAD_DIM = 64
STATE = 128
GROUPS = 8
PER_GROUP = HEADS // GROUPS
GROUP_COLS = PER_GROUP * HEAD_DIM
INNER = HEADS * HEAD_DIM
KEYS = GROUPS * STATE
CONV_COLS = INNER + 2 * KEYS
SPAN = 128
LANES = 128
TILES = GROUP_COLS // LANES
PARTS = 2
PART_GROUPS = GROUPS // PARTS
HALF_GROUPS = PART_GROUPS // 2
QUARTER_GROUPS = HALF_GROUPS // 2
HALF_TILES = HALF_GROUPS * TILES
QUARTER_TILES = QUARTER_GROUPS * TILES
HALF_ROWS = HALF_TILES * STATE
QUARTER_ROWS = QUARTER_TILES * STATE
F32 = jnp.float32
BF16 = jnp.bfloat16
VMEM_LIMIT = 24 * 1024 * 1024


def extra_rows(tiles):
    return -(-2 * tiles // 16) * 16


def decay_rows(tiles):
    return -(-tiles // 8) * 8


def call(body, outs, *args, after=(), hbm=(), aliases=None, scratch=()):
    count = len(args)
    args = [pltpu.with_memory_space_constraint(a, pltpu.HBM) if i in hbm else a for i, a in enumerate(args)]
    specs = [pl.BlockSpec(memory_space=pltpu.HBM if i in hbm else pltpu.VMEM) for i in range(count)]
    specs += [pl.BlockSpec(memory_space=pl.ANY) for _ in after]

    def kernel(*refs):
        body(*refs[:count], *refs[count + len(after) :])

    return pl.pallas_call(
        kernel,
        out_shape=[space(shape, kind) for shape, kind, space in outs],
        in_specs=specs,
        out_specs=[pl.BlockSpec(memory_space=space) for _, _, space in outs],
        scratch_shapes=list(scratch),
        input_output_aliases=aliases or {},
        compiler_params=pltpu.CompilerParams(vmem_limit_bytes=VMEM_LIMIT),
    )(*args, *after)


def vmem(rows, cols, kind):
    return ((rows, cols), kind, pltpu.VMEM)


def dot(a, b, dims=((1,), (0,))):
    return lax.dot_general(a, b, (dims, ((), ())), preferred_element_type=F32)


def silu(v):
    return v / (1.0 + jnp.exp(-v))


def pieces(v, count):
    found = []
    for _ in range(count):
        piece = v.astype(BF16)
        found.append(piece)
        v = v - piece.astype(F32)
    return found


def spread(group):
    row = lax.broadcasted_iota(jnp.int32, (2 * HEADS, GROUP_COLS), 0)
    lane = lax.broadcasted_iota(jnp.int32, (2 * HEADS, GROUP_COLS), 1)
    head = group * PER_GROUP + lane // HEAD_DIM
    return ((row == head) | (row == head + HEADS)).astype(BF16)


def columns(group, width, start=0):
    return pl.ds(pl.multiple_of(start + group * width, LANES), width)


def convolve_into(rows, padded, weight_ref, bias_ref, cols):
    total = bias_ref[:, cols]
    for tap in range(4):
        total = total + weight_ref[tap : tap + 1, cols].astype(F32) * padded[5 + tap : 5 + tap + rows, :]
    return silu(total).astype(BF16)


def accurate_log1p(u):
    w = 1.0 + u
    return jnp.where(w == 1.0, u, jnp.log(w) * (u / jnp.where(w == 1.0, 1.0, w - 1.0)))


def part_columns(part):
    return (
        (part * PART_GROUPS * GROUP_COLS, PART_GROUPS * GROUP_COLS),
        (INNER + part * PART_GROUPS * STATE, PART_GROUPS * STATE),
    )


def convolve_part(source, halo, weight, bias, padded, spans, outs, rows=SPAN):
    for (start, width), out in zip(spans, outs):

        @pl.loop(0, width // 512)
        def _(i, start=start, out=out):
            cols = columns(i, 512, start)
            padded[0:8, :] = jnp.zeros((8, 512), F32)
            if halo is not None:
                padded[5:8, :] = halo[:, cols].astype(F32)
            padded[8 : 8 + rows, :] = source[0:rows, cols].astype(F32)
            out[0:rows, columns(i, 512)] = convolve_into(rows, padded, weight, bias, cols)


def prepare(
    x, raw_t, step_bias, decay_log, skip, weight_in, bias_in,
    held, weight, bias, values, keys, both, both_t, tail_pair, carry_pair, row_pair,
    padded, raw_here, small, sems,
):
    first = part_columns(0)
    pieces_of_x = list(first)
    at = 0
    for start, width in sorted(first) + [(CONV_COLS, 0)]:
        if start > at:
            pieces_of_x.append((at, start - at))
        at = start + width
    copies = [
        pltpu.make_async_copy(raw_t, raw_here, sems.at[0]),
        pltpu.make_async_copy(step_bias, small.at[0:1], sems.at[1]),
        pltpu.make_async_copy(decay_log, small.at[8:9], sems.at[2]),
        pltpu.make_async_copy(skip, small.at[16:17], sems.at[3]),
        pltpu.make_async_copy(weight_in, weight, sems.at[4]),
        pltpu.make_async_copy(bias_in, bias, sems.at[5]),
    ]
    for i, (start, width) in enumerate(pieces_of_x):
        cols = slice(start, start + width)
        copies.append(pltpu.make_async_copy(x.at[:, cols], held.at[:, cols], sems.at[6 + i]))
    for copy in copies:
        copy.start()
    for copy in copies[:4]:
        copy.wait()
    raw = raw_here[...].astype(F32)
    raw = jnp.concatenate([raw, raw], axis=0).T[:, :HEADS] + small[0:1, :]
    sizes = jnp.maximum(raw, 0.0) + accurate_log1p(jnp.exp(-jnp.abs(raw)))
    log_decay = sizes * -jnp.exp(small[8:9, :])
    row = lax.broadcasted_iota(jnp.int32, (SPAN, SPAN), 0)
    lane = lax.broadcasted_iota(jnp.int32, (SPAN, SPAN), 1)
    lower = (row >= lane).astype(BF16)
    cumulative = sum(dot(lower, piece) for piece in pieces(log_decay, 3))
    total = cumulative[SPAN - 1 : SPAN, :]
    tail = jnp.exp(total - cumulative) * sizes
    joined = jnp.concatenate([cumulative, sizes], axis=1)
    both[...] = joined
    both_t[...] = joined.T
    tail_pair[...] = jnp.concatenate(pieces(tail, 2), axis=1)
    carry_pair[...] = jnp.concatenate(pieces(jnp.exp(cumulative), 2), axis=1)
    rows = jnp.concatenate(
        [jnp.broadcast_to(jnp.exp(total), (8, HEADS)), jnp.broadcast_to(small[16:17, :], (8, HEADS))], axis=0
    )
    row_pair[...] = jnp.concatenate(pieces(rows, 2), axis=1)
    for copy in copies[4:8]:
        copy.wait()
    convolve_part(held, None, weight, bias, padded, first, (values, keys))
    for copy in copies[8:]:
        copy.wait()


def prepare_rest(held, halo, weight, bias, *refs):
    spans = [span for part in range(1, PARTS) for span in part_columns(part)] + [(INNER + KEYS, KEYS)]
    convolve_part(held, halo, weight, bias, refs[-1], spans, refs[:-1])


def put_decays(send, tiles, decays):
    high = [d.astype(BF16).astype(F32) for d in decays]
    low = [d - h for d, h in zip(decays, high)]
    rows = high + low
    spare = extra_rows(tiles) - len(rows)
    block = jnp.concatenate(rows + [jnp.zeros((spare, LANES), F32)] * (spare > 0), axis=0)
    send[tiles * STATE : tiles * STATE + extra_rows(tiles), :] = block.astype(BF16)


def increments(first, *refs):
    if first:
        held, halo, weight, bias, raw_values, raw_keys = refs[:6]
        tail_pair, row_pair, send, keep, keep_decay, values_ref, keys_ref, padded, value_fix, key_fix = refs[6:]
        convolve_part(held, halo, weight, bias, padded, part_columns(0), (value_fix, key_fix), 16)
    else:
        values_ref, keys_ref, tail_pair, row_pair, send, keep, keep_decay = refs
    part = 0 if first else 1
    core = lax.axis_index("seq") & 1
    for target, side in ((send, 1 - core), (keep, core)):
        decays = []
        for j in range(HALF_GROUPS):
            local = side * HALF_GROUPS + j
            value_cols, key_cols = columns(local, GROUP_COLS), columns(local, STATE)
            to_channels = spread(part * PART_GROUPS + local)
            scale = dot(tail_pair[...], to_channels)
            if first:
                values = jnp.concatenate([value_fix[:, value_cols], raw_values[16:, value_cols]], axis=0)
                keys = jnp.concatenate([key_fix[:, key_cols], raw_keys[16:, key_cols]], axis=0)
                values_ref[:, value_cols] = values
                keys_ref[:, key_cols] = keys
            else:
                values, keys = values_ref[:, value_cols], keys_ref[:, key_cols]
            grown = dot(keys, (values.astype(F32) * scale).astype(BF16), ((0,), (0,)))
            decay = dot(row_pair[...], to_channels)
            for t in range(TILES):
                at = (j * TILES + t) * STATE
                target[at : at + STATE, :] = grown[:, t * LANES : (t + 1) * LANES].astype(target.dtype)
                decays.append(decay[0:1, t * LANES : (t + 1) * LANES])
        if target is send:
            put_decays(send, HALF_TILES, decays)
        else:
            for t, d in enumerate(decays):
                keep_decay[t : t + 1, :] = d


def tile_rows(t):
    return pl.ds(pl.multiple_of(t * STATE, STATE), STATE)


def received_decays(recv, tiles, scratch):
    rows = recv[tiles * STATE : tiles * STATE + extra_rows(tiles), :].astype(F32)
    scratch[0:tiles, :] = rows[0:tiles] + rows[tiles : 2 * tiles]


def join_cores(keep, keep_decay, recv, send, own, own_decay, other):
    me = lax.axis_index("seq")
    first = (me & 1) == 0
    y = (me >> 1) & 1
    received_decays(recv, HALF_TILES, other)

    def joined(t):
        mine, theirs = keep[tile_rows(t), :], recv[tile_rows(t), :].astype(F32)
        decay_mine, decay_theirs = keep_decay[pl.ds(t, 1), :], other[pl.ds(t, 1), :]
        early, late = jnp.where(first, mine, theirs), jnp.where(first, theirs, mine)
        return jnp.where(first, decay_theirs, decay_mine) * early + late, decay_mine * decay_theirs

    decays = []
    for t in range(QUARTER_TILES):
        state, decay = joined((1 - y) * QUARTER_TILES + t)
        send[t * STATE : (t + 1) * STATE, :] = state.astype(BF16)
        decays.append(decay)
    put_decays(send, QUARTER_TILES, decays)
    for t in range(QUARTER_TILES):
        state, decay = joined(y * QUARTER_TILES + t)
        own[t * STATE : (t + 1) * STATE, :] = state
        own_decay[t : t + 1, :] = decay


def join_pair(bit, carried, totals, *refs):
    state, decay, recv = refs[:3]
    refs = refs[3:]
    if carried:
        before, before_decay = refs[:2]
        refs = refs[2:]
    send = refs[0]
    refs = refs[1:]
    if totals:
        new_state, new_decay = refs[:2]
        refs = refs[2:]
    if bit >= 2:
        new_before, new_before_decay = refs[:2]
        refs = refs[2:]
    (other,) = refs
    upper = ((lax.axis_index("seq") >> bit) & 1) == 1
    received_decays(recv, QUARTER_TILES, other)
    decays = []
    for t in range(QUARTER_TILES):
        rows = slice(t * STATE, (t + 1) * STATE)
        mine, theirs = state[rows, :], recv[rows, :].astype(F32)
        d_mine, d_theirs = decay[t : t + 1, :], other[t : t + 1, :]
        early, late = jnp.where(upper, theirs, mine), jnp.where(upper, mine, theirs)
        total = jnp.where(upper, d_mine, d_theirs) * early + late
        send[rows, :] = total.astype(BF16)
        if totals:
            new_state[rows, :] = total
            new_decay[t : t + 1, :] = d_mine * d_theirs
        decays.append(d_mine * d_theirs)
        if bit >= 2:
            if carried:
                b, bd = before[rows, :], before_decay[t : t + 1, :]
                new_before[rows, :] = jnp.where(upper, b + bd * theirs, b)
                new_before_decay[t : t + 1, :] = jnp.where(upper, bd * d_theirs, bd)
            else:
                new_before[rows, :] = jnp.where(upper, theirs, 0.0)
                new_before_decay[t : t + 1, :] = jnp.where(upper, d_theirs, 1.0)
    put_decays(send, QUARTER_TILES, decays)


def to_planes(bit, carried, *refs):
    recv = refs[0]
    refs = refs[1:]
    if carried:
        before, before_decay = refs[:2]
        refs = refs[2:]
    own, own_decay, recv_pair, send, start, other = refs
    me = lax.axis_index("seq")
    upper = ((me >> bit) & 1) == 1
    y = ((me >> 1) & 1) == 1
    received_decays(recv_pair, QUARTER_TILES, other)
    for t in range(QUARTER_TILES):
        rows = slice(t * STATE, (t + 1) * STATE)
        theirs = recv[rows, :].astype(F32)
        if carried:
            b = before[rows, :]
            plane = jnp.where(upper, b + before_decay[t : t + 1, :] * theirs, b)
        else:
            plane = jnp.where(upper, theirs, 0.0)
        d = jnp.where(y, other[t : t + 1, :], own_decay[t : t + 1, :])
        grown = jnp.where(y, recv_pair[rows, :].astype(F32), own[rows, :])
        later = d * plane + grown
        send[rows, :] = jnp.where(y, plane, later).astype(BF16)
        start[rows, :] = jnp.where(y, later, plane)


def to_cores(start, recv_start, keep, keep_decay, recv, send, own, other):
    me = lax.axis_index("seq")
    first = (me & 1) == 0
    y = (me >> 1) & 1
    received_decays(recv, HALF_TILES, other)
    for side in range(2):
        for t in range(QUARTER_TILES):
            rows = slice(t * STATE, (t + 1) * STATE)
            at = (y if side == 0 else 1 - y) * QUARTER_TILES + t
            chip = start[rows, :] if side == 0 else recv_start[rows, :].astype(F32)
            d = jnp.where(first, keep_decay[pl.ds(at, 1), :], other[pl.ds(at, 1), :])
            grown = jnp.where(first, keep[tile_rows(at), :], recv[tile_rows(at), :].astype(F32))
            later = d * chip + grown
            send[tile_rows(at), :] = jnp.where(first, later, chip).astype(BF16)
            own[tile_rows(at), :] = jnp.where(first, chip, later).astype(BF16)


def inside(part, values_ref, keys_ref, reads_ref, both, both_t, carry_pair, row_pair, gate, base, slope):
    row = lax.broadcasted_iota(jnp.int32, (SPAN, SPAN), 0)
    lane = lax.broadcasted_iota(jnp.int32, (SPAN, SPAN), 1)
    causal = row >= lane
    for j in range(PART_GROUPS):
        group = part * PART_GROUPS + j
        cols = slice(j * GROUP_COLS, (j + 1) * GROUP_COLS)
        values = values_ref[:, cols]
        writes = keys_ref[:, j * STATE : (j + 1) * STATE]
        reads = reads_ref[:, group * STATE : (group + 1) * STATE]
        scores = dot(reads, writes, ((1,), (1,)))
        found = []
        for i in range(PER_GROUP):
            h = group * PER_GROUP + i
            gap = both[:, h : h + 1] - both_t[h : h + 1, :]
            weights = scores * jnp.exp(jnp.where(causal, gap, -jnp.inf)) * both_t[HEADS + h : HEADS + h + 1, :]
            found.append(dot(weights.astype(BF16), values[:, i * HEAD_DIM : (i + 1) * HEAD_DIM]))
        within = jnp.concatenate(found, axis=1)
        to_channels = spread(group)
        skip = dot(row_pair[...], to_channels)[8:9, :]
        opened = silu(gate[:, group * GROUP_COLS : (group + 1) * GROUP_COLS].astype(F32))
        base[:, cols] = (within + skip * values.astype(F32)) * opened
        slope[:, cols] = dot(carry_pair[...], to_channels) * opened


def finish(part, mine, chained, *refs):
    reads_ref, source, base, slope, gain = refs[:5]
    out, made, sems = refs[-3:]
    core = lax.axis_index("seq") & 1
    side = core if mine else 1 - core
    copies = []
    for j in range(HALF_GROUPS):
        local = side * HALF_GROUPS + j
        group = part * PART_GROUPS + local
        cols = columns(local, GROUP_COLS)
        starts = jnp.concatenate(
            [source[(j * TILES + t) * STATE : (j * TILES + t + 1) * STATE, :] for t in range(TILES)], axis=1
        )
        gated = base[:, cols] + slope[:, cols] * dot(reads_ref[:, columns(group, STATE)], starts)
        mean = jnp.mean(gated * gated, axis=1, keepdims=True)
        made[j] = (gated * lax.rsqrt(mean + 1e-5) * gain[:, columns(group, GROUP_COLS)]).astype(BF16)
        copy = pltpu.make_async_copy(made.at[j], out.at[:, columns(group, GROUP_COLS)], sems.at[j])
        copy.start()
        copies.append(copy)
    for copy in copies:
        copy.wait()


def shards(mixer_input, gate_input, step_raw, conv_weight, conv_bias, step_bias, decay_log, skip_gain, norm_gain):
    devices = lax.axis_size("seq")
    bits = devices.bit_length() - 1

    def across(value, bit):
        return lax.ppermute(value, "seq", [(i, i ^ (1 << bit)) for i in range(devices)])

    part_values = vmem(SPAN, PART_GROUPS * GROUP_COLS, BF16)
    part_keys = vmem(SPAN, PART_GROUPS * STATE, BF16)
    half_send = vmem(HALF_ROWS + extra_rows(HALF_TILES), LANES, BF16)
    quarter_send = vmem(QUARTER_ROWS + extra_rows(QUARTER_TILES), LANES, BF16)
    quarter = vmem(QUARTER_ROWS, LANES, F32)
    quarter_decay = vmem(decay_rows(QUARTER_TILES), LANES, F32)
    half_keep = [half_send, vmem(HALF_ROWS, LANES, F32), vmem(decay_rows(HALF_TILES), LANES, F32)]
    half_scratch = [pltpu.VMEM((decay_rows(HALF_TILES), LANES), F32)]
    quarter_scratch = [pltpu.VMEM((decay_rows(QUARTER_TILES), LANES), F32)]

    halo = lax.ppermute(mixer_input[SPAN - 3 :], "seq", [(i, i + 1) for i in range(devices - 1)])
    held, weight, bias, raw_values, raw_keys, both, both_t, tail_pair, carry_pair, row_pair = call(
        prepare,
        [
            vmem(SPAN, CONV_COLS, BF16),
            vmem(4, CONV_COLS, BF16),
            vmem(1, CONV_COLS, F32),
            part_values,
            part_keys,
            vmem(SPAN, 2 * HEADS, F32),
            vmem(2 * HEADS, SPAN, F32),
            vmem(SPAN, 2 * HEADS, BF16),
            vmem(SPAN, 2 * HEADS, BF16),
            vmem(16, 2 * HEADS, BF16),
        ],
        mixer_input, step_raw.T, step_bias[None, :], decay_log[None, :], skip_gain[None, :],
        conv_weight, conv_bias[None, :],
        hbm=range(7),
        scratch=[
            pltpu.VMEM((8 + SPAN, 512), F32),
            pltpu.VMEM((HEADS, SPAN), BF16),
            pltpu.VMEM((24, HEADS), F32),
            pltpu.SemaphoreType.DMA((12,)),
        ],
    )
    send_a, keep_a, keep_decay_a, values_a, keys_a = call(
        functools.partial(increments, True), half_keep + [part_values, part_keys],
        held, halo, weight, bias, raw_values, raw_keys, tail_pair, row_pair,
        scratch=[
            pltpu.VMEM((24, 512), F32),
            pltpu.VMEM((16, PART_GROUPS * GROUP_COLS), BF16),
            pltpu.VMEM((16, PART_GROUPS * STATE), BF16),
        ],
    )
    recv_a = across(send_a, 0)
    values_b, keys_b, reads = call(
        prepare_rest, [part_values, part_keys, vmem(SPAN, KEYS, BF16)],
        held, halo, weight, bias, after=(keep_decay_a,), scratch=[pltpu.VMEM((8 + SPAN, 512), F32)],
    )

    def cores(keep, keep_decay, recv, after):
        return call(
            join_cores, [quarter_send, quarter, quarter_decay], keep, keep_decay, recv,
            after=after, scratch=half_scratch,
        )

    def pair(bit, state, decay, recv, carried, after):
        totals = bit + 1 < bits - 1
        outs = call(
            functools.partial(join_pair, bit, bool(carried), totals),
            [quarter_send] + [quarter, quarter_decay] * totals + [quarter, quarter_decay] * (bit >= 2),
            state, decay, recv, *carried, after=after, scratch=quarter_scratch,
        )
        send = outs[0]
        state, decay = outs[1:3] if totals else (None, None)
        return send, state, decay, tuple(outs[-2:]) if bit >= 2 else ()

    def planes(recv, carried, own, own_decay, recv_pair, after):
        return call(
            functools.partial(to_planes, bits - 1, bool(carried)), [vmem(QUARTER_ROWS, LANES, BF16), quarter],
            recv, *carried, own, own_decay, recv_pair, after=after, scratch=quarter_scratch,
        )

    def split(start, recv_start, keep, keep_decay, recv, after):
        return call(
            to_cores, [vmem(HALF_ROWS, LANES, BF16)] * 2, start, recv_start, keep, keep_decay, recv,
            after=after, scratch=half_scratch,
        )

    def within(part, values, keys, after):
        return call(
            functools.partial(inside, part), [vmem(SPAN, PART_GROUPS * GROUP_COLS, F32)] * 2,
            values, keys, reads, both, both_t, carry_pair, row_pair, gate_input, after=after,
        )

    out = None

    def last(part, mine, source, base, slope):
        args = (reads, source, base, slope, norm_gain[None, :]) + ((out,) if out is not None else ())
        return call(
            functools.partial(finish, part, mine, out is not None),
            [((SPAN, INNER), BF16, pltpu.HBM)],
            *args,
            hbm=(5,) if out is not None else (),
            aliases={5: 0} if out is not None else None,
            scratch=[pltpu.VMEM((HALF_GROUPS, SPAN, GROUP_COLS), BF16), pltpu.SemaphoreType.DMA((HALF_GROUPS,))],
        )[0]

    send_pair_a, own_a, own_decay_a = cores(keep_a, keep_decay_a, recv_a, (reads,))
    recv_pair_a = across(send_pair_a, 1)
    send_b, keep_b, keep_decay_b = call(
        functools.partial(increments, False), half_keep, values_b, keys_b, tail_pair, row_pair,
        after=(own_decay_a,),
    )
    recv_b = across(send_b, 0)
    send_pair_b, own_b, own_decay_b = cores(keep_b, keep_decay_b, recv_b, ())
    recv_pair_b = across(send_pair_b, 1)
    found_a = pair(1, own_a, own_decay_a, recv_pair_a, (), (own_decay_b,))
    base_a, slope_a = within(0, values_a, keys_a, (found_a[0],))
    found_b = pair(1, own_b, own_decay_b, recv_pair_b, (), (base_a,))
    base_b = None
    for bit in range(2, bits - 1):
        send, state, decay, carried = found_a
        found_a = pair(bit, state, decay, across(send, bit), carried, (found_b[0],))
        if base_b is None:
            base_b, slope_b = within(1, values_b, keys_b, (found_a[0],))
        send, state, decay, carried = found_b
        found_b = pair(bit, state, decay, across(send, bit), carried, (found_a[0], base_b))
    start_send_a, start_a = planes(
        across(found_a[0], bits - 1), found_a[3], own_a, own_decay_a, recv_pair_a, (found_b[0],)
    )
    start_send_b, start_b = planes(
        across(found_b[0], bits - 1), found_b[3], own_b, own_decay_b, recv_pair_b, (start_send_a,)
    )
    core_send_a, own_start_a = split(
        start_a, across(start_send_a, 1), keep_a, keep_decay_a, recv_a, (start_send_b,)
    )
    out = last(0, True, own_start_a, base_a, slope_a)
    out = last(0, False, across(core_send_a, 0), base_a, slope_a)
    core_send_b, own_start_b = split(start_b, across(start_send_b, 1), keep_b, keep_decay_b, recv_b, ())
    out = last(1, True, own_start_b, base_b, slope_b)
    return last(1, False, across(core_send_b, 0), base_b, slope_b)


def solution(mesh):
    in_specs = (
        P(("groups", "seq"), None),
        P(("groups", "seq"), None),
        P(("groups", "seq"), None),
        P(),
        P(),
        P("groups"),
        P("groups"),
        P(),
        P(),
    )
    return jax.shard_map(
        shards, mesh=mesh, in_specs=in_specs, out_specs=P(("groups", "seq"), None), check_vma=False
    )
```

```python
import functools

import jax
import jax.numpy as jnp
from jax import lax
from jax.experimental import pallas as pl
from jax.experimental.pallas import tpu as pltpu
from jax.sharding import PartitionSpec as P

HEADS = 64
HEAD_DIM = 64
STATE = 128
GROUPS = 8
PER_GROUP = HEADS // GROUPS
GROUP_COLS = PER_GROUP * HEAD_DIM
INNER = HEADS * HEAD_DIM
KEYS = GROUPS * STATE
CONV_COLS = INNER + 2 * KEYS
SPAN = 128
LANES = 128
TILES = GROUP_COLS // LANES
SIZES = (4, 4)
F32 = jnp.float32
BF16 = jnp.bfloat16


class Part:
    def __init__(self, index):
        self.index = index
        self.first = sum(SIZES[:index])
        self.groups = SIZES[index]
        self.half_groups = self.groups // 2
        self.half_tiles = self.half_groups * TILES
        self.quarter_tiles = self.half_tiles // 2
        self.half_rows = self.half_tiles * STATE
        self.quarter_rows = self.quarter_tiles * STATE
        self.width = self.groups * GROUP_COLS
        self.spans = (
            (self.first * GROUP_COLS, self.width),
            (INNER + self.first * STATE, self.groups * STATE),
        )


VMEM_LIMIT = 24 * 1024 * 1024
FLOPS, BYTES = 1e9, 3e6


def extra_rows(tiles):
    return -(-2 * tiles // 16) * 16


def decay_rows(tiles):
    return -(-tiles // 8) * 8


def call(body, outs, *args, after=(), hbm=(), cost=0.1, scratch=()):
    count = len(args)
    args = [pltpu.with_memory_space_constraint(a, pltpu.HBM) if i in hbm else a for i, a in enumerate(args)]
    specs = [pl.BlockSpec(memory_space=pltpu.HBM if i in hbm else pltpu.VMEM) for i in range(count)]
    specs += [pl.BlockSpec(memory_space=pl.ANY) for _ in after]

    def kernel(*refs):
        body(*refs[:count], *refs[count + len(after) :])

    return pl.pallas_call(
        kernel,
        out_shape=[space(shape, kind) for shape, kind, space in outs],
        in_specs=specs,
        out_specs=[pl.BlockSpec(memory_space=space) for _, _, space in outs],
        scratch_shapes=list(scratch),
        compiler_params=pltpu.CompilerParams(vmem_limit_bytes=VMEM_LIMIT),
        cost_estimate=pl.CostEstimate(flops=int(cost * FLOPS), bytes_accessed=int(cost * BYTES), transcendentals=0),
    )(*args, *after)


def vmem(rows, cols, kind):
    return ((rows, cols), kind, pltpu.VMEM)


def dot(a, b, dims=((1,), (0,))):
    return lax.dot_general(a, b, (dims, ((), ())), preferred_element_type=F32)


def silu(v):
    half = 0.5 * v
    return half + half * jnp.tanh(half)


def pieces(v, count):
    found = []
    for _ in range(count):
        piece = v.astype(BF16)
        found.append(piece)
        v = v - piece.astype(F32)
    return found


def spread(group):
    row = lax.broadcasted_iota(jnp.int32, (2 * HEADS, GROUP_COLS), 0)
    lane = lax.broadcasted_iota(jnp.int32, (2 * HEADS, GROUP_COLS), 1)
    head = group * PER_GROUP + lane // HEAD_DIM
    return ((row == head) | (row == head + HEADS)).astype(BF16)


def columns(group, width, start=0):
    return pl.ds(pl.multiple_of(start + group * width, LANES), width)


def convolve_into(rows, padded, weight_ref, bias_ref, cols):
    total = bias_ref[:, cols]
    for tap in range(4):
        total = total + weight_ref[tap : tap + 1, cols].astype(F32) * padded[5 + tap : 5 + tap + rows, :]
    return silu(total).astype(BF16)


def accurate_log1p(u):
    w = 1.0 + u
    return jnp.where(w == 1.0, u, jnp.log(w) * (u / jnp.where(w == 1.0, 1.0, w - 1.0)))


def convolve_part(source, halo, weight, bias, padded, spans, outs, rows=SPAN):
    for (start, width), out in zip(spans, outs):

        block = min(width, 512)

        @pl.loop(0, width // block)
        def _(i, start=start, out=out, block=block):
            cols = columns(i, block, start)
            here = padded.at[:, 0:block]
            here[0:8, :] = jnp.zeros((8, block), F32)
            if halo is not None:
                here[5:8, :] = halo[:, cols].astype(F32)
            here[8 : 8 + rows, :] = source[0:rows, cols].astype(F32)
            out[0:rows, columns(i, block)] = convolve_into(rows, here, weight, bias, cols)


def prepare(
    part, x, raw_t, step_bias, decay_log, skip, weight_in, bias_in,
    held, weight, bias, values, keys, both, both_t, tail_pair, carry_pair, row_pair,
    padded, raw_here, small, sems,
):
    first = part.spans
    pieces_of_x = list(first)
    at = 0
    for start, width in sorted(first) + [(CONV_COLS, 0)]:
        if start > at:
            pieces_of_x.append((at, start - at))
        at = start + width
    copies = [
        pltpu.make_async_copy(raw_t, raw_here, sems.at[0]),
        pltpu.make_async_copy(step_bias, small.at[0:1], sems.at[1]),
        pltpu.make_async_copy(decay_log, small.at[8:9], sems.at[2]),
        pltpu.make_async_copy(skip, small.at[16:17], sems.at[3]),
        pltpu.make_async_copy(weight_in, weight, sems.at[4]),
        pltpu.make_async_copy(bias_in, bias, sems.at[5]),
    ]
    for i, (start, width) in enumerate(pieces_of_x):
        cols = slice(start, start + width)
        copies.append(pltpu.make_async_copy(x.at[:, cols], held.at[:, cols], sems.at[6 + i]))
    for copy in copies:
        copy.start()
    for copy in copies[:4]:
        copy.wait()
    raw = raw_here[...].astype(F32)
    raw = jnp.concatenate([raw, raw], axis=0).T[:, :HEADS] + small[0:1, :]
    sizes = jnp.maximum(raw, 0.0) + accurate_log1p(jnp.exp(-jnp.abs(raw)))
    log_decay = sizes * -jnp.exp(small[8:9, :])
    row = lax.broadcasted_iota(jnp.int32, (SPAN, SPAN), 0)
    lane = lax.broadcasted_iota(jnp.int32, (SPAN, SPAN), 1)
    lower = (row >= lane).astype(BF16)
    cumulative = sum(dot(lower, piece) for piece in pieces(log_decay, 3))
    total = cumulative[SPAN - 1 : SPAN, :]
    tail = jnp.exp(total - cumulative) * sizes
    joined = jnp.concatenate([cumulative, sizes], axis=1)
    both[...] = joined
    both_t[...] = joined.T
    tail_pair[...] = jnp.concatenate(pieces(tail, 2), axis=1)
    carry_pair[...] = jnp.concatenate(pieces(jnp.exp(cumulative), 2), axis=1)
    rows = jnp.concatenate(
        [jnp.broadcast_to(jnp.exp(total), (8, HEADS)), jnp.broadcast_to(small[16:17, :], (8, HEADS))], axis=0
    )
    row_pair[...] = jnp.concatenate(pieces(rows, 2), axis=1)
    for copy in copies[4:8]:
        copy.wait()
    convolve_part(held, None, weight, bias, padded, first, (values, keys))
    for copy in copies[8:]:
        copy.wait()


def prepare_rest(spans, held, halo, weight, bias, *refs):
    convolve_part(held, halo, weight, bias, refs[-1], spans, refs[:-1])


def put_decays(send, tiles, decays):
    high = [d.astype(BF16).astype(F32) for d in decays]
    low = [d - h for d, h in zip(decays, high)]
    rows = high + low
    spare = extra_rows(tiles) - len(rows)
    block = jnp.concatenate(rows + [jnp.zeros((spare, LANES), F32)] * (spare > 0), axis=0)
    send[tiles * STATE : tiles * STATE + extra_rows(tiles), :] = block.astype(BF16)


def increments(part, *refs):
    first = part.index == 0
    if first:
        held, halo, weight, bias, raw_values, raw_keys = refs[:6]
        tail_pair, row_pair, send, keep, keep_decay, values_ref, keys_ref, padded, value_fix, key_fix = refs[6:]
        convolve_part(held, halo, weight, bias, padded, part.spans, (value_fix, key_fix), 16)
    else:
        values_ref, keys_ref, tail_pair, row_pair, send, keep, keep_decay = refs
    core = lax.axis_index("seq") & 1
    for target, side in ((send, 1 - core), (keep, core)):
        decays = []
        for j in range(part.half_groups):
            local = side * part.half_groups + j
            value_cols, key_cols = columns(local, GROUP_COLS), columns(local, STATE)
            to_channels = spread(part.first + local)
            scale = dot(tail_pair[...], to_channels)
            if first:
                values = jnp.concatenate([value_fix[:, value_cols], raw_values[16:, value_cols]], axis=0)
                keys = jnp.concatenate([key_fix[:, key_cols], raw_keys[16:, key_cols]], axis=0)
                values_ref[:, value_cols] = values
                keys_ref[:, key_cols] = keys
            else:
                values, keys = values_ref[:, value_cols], keys_ref[:, key_cols]
            grown = dot(keys, (values.astype(F32) * scale).astype(BF16), ((0,), (0,)))
            decay = dot(row_pair[...], to_channels)
            for t in range(TILES):
                at = (j * TILES + t) * STATE
                target[at : at + STATE, :] = grown[:, t * LANES : (t + 1) * LANES].astype(target.dtype)
                decays.append(decay[0:1, t * LANES : (t + 1) * LANES])
        if target is send:
            put_decays(send, part.half_tiles, decays)
        else:
            for t, d in enumerate(decays):
                keep_decay[t : t + 1, :] = d


def tile_rows(t):
    return pl.ds(pl.multiple_of(t * STATE, STATE), STATE)


def received_decays(recv, tiles, scratch):
    rows = recv[tiles * STATE : tiles * STATE + extra_rows(tiles), :].astype(F32)
    scratch[0:tiles, :] = rows[0:tiles] + rows[tiles : 2 * tiles]


def join_cores(part, keep, keep_decay, recv, send, own, own_decay, other):
    me = lax.axis_index("seq")
    first = (me & 1) == 0
    y = (me >> 1) & 1
    received_decays(recv, part.half_tiles, other)

    def joined(t):
        mine, theirs = keep[tile_rows(t), :], recv[tile_rows(t), :].astype(F32)
        decay_mine, decay_theirs = keep_decay[pl.ds(t, 1), :], other[pl.ds(t, 1), :]
        early, late = jnp.where(first, mine, theirs), jnp.where(first, theirs, mine)
        return jnp.where(first, decay_theirs, decay_mine) * early + late, decay_mine * decay_theirs

    decays = []
    for t in range(part.quarter_tiles):
        state, decay = joined((1 - y) * part.quarter_tiles + t)
        send[t * STATE : (t + 1) * STATE, :] = state.astype(BF16)
        decays.append(decay)
    put_decays(send, part.quarter_tiles, decays)
    for t in range(part.quarter_tiles):
        state, decay = joined(y * part.quarter_tiles + t)
        own[t * STATE : (t + 1) * STATE, :] = state
        own_decay[t : t + 1, :] = decay


def join_pair(part, bit, carried, totals, *refs):
    state, decay, recv = refs[:3]
    refs = refs[3:]
    if carried:
        before, before_decay = refs[:2]
        refs = refs[2:]
    send = refs[0]
    refs = refs[1:]
    if totals:
        new_state, new_decay = refs[:2]
        refs = refs[2:]
    if bit >= 2:
        new_before, new_before_decay = refs[:2]
        refs = refs[2:]
    (other,) = refs
    upper = ((lax.axis_index("seq") >> bit) & 1) == 1
    received_decays(recv, part.quarter_tiles, other)
    decays = []
    for t in range(part.quarter_tiles):
        rows = slice(t * STATE, (t + 1) * STATE)
        mine, theirs = state[rows, :], recv[rows, :].astype(F32)
        d_mine, d_theirs = decay[t : t + 1, :], other[t : t + 1, :]
        early, late = jnp.where(upper, theirs, mine), jnp.where(upper, mine, theirs)
        total = jnp.where(upper, d_mine, d_theirs) * early + late
        send[rows, :] = total.astype(BF16)
        if totals:
            new_state[rows, :] = total
            new_decay[t : t + 1, :] = d_mine * d_theirs
        decays.append(d_mine * d_theirs)
        if bit >= 2:
            if carried:
                b, bd = before[rows, :], before_decay[t : t + 1, :]
                new_before[rows, :] = jnp.where(upper, b + bd * theirs, b)
                new_before_decay[t : t + 1, :] = jnp.where(upper, bd * d_theirs, bd)
            else:
                new_before[rows, :] = jnp.where(upper, theirs, 0.0)
                new_before_decay[t : t + 1, :] = jnp.where(upper, d_theirs, 1.0)
    put_decays(send, part.quarter_tiles, decays)


def to_planes(part, bit, carried, *refs):
    recv = refs[0]
    refs = refs[1:]
    if carried:
        before, before_decay = refs[:2]
        refs = refs[2:]
    own, own_decay, recv_pair, send, start, other = refs
    me = lax.axis_index("seq")
    upper = ((me >> bit) & 1) == 1
    y = ((me >> 1) & 1) == 1
    received_decays(recv_pair, part.quarter_tiles, other)
    for t in range(part.quarter_tiles):
        rows = slice(t * STATE, (t + 1) * STATE)
        theirs = recv[rows, :].astype(F32)
        if carried:
            b = before[rows, :]
            plane = jnp.where(upper, b + before_decay[t : t + 1, :] * theirs, b)
        else:
            plane = jnp.where(upper, theirs, 0.0)
        d = jnp.where(y, other[t : t + 1, :], own_decay[t : t + 1, :])
        grown = jnp.where(y, recv_pair[rows, :].astype(F32), own[rows, :])
        later = d * plane + grown
        send[rows, :] = jnp.where(y, plane, later).astype(BF16)
        start[rows, :] = jnp.where(y, later, plane)


def to_cores(part, start, recv_start, keep, keep_decay, recv, send, own, other):
    me = lax.axis_index("seq")
    first = (me & 1) == 0
    y = (me >> 1) & 1
    received_decays(recv, part.half_tiles, other)
    for side in range(2):
        for t in range(part.quarter_tiles):
            rows = slice(t * STATE, (t + 1) * STATE)
            at = (y if side == 0 else 1 - y) * part.quarter_tiles + t
            chip = start[rows, :] if side == 0 else recv_start[rows, :].astype(F32)
            d = jnp.where(first, keep_decay[pl.ds(at, 1), :], other[pl.ds(at, 1), :])
            grown = jnp.where(first, keep[tile_rows(at), :], recv[tile_rows(at), :].astype(F32))
            later = d * chip + grown
            send[tile_rows(at), :] = jnp.where(first, later, chip).astype(BF16)
            own[tile_rows(at), :] = jnp.where(first, chip, later).astype(BF16)


def inside(part, values_ref, keys_ref, reads_ref, both, both_t, carry_pair, row_pair, gate, base, slope):
    row = lax.broadcasted_iota(jnp.int32, (SPAN, SPAN), 0)
    lane = lax.broadcasted_iota(jnp.int32, (SPAN, SPAN), 1)
    causal = row >= lane
    for j in range(part.groups):
        group = part.first + j
        cols = slice(j * GROUP_COLS, (j + 1) * GROUP_COLS)
        values = values_ref[:, cols]
        writes = keys_ref[:, j * STATE : (j + 1) * STATE]
        reads = reads_ref[:, group * STATE : (group + 1) * STATE]
        scores = dot(reads, writes, ((1,), (1,)))
        found = []
        for i in range(PER_GROUP):
            h = group * PER_GROUP + i
            gap = both[:, h : h + 1] - both_t[h : h + 1, :]
            weights = scores * jnp.exp(jnp.where(causal, gap, -jnp.inf)) * both_t[HEADS + h : HEADS + h + 1, :]
            found.append(dot(weights.astype(BF16), values[:, i * HEAD_DIM : (i + 1) * HEAD_DIM]))
        within = jnp.concatenate(found, axis=1)
        to_channels = spread(group)
        skip = dot(row_pair[...], to_channels)[8:9, :]
        opened = silu(gate[:, group * GROUP_COLS : (group + 1) * GROUP_COLS].astype(F32))
        base[:, cols] = (within + skip * values.astype(F32)) * opened
        slope[:, cols] = dot(carry_pair[...], to_channels) * opened


def finish(part, mine, reads_ref, source, base, slope, gain, made):
    core = lax.axis_index("seq") & 1
    side = core if mine else 1 - core
    for j in range(part.half_groups):
        local = side * part.half_groups + j
        group = part.first + local
        cols = columns(local, GROUP_COLS)
        starts = jnp.concatenate(
            [source[(j * TILES + t) * STATE : (j * TILES + t + 1) * STATE, :] for t in range(TILES)], axis=1
        )
        gated = base[:, cols] + slope[:, cols] * dot(reads_ref[:, columns(group, STATE)], starts)
        mean = jnp.mean(gated * gated, axis=1, keepdims=True)
        normed = gated * lax.rsqrt(mean + 1e-5) * gain[:, columns(group, GROUP_COLS)]
        made[:, j * GROUP_COLS : (j + 1) * GROUP_COLS] = normed.astype(BF16)


def finish_last(part, others, *refs):
    count = len(others)
    arrays, out, made, sems = refs[:count], refs[-3], refs[-2], refs[-1]
    core = lax.axis_index("seq") & 1

    def copy_out(i, other, mine, array):
        group = other.first + (core if mine else 1 - core) * other.half_groups
        return pltpu.make_async_copy(
            array, out.at[:, pl.ds(pl.multiple_of(group * GROUP_COLS, GROUP_COLS), other.width // 2)], sems.at[i]
        )

    copies = [copy_out(i, *other, array) for i, (other, array) in enumerate(zip(others, arrays))]
    for copy in copies:
        copy.start()
    finish(part, False, *refs[count:-3], made)
    copies.append(copy_out(count, part, False, made))
    copies[-1].start()
    for copy in copies:
        copy.wait()


ORDER = "I0 P1 I1 A0 A1 R0 B0 B1 C0 C1 W0 W1 S0 S1 H0 H1 E0 F0 E1 F1"


def shards(mixer_input, gate_input, step_raw, conv_weight, conv_bias, step_bias, decay_log, skip_gain, norm_gain):
    devices = lax.axis_size("seq")
    bits = devices.bit_length() - 1
    parts = [Part(i) for i in range(len(SIZES))]

    def across(value, bit):
        return lax.ppermute(value, "seq", [(i, i ^ (1 << bit)) for i in range(devices)])

    def padded(rows):
        return pltpu.VMEM((8 + rows, 512), F32)

    def decays_of(tiles):
        return vmem(decay_rows(tiles), LANES, F32)

    def decay_scratch(tiles):
        return [pltpu.VMEM((decay_rows(tiles), LANES), F32)]

    def rows_of(p):
        return [vmem(SPAN, p.width, BF16), vmem(SPAN, p.groups * STATE, BF16)]

    def half_send(p):
        return vmem(p.half_rows + extra_rows(p.half_tiles), LANES, BF16)

    def quarter_send(p):
        return vmem(p.quarter_rows + extra_rows(p.quarter_tiles), LANES, BF16)

    def quarter(p):
        return [vmem(p.quarter_rows, LANES, F32), decays_of(p.quarter_tiles)]

    halo = lax.ppermute(mixer_input[SPAN - 3 :], "seq", [(i, i + 1) for i in range(devices - 1)])
    p = parts[0]
    held, weight, bias, raw_values, raw_keys, both, both_t, tail_pair, carry_pair, row_pair = call(
        functools.partial(prepare, p),
        [
            vmem(SPAN, CONV_COLS, BF16),
            vmem(4, CONV_COLS, BF16),
            vmem(1, CONV_COLS, F32),
            *rows_of(p),
            vmem(SPAN, 2 * HEADS, F32),
            vmem(2 * HEADS, SPAN, F32),
            vmem(SPAN, 2 * HEADS, BF16),
            vmem(SPAN, 2 * HEADS, BF16),
            vmem(16, 2 * HEADS, BF16),
        ],
        mixer_input, step_raw.T, step_bias[None, :], decay_log[None, :], skip_gain[None, :],
        conv_weight, conv_bias[None, :],
        hbm=range(7),
        cost=2.5,
        scratch=[
            padded(SPAN),
            pltpu.VMEM((HEADS, SPAN), BF16),
            pltpu.VMEM((24, HEADS), F32),
            pltpu.SemaphoreType.DMA((12,)),
        ],
    )
    gain = norm_gain[None, :]
    have = {}
    token = ()
    results = []
    for stage in ORDER.split():
        kind, p = stage[0], parts[int(stage[1:])]
        n = p.index
        get = lambda name: have[name, n]

        def put(**values):
            have.update({(name, n): value for name, value in values.items()})

        if kind == "P":
            values, keys = call(
                functools.partial(prepare_rest, p.spans), rows_of(p), held, halo, weight, bias,
                after=token, cost=0.4 * p.groups, scratch=[padded(SPAN)],
            )
            put(values=values, keys=keys)
            token = (keys,)
        elif kind == "R":
            (reads,) = call(
                functools.partial(prepare_rest, [(INNER + KEYS, KEYS)]), [vmem(SPAN, KEYS, BF16)],
                held, halo, weight, bias, after=token, cost=0.6, scratch=[padded(SPAN)],
            )
            token = (reads,)
        elif kind == "I":
            outs = [half_send(p), vmem(p.half_rows, LANES, F32), decays_of(p.half_tiles)]
            if n == 0:
                send, keep, keep_decay, values, keys = call(
                    functools.partial(increments, p), outs + rows_of(p),
                    held, halo, weight, bias, raw_values, raw_keys, tail_pair, row_pair,
                    cost=0.3 * p.groups,
                    scratch=[
                        padded(16),
                        pltpu.VMEM((16, p.width), BF16),
                        pltpu.VMEM((16, p.groups * STATE), BF16),
                    ],
                )
                put(values=values, keys=keys)
            else:
                send, keep, keep_decay = call(
                    functools.partial(increments, p), outs, get("values"), get("keys"), tail_pair, row_pair,
                    after=token, cost=0.3 * p.groups,
                )
            put(kept=(keep, keep_decay, across(send, 0)))
            token = (keep_decay,)
        elif kind == "A":
            send, own, own_decay = call(
                functools.partial(join_cores, p), [quarter_send(p), *quarter(p)], *get("kept"),
                after=token, scratch=decay_scratch(p.half_tiles),
            )
            put(own=(own, own_decay, across(send, 1)), bit=1, carried=())
            have["state", n] = have["own", n]
            token = (own_decay,)
        elif kind in "BC":
            for bit in range(1, 2) if kind == "B" else range(2, bits - 1):
                totals, carried = bit + 1 < bits - 1, get("carried")
                outs = call(
                    functools.partial(join_pair, p, bit, bool(carried), totals),
                    [quarter_send(p)] + quarter(p) * totals + quarter(p) * (bit >= 2),
                    *get("state"), *carried, after=token, scratch=decay_scratch(p.quarter_tiles),
                )
                recv = across(outs[0], bit + 1)
                put(
                    state=(*(outs[1:3] if totals else (None, None)), recv),
                    carried=tuple(outs[-2:]) if bit >= 2 else (),
                )
                token = (outs[-1],) if len(outs) > 1 else (outs[0],)
        elif kind == "S":
            send, start = call(
                functools.partial(to_planes, p, bits - 1, bool(get("carried"))),
                [vmem(p.quarter_rows, LANES, BF16), quarter(p)[0]],
                get("state")[2], *get("carried"), *get("own"),
                after=token, scratch=decay_scratch(p.quarter_tiles),
            )
            put(start=(start, across(send, 1)))
            token = (start,)
        elif kind == "H":
            send, own_start = call(
                functools.partial(to_cores, p), [vmem(p.half_rows, LANES, BF16)] * 2, *get("start"), *get("kept"),
                after=token, scratch=decay_scratch(p.half_tiles),
            )
            put(own_start=own_start, recv_start=across(send, 0))
            token = (own_start,)
        elif kind == "W":
            put(
                mixed=call(
                    functools.partial(inside, p), [vmem(SPAN, p.width, F32)] * 2,
                    get("values"), get("keys"), reads, both, both_t, carry_pair, row_pair, gate_input,
                    after=token, cost=0.42 * p.groups,
                )
            )
            token = (get("mixed")[0],)
        elif kind in "EF" and len(results) < 2 * len(SIZES) - 1:
            name = "own_start" if kind == "E" else "recv_start"
            (made,) = call(
                functools.partial(finish, p, kind == "E"), [vmem(SPAN, p.width // 2, BF16)],
                reads, get(name), *get("mixed"), gain, after=token, cost=0.2 * p.half_groups,
            )
            results.append(((p, kind == "E"), made))
            token = (made,)
        else:
            (out,) = call(
                functools.partial(finish_last, p, [where for where, _ in results]),
                [((SPAN, INNER), BF16, pltpu.HBM)],
                *[made for _, made in results], reads, get("recv_start"), *get("mixed"), gain,
                after=token, cost=0.2 * p.half_groups,
                scratch=[pltpu.VMEM((SPAN, p.width // 2), BF16), pltpu.SemaphoreType.DMA((2 * len(SIZES),))],
            )
    return out


def solution(mesh):
    in_specs = (
        P(("groups", "seq"), None),
        P(("groups", "seq"), None),
        P(("groups", "seq"), None),
        P(),
        P(),
        P("groups"),
        P("groups"),
        P(),
        P(),
    )
    return jax.shard_map(
        shards, mesh=mesh, in_specs=in_specs, out_specs=P(("groups", "seq"), None), check_vma=False
    )
```

```python
import functools

import jax
import jax.numpy as jnp
from jax import lax
from jax.experimental import pallas as pl
from jax.experimental.pallas import tpu as pltpu
from jax.sharding import PartitionSpec as P

HEADS = 64
HEAD_DIM = 64
STATE = 128
GROUPS = 8
PER_GROUP = HEADS // GROUPS
GROUP_COLS = PER_GROUP * HEAD_DIM
INNER = HEADS * HEAD_DIM
KEYS = GROUPS * STATE
CONV_COLS = INNER + 2 * KEYS
SPAN = 128
LANES = 128
TILES = GROUP_COLS // LANES
SIZES = (4, 4)
F32 = jnp.float32
BF16 = jnp.bfloat16


class Part:
    def __init__(self, index):
        self.index = index
        self.first = sum(SIZES[:index])
        self.groups = SIZES[index]
        self.half_groups = self.groups // 2
        self.half_tiles = self.half_groups * TILES
        self.quarter_tiles = self.half_tiles // 2
        self.half_rows = self.half_tiles * STATE
        self.quarter_rows = self.quarter_tiles * STATE
        self.width = self.groups * GROUP_COLS
        self.spans = (
            (self.first * GROUP_COLS, self.width),
            (INNER + self.first * STATE, self.groups * STATE),
        )


VMEM_LIMIT = 24 * 1024 * 1024
FLOPS, BYTES = 1e9, 3e6


def extra_rows(tiles):
    return -(-2 * tiles // 16) * 16


def decay_rows(tiles):
    return -(-tiles // 8) * 8


def call(body, outs, *args, after=(), hbm=(), cost=0.1, scratch=()):
    count = len(args)
    args = [pltpu.with_memory_space_constraint(a, pltpu.HBM) if i in hbm else a for i, a in enumerate(args)]
    specs = [pl.BlockSpec(memory_space=pltpu.HBM if i in hbm else pltpu.VMEM) for i in range(count)]
    specs += [pl.BlockSpec(memory_space=pl.ANY) for _ in after]

    def kernel(*refs):
        body(*refs[:count], *refs[count + len(after) :])

    return pl.pallas_call(
        kernel,
        out_shape=[space(shape, kind) for shape, kind, space in outs],
        in_specs=specs,
        out_specs=[pl.BlockSpec(memory_space=space) for _, _, space in outs],
        scratch_shapes=list(scratch),
        compiler_params=pltpu.CompilerParams(vmem_limit_bytes=VMEM_LIMIT),
        cost_estimate=pl.CostEstimate(flops=int(cost * FLOPS), bytes_accessed=int(cost * BYTES), transcendentals=0),
    )(*args, *after)


def vmem(rows, cols, kind):
    return ((rows, cols), kind, pltpu.VMEM)


def dot(a, b, dims=((1,), (0,))):
    return lax.dot_general(a, b, (dims, ((), ())), preferred_element_type=F32)


def silu(v):
    return silu_of_twice(0.5 * v)


def pieces(v, count):
    found = []
    for _ in range(count):
        piece = v.astype(BF16)
        found.append(piece)
        v = v - piece.astype(F32)
    return found


def columns(group, width, start=0):
    return pl.ds(pl.multiple_of(start + group * width, LANES), width)


def silu_of_twice(half):
    return half + half * jnp.tanh(half)


def halved_taps(weight, bias, cols):
    return 0.5 * weight[:, cols].astype(F32), 0.5 * bias[:, cols]


def convolve_into(rows, padded, weight, bias, cols):
    taps, total = halved_taps(weight, bias, cols)
    for tap in range(4):
        total = total + taps[tap : tap + 1] * padded[5 + tap : 5 + tap + rows, :]
    return silu_of_twice(total).astype(BF16)


def accurate_log1p(u):
    w = 1.0 + u
    return jnp.where(w == 1.0, u, jnp.log(w) * (u / jnp.where(w == 1.0, 1.0, w - 1.0)))


def convolve_body(source, weight, bias, spans, outs):
    for (start, width), out in zip(spans, outs):
        block = min(width, 256)

        @pl.loop(0, width // block)
        def _(i, start=start, out=out, block=block):
            cols = columns(i, block, start)
            here = source[:, cols].astype(F32)
            taps, total = halved_taps(weight, bias, cols)
            total = total + taps[3:4] * here
            for back in range(1, 4):
                total = total + taps[3 - back : 4 - back] * pltpu.roll(here, back, 0)
            out[:, columns(i, block)] = silu_of_twice(total).astype(BF16)


def convolve_head(source, halo, weight, bias, padded, spans, outs):
    for (start, width), out in zip(spans, outs):
        block = min(width, 512)

        @pl.loop(0, width // block)
        def _(i, start=start, out=out, block=block):
            cols = columns(i, block, start)
            here = padded.at[:, 0:block]
            here[0:8, :] = jnp.zeros((8, block), F32)
            here[5:8, :] = halo[:, cols].astype(F32)
            here[8:24, :] = source[0:16, cols].astype(F32)
            out[0:16, columns(i, block)] = convolve_into(16, here, weight, bias, cols)


def prepare(
    part, x, raw_t, step_bias, decay_log, skip, weight_in, bias_in,
    held, weight, bias, values, keys, both, both_t, tail_pair, carry_pair, row_pair, spread,
    raw_here, small, sems,
):
    first = part.spans
    pieces_of_x = list(first)
    at = 0
    for start, width in sorted(first) + [(CONV_COLS, 0)]:
        if start > at:
            pieces_of_x.append((at, start - at))
        at = start + width
    copies = [
        pltpu.make_async_copy(raw_t, raw_here, sems.at[0]),
        pltpu.make_async_copy(step_bias, small.at[0:1], sems.at[1]),
        pltpu.make_async_copy(decay_log, small.at[8:9], sems.at[2]),
        pltpu.make_async_copy(skip, small.at[16:17], sems.at[3]),
        pltpu.make_async_copy(weight_in, weight, sems.at[4]),
        pltpu.make_async_copy(bias_in, bias, sems.at[5]),
    ]
    for i, (start, width) in enumerate(pieces_of_x):
        cols = slice(start, start + width)
        copies.append(pltpu.make_async_copy(x.at[:, cols], held.at[:, cols], sems.at[6 + i]))
    for copy in copies:
        copy.start()
    channel = lax.broadcasted_iota(jnp.int32, (2 * HEADS, GROUP_COLS), 1)
    head = (lax.broadcasted_iota(jnp.int32, (2 * HEADS, GROUP_COLS), 0) & (HEADS - 1)) - channel // HEAD_DIM
    for group in range(GROUPS):
        spread[:, group * GROUP_COLS : (group + 1) * GROUP_COLS] = (head == group * PER_GROUP).astype(BF16)
    for copy in copies[:4]:
        copy.wait()
    raw = raw_here[...].astype(F32)
    raw = jnp.concatenate([raw, raw], axis=0).T[:, :HEADS] + small[0:1, :]
    sizes = jnp.maximum(raw, 0.0) + accurate_log1p(jnp.exp(-jnp.abs(raw)))
    log_decay = sizes * -jnp.exp(small[8:9, :])
    row = lax.broadcasted_iota(jnp.int32, (SPAN, SPAN), 0)
    lane = lax.broadcasted_iota(jnp.int32, (SPAN, SPAN), 1)
    lower = (row >= lane).astype(BF16)
    cumulative = sum(dot(lower, piece) for piece in pieces(log_decay, 3))
    total = cumulative[SPAN - 1 : SPAN, :]
    tail = jnp.exp(total - cumulative) * sizes
    joined = jnp.concatenate([cumulative, sizes], axis=1)
    both[...] = joined
    both_t[...] = joined.T
    tail_pair[...] = jnp.concatenate(pieces(tail, 2), axis=1)
    carry_pair[...] = jnp.concatenate(pieces(jnp.exp(cumulative), 2), axis=1)
    rows = jnp.concatenate(
        [jnp.broadcast_to(jnp.exp(total), (8, HEADS)), jnp.broadcast_to(small[16:17, :], (8, HEADS))], axis=0
    )
    row_pair[...] = jnp.concatenate(pieces(rows, 2), axis=1)
    for copy in copies[4:8]:
        copy.wait()
    convolve_body(held, weight, bias, first, (values, keys))
    for copy in copies[8:]:
        copy.wait()


def prepare_rest(spans, held, halo, weight, bias, *refs):
    convolve_body(held, weight, bias, spans, refs[:-1])
    convolve_head(held, halo, weight, bias, refs[-1], spans, refs[:-1])


def put_decays(send, tiles, decays):
    high = [d.astype(BF16).astype(F32) for d in decays]
    low = [d - h for d, h in zip(decays, high)]
    rows = high + low
    spare = extra_rows(tiles) - len(rows)
    block = jnp.concatenate(rows + [jnp.zeros((spare, LANES), F32)] * (spare > 0), axis=0)
    send[tiles * STATE : tiles * STATE + extra_rows(tiles), :] = block.astype(BF16)


def increments(part, *refs):
    if part.index == 0:
        held, halo, weight, bias, raw_values, raw_keys = refs[:6]
        tail_pair, row_pair, spread, send, keep, keep_decay, values_ref, keys_ref = refs[6:14]
        scaled, padded, value_fix, key_fix = refs[14:]
        convolve_head(held, halo, weight, bias, padded, part.spans, (value_fix, key_fix))
        keys_ref[0:16, :] = key_fix[...]
        keys_ref[16:, :] = raw_keys[16:, :]
    else:
        values_ref, keys_ref, tail_pair, row_pair, spread, send, keep, keep_decay, scaled = refs
    core = lax.axis_index("seq") & 1
    targets = ((send, 1 - core), (keep, core))
    order = [(target, side * part.half_groups + j, j) for target, side in targets for j in range(part.half_groups)]
    for i, (_, local, _) in enumerate(order):
        cols = columns(local, GROUP_COLS)
        scale = dot(tail_pair[...], spread[:, columns(part.first + local, GROUP_COLS)])
        if part.index == 0:
            values = jnp.concatenate([value_fix[:, cols], raw_values[16:, cols]], axis=0)
            values_ref[:, cols] = values
        else:
            values = values_ref[:, cols]
        scaled[i] = (values.astype(F32) * scale).astype(BF16)
    for target, side in targets:
        decay = dot(
            row_pair[...],
            spread[:, columns((part.first + side * part.half_groups) // part.half_groups, part.width // 2)],
        )
        decays = [decay[0:1, t * LANES : (t + 1) * LANES] for t in range(part.half_tiles)]
        if target is send:
            put_decays(send, part.half_tiles, decays)
        else:
            for t, d in enumerate(decays):
                keep_decay[t : t + 1, :] = d
    for i, (target, local, j) in enumerate(order):
        grown = dot(keys_ref[:, columns(local, STATE)], scaled[i], ((0,), (0,)))
        for t in range(TILES):
            at = (j * TILES + t) * STATE
            target[at : at + STATE, :] = grown[:, t * LANES : (t + 1) * LANES].astype(target.dtype)


def tile_rows(t):
    return pl.ds(pl.multiple_of(t * STATE, STATE), STATE)


def received_decays(recv, tiles, scratch):
    rows = recv[tiles * STATE : tiles * STATE + extra_rows(tiles), :].astype(F32)
    scratch[0:tiles, :] = rows[0:tiles] + rows[tiles : 2 * tiles]


def join_cores(part, keep, keep_decay, recv, send, own, own_decay, other):
    me = lax.axis_index("seq")
    first = (me & 1) == 0
    y = (me >> 1) & 1
    received_decays(recv, part.half_tiles, other)

    def joined(t):
        mine, theirs = keep[tile_rows(t), :], recv[tile_rows(t), :].astype(F32)
        decay_mine, decay_theirs = keep_decay[pl.ds(t, 1), :], other[pl.ds(t, 1), :]
        early, late = jnp.where(first, mine, theirs), jnp.where(first, theirs, mine)
        return jnp.where(first, decay_theirs, decay_mine) * early + late, decay_mine * decay_theirs

    decays = []
    for t in range(part.quarter_tiles):
        state, decay = joined((1 - y) * part.quarter_tiles + t)
        send[t * STATE : (t + 1) * STATE, :] = state.astype(BF16)
        decays.append(decay)
    put_decays(send, part.quarter_tiles, decays)
    for t in range(part.quarter_tiles):
        state, decay = joined(y * part.quarter_tiles + t)
        own[t * STATE : (t + 1) * STATE, :] = state
        own_decay[t : t + 1, :] = decay


def join_pair(part, bit, carried, totals, *refs):
    state, decay, recv = refs[:3]
    refs = refs[3:]
    if carried:
        before, before_decay = refs[:2]
        refs = refs[2:]
    send = refs[0]
    refs = refs[1:]
    if totals:
        new_state, new_decay = refs[:2]
        refs = refs[2:]
    if bit >= 2:
        new_before, new_before_decay = refs[:2]
        refs = refs[2:]
    (other,) = refs
    upper = ((lax.axis_index("seq") >> bit) & 1) == 1
    received_decays(recv, part.quarter_tiles, other)
    decays = []
    for t in range(part.quarter_tiles):
        rows = slice(t * STATE, (t + 1) * STATE)
        mine, theirs = state[rows, :], recv[rows, :].astype(F32)
        d_mine, d_theirs = decay[t : t + 1, :], other[t : t + 1, :]
        early, late = jnp.where(upper, theirs, mine), jnp.where(upper, mine, theirs)
        total = jnp.where(upper, d_mine, d_theirs) * early + late
        send[rows, :] = total.astype(BF16)
        if totals:
            new_state[rows, :] = total
            new_decay[t : t + 1, :] = d_mine * d_theirs
        decays.append(d_mine * d_theirs)
        if bit >= 2:
            if carried:
                b, bd = before[rows, :], before_decay[t : t + 1, :]
                new_before[rows, :] = jnp.where(upper, b + bd * theirs, b)
                new_before_decay[t : t + 1, :] = jnp.where(upper, bd * d_theirs, bd)
            else:
                new_before[rows, :] = jnp.where(upper, theirs, 0.0)
                new_before_decay[t : t + 1, :] = jnp.where(upper, d_theirs, 1.0)
    put_decays(send, part.quarter_tiles, decays)


def to_planes(part, bit, carried, *refs):
    recv = refs[0]
    refs = refs[1:]
    if carried:
        before, before_decay = refs[:2]
        refs = refs[2:]
    own, own_decay, recv_pair, send, start, other = refs
    me = lax.axis_index("seq")
    upper = ((me >> bit) & 1) == 1
    y = ((me >> 1) & 1) == 1
    received_decays(recv_pair, part.quarter_tiles, other)
    for t in range(part.quarter_tiles):
        rows = slice(t * STATE, (t + 1) * STATE)
        theirs = recv[rows, :].astype(F32)
        if carried:
            b = before[rows, :]
            plane = jnp.where(upper, b + before_decay[t : t + 1, :] * theirs, b)
        else:
            plane = jnp.where(upper, theirs, 0.0)
        d = jnp.where(y, other[t : t + 1, :], own_decay[t : t + 1, :])
        grown = jnp.where(y, recv_pair[rows, :].astype(F32), own[rows, :])
        later = d * plane + grown
        send[rows, :] = jnp.where(y, plane, later).astype(BF16)
        start[rows, :] = jnp.where(y, later, plane)


def to_cores(part, start, recv_start, keep, keep_decay, recv, send, own, other):
    me = lax.axis_index("seq")
    first = (me & 1) == 0
    y = (me >> 1) & 1
    received_decays(recv, part.half_tiles, other)
    for side in range(2):
        for t in range(part.quarter_tiles):
            rows = slice(t * STATE, (t + 1) * STATE)
            at = (y if side == 0 else 1 - y) * part.quarter_tiles + t
            chip = start[rows, :] if side == 0 else recv_start[rows, :].astype(F32)
            d = jnp.where(first, keep_decay[pl.ds(at, 1), :], other[pl.ds(at, 1), :])
            grown = jnp.where(first, keep[tile_rows(at), :], recv[tile_rows(at), :].astype(F32))
            later = d * chip + grown
            send[tile_rows(at), :] = jnp.where(first, later, chip).astype(BF16)
            own[tile_rows(at), :] = jnp.where(first, chip, later).astype(BF16)


def inside(part, values_ref, keys_ref, reads_ref, both, both_t, carry_pair, row_pair, spread, gate, base, slope):
    row = lax.broadcasted_iota(jnp.int32, (SPAN, SPAN), 0)
    lane = lax.broadcasted_iota(jnp.int32, (SPAN, SPAN), 1)
    causal = row >= lane
    for j in range(part.groups):
        group = part.first + j
        cols = slice(j * GROUP_COLS, (j + 1) * GROUP_COLS)
        values = values_ref[:, cols]
        writes = keys_ref[:, j * STATE : (j + 1) * STATE]
        reads = reads_ref[:, group * STATE : (group + 1) * STATE]
        scores = dot(reads, writes, ((1,), (1,)))
        found = []
        for i in range(PER_GROUP):
            h = group * PER_GROUP + i
            gap = both[:, h : h + 1] - both_t[h : h + 1, :]
            weights = scores * jnp.exp(jnp.where(causal, gap, -jnp.inf)) * both_t[HEADS + h : HEADS + h + 1, :]
            found.append(dot(weights.astype(BF16), values[:, i * HEAD_DIM : (i + 1) * HEAD_DIM]))
        within = jnp.concatenate(found, axis=1)
        to_channels = spread[:, group * GROUP_COLS : (group + 1) * GROUP_COLS]
        skip = dot(row_pair[...], to_channels)[8:9, :]
        opened = silu(gate[:, group * GROUP_COLS : (group + 1) * GROUP_COLS].astype(F32))
        base[:, cols] = (within + skip * values.astype(F32)) * opened
        slope[:, cols] = dot(carry_pair[...], to_channels) * opened


def finish(part, mine, reads_ref, source, base, slope, gain, made):
    core = lax.axis_index("seq") & 1
    side = core if mine else 1 - core
    for j in range(part.half_groups):
        local = side * part.half_groups + j
        group = part.first + local
        cols = columns(local, GROUP_COLS)
        starts = jnp.concatenate(
            [source[(j * TILES + t) * STATE : (j * TILES + t + 1) * STATE, :] for t in range(TILES)], axis=1
        )
        gated = base[:, cols] + slope[:, cols] * dot(reads_ref[:, columns(group, STATE)], starts)
        mean = jnp.mean(gated * gated, axis=1, keepdims=True)
        normed = gated * lax.rsqrt(mean + 1e-5) * gain[:, columns(group, GROUP_COLS)]
        made[:, j * GROUP_COLS : (j + 1) * GROUP_COLS] = normed.astype(BF16)


def finish_last(part, others, *refs):
    count = len(others)
    arrays, out, made, sems = refs[:count], refs[-3], refs[-2], refs[-1]
    core = lax.axis_index("seq") & 1

    def copy_out(i, other, mine, array):
        group = other.first + (core if mine else 1 - core) * other.half_groups
        return pltpu.make_async_copy(
            array, out.at[:, pl.ds(pl.multiple_of(group * GROUP_COLS, GROUP_COLS), other.width // 2)], sems.at[i]
        )

    copies = [copy_out(i, *other, array) for i, (other, array) in enumerate(zip(others, arrays))]
    for copy in copies:
        copy.start()
    finish(part, False, *refs[count:-3], made)
    copies.append(copy_out(count, part, False, made))
    copies[-1].start()
    for copy in copies:
        copy.wait()


ORDER = (
    "I0", "P1", "I1", "A0", "A1", "B0", "B1", "C0", "C1", "R0", "W0", "W1", "S0", "S1",
    "H0", "H1", "E0", "F0", "E1", "F1",
)


def shards(mixer_input, gate_input, step_raw, conv_weight, conv_bias, step_bias, decay_log, skip_gain, norm_gain):
    devices = lax.axis_size("seq")
    bits = devices.bit_length() - 1
    parts = [Part(i) for i in range(len(SIZES))]

    def across(value, bit):
        flipped = 1 << bit if bit < 2 else (2 << bit) - 4
        return lax.ppermute(value, "seq", [(i, i ^ flipped) for i in range(devices)])

    padded = pltpu.VMEM((24, 512), F32)

    def decays_of(tiles):
        return vmem(decay_rows(tiles), LANES, F32)

    def decay_scratch(tiles):
        return [pltpu.VMEM((decay_rows(tiles), LANES), F32)]

    def rows_of(p):
        return [vmem(SPAN, p.width, BF16), vmem(SPAN, p.groups * STATE, BF16)]

    def half_send(p):
        return vmem(p.half_rows + extra_rows(p.half_tiles), LANES, BF16)

    def quarter_send(p):
        return vmem(p.quarter_rows + extra_rows(p.quarter_tiles), LANES, BF16)

    def quarter(p):
        return [vmem(p.quarter_rows, LANES, F32), decays_of(p.quarter_tiles)]

    halo = lax.ppermute(mixer_input[SPAN - 3 :], "seq", [(i, i + 1) for i in range(devices - 1)])
    p = parts[0]
    held, weight, bias, raw_values, raw_keys, both, both_t, tail_pair, carry_pair, row_pair, spread = call(
        functools.partial(prepare, p),
        [
            vmem(SPAN, CONV_COLS, BF16),
            vmem(4, CONV_COLS, BF16),
            vmem(1, CONV_COLS, F32),
            *rows_of(p),
            vmem(SPAN, 2 * HEADS, F32),
            vmem(2 * HEADS, SPAN, F32),
            vmem(SPAN, 2 * HEADS, BF16),
            vmem(SPAN, 2 * HEADS, BF16),
            vmem(16, 2 * HEADS, BF16),
            vmem(2 * HEADS, INNER, BF16),
        ],
        mixer_input, step_raw.T, step_bias[None, :], decay_log[None, :], skip_gain[None, :],
        conv_weight, conv_bias[None, :],
        hbm=range(7),
        cost=2.5,
        scratch=[
            pltpu.VMEM((HEADS, SPAN), BF16),
            pltpu.VMEM((24, HEADS), F32),
            pltpu.SemaphoreType.DMA((12,)),
        ],
    )
    gain = norm_gain[None, :]
    have = {}
    token = ()
    results = []
    for stage in ORDER:
        kind, p = stage[0], parts[int(stage[1:])]
        n = p.index
        get = lambda name: have[name, n]

        def put(**values):
            have.update({(name, n): value for name, value in values.items()})

        if kind == "P":
            values, keys = call(
                functools.partial(prepare_rest, p.spans), rows_of(p), held, halo, weight, bias,
                after=token, cost=0.4 * p.groups, scratch=[padded],
            )
            put(values=values, keys=keys)
            token = (keys,)
        elif kind == "R":
            (reads,) = call(
                functools.partial(prepare_rest, [(INNER + KEYS, KEYS)]), [vmem(SPAN, KEYS, BF16)],
                held, halo, weight, bias, after=token, cost=0.6, scratch=[padded],
            )
            token = (reads,)
        elif kind == "I":
            outs = [half_send(p), vmem(p.half_rows, LANES, F32), decays_of(p.half_tiles)]
            scaled = pltpu.VMEM((p.groups, SPAN, GROUP_COLS), BF16)
            if n == 0:
                send, keep, keep_decay, values, keys = call(
                    functools.partial(increments, p), outs + rows_of(p),
                    held, halo, weight, bias, raw_values, raw_keys, tail_pair, row_pair, spread,
                    cost=0.3 * p.groups,
                    scratch=[
                        scaled,
                        padded,
                        pltpu.VMEM((16, p.width), BF16),
                        pltpu.VMEM((16, p.groups * STATE), BF16),
                    ],
                )
                put(values=values, keys=keys)
            else:
                send, keep, keep_decay = call(
                    functools.partial(increments, p), outs, get("values"), get("keys"), tail_pair, row_pair, spread,
                    after=token, cost=0.3 * p.groups, scratch=[scaled],
                )
            put(kept=(keep, keep_decay, across(send, 0)))
            token = (keep_decay,)
        elif kind == "A":
            send, own, own_decay = call(
                functools.partial(join_cores, p), [quarter_send(p), *quarter(p)], *get("kept"),
                after=token, scratch=decay_scratch(p.half_tiles),
            )
            put(own=(own, own_decay, across(send, 1)), bit=1, carried=())
            have["state", n] = have["own", n]
            token = (own_decay,)
        elif kind in "BC":
            for bit in range(1, 2) if kind == "B" else range(2, bits - 1):
                totals, carried = bit + 1 < bits - 1, get("carried")
                outs = call(
                    functools.partial(join_pair, p, bit, bool(carried), totals),
                    [quarter_send(p)] + quarter(p) * totals + quarter(p) * (bit >= 2),
                    *get("state"), *carried, after=token, scratch=decay_scratch(p.quarter_tiles),
                )
                recv = across(outs[0], bit + 1)
                put(
                    state=(*(outs[1:3] if totals else (None, None)), recv),
                    carried=tuple(outs[-2:]) if bit >= 2 else (),
                )
                token = (outs[-1],) if len(outs) > 1 else (outs[0],)
        elif kind == "S":
            send, start = call(
                functools.partial(to_planes, p, bits - 1, bool(get("carried"))),
                [vmem(p.quarter_rows, LANES, BF16), quarter(p)[0]],
                get("state")[2], *get("carried"), *get("own"),
                after=token, scratch=decay_scratch(p.quarter_tiles),
            )
            put(start=(start, across(send, 1)))
            token = (start,)
        elif kind == "H":
            send, own_start = call(
                functools.partial(to_cores, p), [vmem(p.half_rows, LANES, BF16)] * 2, *get("start"), *get("kept"),
                after=token, scratch=decay_scratch(p.half_tiles),
            )
            put(own_start=own_start, recv_start=across(send, 0))
            token = (own_start,)
        elif kind == "W":
            put(
                mixed=call(
                    functools.partial(inside, p), [vmem(SPAN, p.width, F32)] * 2,
                    get("values"), get("keys"), reads, both, both_t, carry_pair, row_pair, spread, gate_input,
                    after=token, cost=0.42 * p.groups,
                )
            )
            token = (get("mixed")[0],)
        elif kind in "EF" and len(results) < 2 * len(SIZES) - 1:
            name = "own_start" if kind == "E" else "recv_start"
            (made,) = call(
                functools.partial(finish, p, kind == "E"), [vmem(SPAN, p.width // 2, BF16)],
                reads, get(name), *get("mixed"), gain, after=token, cost=0.2 * p.half_groups,
            )
            results.append(((p, kind == "E"), made))
            token = (made,)
        else:
            (out,) = call(
                functools.partial(finish_last, p, [where for where, _ in results]),
                [((SPAN, INNER), BF16, pltpu.HBM)],
                *[made for _, made in results], reads, get("recv_start"), *get("mixed"), gain,
                after=token, cost=0.2 * p.half_groups,
                scratch=[pltpu.VMEM((SPAN, p.width // 2), BF16), pltpu.SemaphoreType.DMA((2 * len(SIZES),))],
            )
    return out


def solution(mesh):
    in_specs = (
        P(("groups", "seq"), None),
        P(("groups", "seq"), None),
        P(("groups", "seq"), None),
        P(),
        P(),
        P("groups"),
        P("groups"),
        P(),
        P(),
    )
    return jax.shard_map(
        shards, mesh=mesh, in_specs=in_specs, out_specs=P(("groups", "seq"), None), check_vma=False
    )
```

```python
import functools

import jax
import jax.numpy as jnp
from jax import lax
from jax.experimental import pallas as pl
from jax.experimental.pallas import tpu as pltpu
from jax.sharding import PartitionSpec as P

HEADS = 64
HEAD_DIM = 64
STATE = 128
GROUPS = 8
PER_GROUP = HEADS // GROUPS
GROUP_COLS = PER_GROUP * HEAD_DIM
INNER = HEADS * HEAD_DIM
KEYS = GROUPS * STATE
CONV_COLS = INNER + 2 * KEYS
SPAN = 128
LANES = 128
TILES = GROUP_COLS // LANES
SIZES = (4, 4)
F32 = jnp.float32
BF16 = jnp.bfloat16


class Part:
    def __init__(self, index):
        self.index = index
        self.first = sum(SIZES[:index])
        self.groups = SIZES[index]
        self.half_groups = self.groups // 2
        self.half_tiles = self.half_groups * TILES
        self.quarter_tiles = self.half_tiles // 2
        self.half_rows = self.half_tiles * STATE
        self.quarter_rows = self.quarter_tiles * STATE
        self.width = self.groups * GROUP_COLS
        self.spans = (
            (self.first * GROUP_COLS, self.width),
            (INNER + self.first * STATE, self.groups * STATE),
        )


VMEM_LIMIT = 24 * 1024 * 1024
FLOPS, BYTES = 1e9, 3e6


def extra_rows(tiles):
    return -(-2 * tiles // 16) * 16


def decay_rows(tiles):
    return -(-tiles // 8) * 8


def call(body, outs, *args, after=(), hbm=(), cost=0.1, scratch=()):
    count = len(args)
    args = [pltpu.with_memory_space_constraint(a, pltpu.HBM) if i in hbm else a for i, a in enumerate(args)]
    specs = [pl.BlockSpec(memory_space=pltpu.HBM if i in hbm else pltpu.VMEM) for i in range(count)]
    specs += [pl.BlockSpec(memory_space=pl.ANY) for _ in after]

    def kernel(*refs):
        body(*refs[:count], *refs[count + len(after) :])

    return pl.pallas_call(
        kernel,
        out_shape=[space(shape, kind) for shape, kind, space in outs],
        in_specs=specs,
        out_specs=[pl.BlockSpec(memory_space=space) for _, _, space in outs],
        scratch_shapes=list(scratch),
        compiler_params=pltpu.CompilerParams(vmem_limit_bytes=VMEM_LIMIT),
        cost_estimate=pl.CostEstimate(flops=int(cost * FLOPS), bytes_accessed=int(cost * BYTES), transcendentals=0),
    )(*args, *after)


def vmem(rows, cols, kind):
    return ((rows, cols), kind, pltpu.VMEM)


def dot(a, b, dims=((1,), (0,))):
    return lax.dot_general(a, b, (dims, ((), ())), preferred_element_type=F32)


def silu(v):
    return silu_of_twice(0.5 * v)


def pieces(v, count):
    found = []
    for _ in range(count):
        piece = v.astype(BF16)
        found.append(piece)
        v = v - piece.astype(F32)
    return found


def columns(group, width, start=0):
    return pl.ds(pl.multiple_of(start + group * width, LANES), width)


def silu_of_twice(half):
    return half + half * jnp.tanh(half)


def halved_taps(weight, bias, cols):
    return 0.5 * weight[:, cols].astype(F32), 0.5 * bias[:, cols]


def convolve_into(rows, padded, weight, bias, cols):
    taps, total = halved_taps(weight, bias, cols)
    for tap in range(4):
        total = total + taps[tap : tap + 1] * padded[5 + tap : 5 + tap + rows, :]
    return silu_of_twice(total).astype(BF16)


def accurate_log1p(u):
    w = 1.0 + u
    return jnp.where(w == 1.0, u, jnp.log(w) * (u / jnp.where(w == 1.0, 1.0, w - 1.0)))


def convolve_body(source, weight, bias, spans, outs):
    for (start, width), out in zip(spans, outs):
        block = min(width, 256)

        @pl.loop(0, width // block)
        def _(i, start=start, out=out, block=block):
            cols = columns(i, block, start)
            here = source[:, cols].astype(F32)
            taps, total = halved_taps(weight, bias, cols)
            total = total + taps[3:4] * here
            for back in range(1, 4):
                total = total + taps[3 - back : 4 - back] * pltpu.roll(here, back, 0)
            out[:, columns(i, block)] = silu_of_twice(total).astype(BF16)


def convolve_head(source, halo, weight, bias, padded, spans, outs):
    first = lax.axis_index("seq") == 0
    for (start, width), out in zip(spans, outs):
        block = min(width, 512)

        @pl.loop(0, width // block)
        def _(i, start=start, out=out, block=block):
            cols = columns(i, block, start)
            here = padded.at[:, 0:block]
            here[0:8, :] = jnp.zeros((8, block), F32)
            here[5:8, :] = jnp.where(first, 0.0, halo[:, cols].astype(F32))
            here[8:24, :] = source[0:16, cols].astype(F32)
            out[0:16, columns(i, block)] = convolve_into(16, here, weight, bias, cols)


def prepare(
    parts, x, raw_t, step_bias, decay_log, skip, weight_in, bias_in,
    held, weight, bias, both, both_t, tail_pair, carry_pair, row_pair, spread, *refs,
):
    *outs, raw_here, small, sems = refs
    spans = [span for part in parts for span in part.spans]
    copies = [
        pltpu.make_async_copy(raw_t, raw_here, sems.at[0]),
        pltpu.make_async_copy(step_bias, small.at[0:1], sems.at[1]),
        pltpu.make_async_copy(decay_log, small.at[8:9], sems.at[2]),
        pltpu.make_async_copy(skip, small.at[16:17], sems.at[3]),
        pltpu.make_async_copy(weight_in, weight, sems.at[4]),
        pltpu.make_async_copy(bias_in, bias, sems.at[5]),
    ]
    for i, (start, width) in enumerate(spans + [(INNER + KEYS, KEYS)]):
        cols = slice(start, start + width)
        copies.append(pltpu.make_async_copy(x.at[:, cols], held.at[:, cols], sems.at[6 + i]))
    for copy in copies:
        copy.start()
    channel = lax.broadcasted_iota(jnp.int32, (2 * HEADS, GROUP_COLS), 1)
    head = (lax.broadcasted_iota(jnp.int32, (2 * HEADS, GROUP_COLS), 0) & (HEADS - 1)) - channel // HEAD_DIM
    for group in range(GROUPS):
        spread[:, group * GROUP_COLS : (group + 1) * GROUP_COLS] = (head == group * PER_GROUP).astype(BF16)
    for copy in copies[:4]:
        copy.wait()
    raw = raw_here[...].astype(F32)
    raw = jnp.concatenate([raw, raw], axis=0).T[:, :HEADS] + small[0:1, :]
    sizes = jnp.maximum(raw, 0.0) + accurate_log1p(jnp.exp(-jnp.abs(raw)))
    log_decay = sizes * -jnp.exp(small[8:9, :])
    row = lax.broadcasted_iota(jnp.int32, (SPAN, SPAN), 0)
    lane = lax.broadcasted_iota(jnp.int32, (SPAN, SPAN), 1)
    lower = (row >= lane).astype(BF16)
    cumulative = sum(dot(lower, piece) for piece in pieces(log_decay, 3))
    total = cumulative[SPAN - 1 : SPAN, :]
    tail = jnp.exp(total - cumulative) * sizes
    joined = jnp.concatenate([cumulative, sizes], axis=1)
    both[...] = joined
    both_t[...] = joined.T
    tail_pair[...] = jnp.concatenate(pieces(tail, 2), axis=1)
    carry_pair[...] = jnp.concatenate(pieces(jnp.exp(cumulative), 2), axis=1)
    rows = jnp.concatenate(
        [jnp.broadcast_to(jnp.exp(total), (8, HEADS)), jnp.broadcast_to(small[16:17, :], (8, HEADS))], axis=0
    )
    row_pair[...] = jnp.concatenate(pieces(rows, 2), axis=1)
    for copy in copies[4:6]:
        copy.wait()
    for i, (span, out) in enumerate(zip(spans, outs)):
        copies[6 + i].wait()
        convolve_body(held, weight, bias, [span], [out])
    copies[-1].wait()


def convolve_reads(held, halo, weight, bias, reads, padded):
    spans = [(INNER + KEYS, KEYS)]
    convolve_body(held, weight, bias, spans, [reads])
    convolve_head(held, halo, weight, bias, padded, spans, [reads])


def put_decays(send, tiles, decays):
    high = [d.astype(BF16).astype(F32) for d in decays]
    low = [d - h for d, h in zip(decays, high)]
    rows = high + low
    spare = extra_rows(tiles) - len(rows)
    block = jnp.concatenate(rows + [jnp.zeros((spare, LANES), F32)] * (spare > 0), axis=0)
    send[tiles * STATE : tiles * STATE + extra_rows(tiles), :] = block.astype(BF16)


def increments(part, *refs):
    held, halo, weight, bias, raw_values, raw_keys = refs[:6]
    tail_pair, row_pair, spread, send, keep, keep_decay, values_ref, keys_ref = refs[6:14]
    scaled, padded, value_fix, key_fix = refs[14:]
    convolve_head(held, halo, weight, bias, padded, part.spans, (value_fix, key_fix))
    keys_ref[0:16, :] = key_fix[...]
    keys_ref[16:, :] = raw_keys[16:, :]
    core = lax.axis_index("seq") & 1
    targets = ((send, 1 - core), (keep, core))
    order = [(target, side * part.half_groups + j, j) for target, side in targets for j in range(part.half_groups)]
    for i, (_, local, _) in enumerate(order):
        cols = columns(local, GROUP_COLS)
        scale = dot(tail_pair[...], spread[:, columns(part.first + local, GROUP_COLS)])
        values = jnp.concatenate([value_fix[:, cols], raw_values[16:, cols]], axis=0)
        values_ref[:, cols] = values
        scaled[i] = (values.astype(F32) * scale).astype(BF16)
    for target, side in targets:
        decay = dot(
            row_pair[...],
            spread[:, columns((part.first + side * part.half_groups) // part.half_groups, part.width // 2)],
        )
        decays = [decay[0:1, t * LANES : (t + 1) * LANES] for t in range(part.half_tiles)]
        if target is send:
            put_decays(send, part.half_tiles, decays)
        else:
            for t, d in enumerate(decays):
                keep_decay[t : t + 1, :] = d
    for i, (target, local, j) in enumerate(order):
        grown = dot(keys_ref[:, columns(local, STATE)], scaled[i], ((0,), (0,)))
        for t in range(TILES):
            at = (j * TILES + t) * STATE
            target[at : at + STATE, :] = grown[:, t * LANES : (t + 1) * LANES].astype(target.dtype)


def tile_rows(t):
    return pl.ds(pl.multiple_of(t * STATE, STATE), STATE)


def received_decays(recv, tiles, scratch):
    rows = recv[tiles * STATE : tiles * STATE + extra_rows(tiles), :].astype(F32)
    scratch[0:tiles, :] = rows[0:tiles] + rows[tiles : 2 * tiles]


def join_cores(part, keep, keep_decay, recv, send, own, own_decay, other):
    me = lax.axis_index("seq")
    first = (me & 1) == 0
    y = (me >> 1) & 1
    received_decays(recv, part.half_tiles, other)

    def joined(t):
        mine, theirs = keep[tile_rows(t), :], recv[tile_rows(t), :].astype(F32)
        decay_mine, decay_theirs = keep_decay[pl.ds(t, 1), :], other[pl.ds(t, 1), :]
        early, late = jnp.where(first, mine, theirs), jnp.where(first, theirs, mine)
        return jnp.where(first, decay_theirs, decay_mine) * early + late, decay_mine * decay_theirs

    decays = []
    for t in range(part.quarter_tiles):
        state, decay = joined((1 - y) * part.quarter_tiles + t)
        send[t * STATE : (t + 1) * STATE, :] = state.astype(BF16)
        decays.append(decay)
    put_decays(send, part.quarter_tiles, decays)
    for t in range(part.quarter_tiles):
        state, decay = joined(y * part.quarter_tiles + t)
        own[t * STATE : (t + 1) * STATE, :] = state
        own_decay[t : t + 1, :] = decay


def join_pair(part, bit, carried, totals, *refs):
    state, decay, recv = refs[:3]
    refs = refs[3:]
    if carried:
        before, before_decay = refs[:2]
        refs = refs[2:]
    send = refs[0]
    refs = refs[1:]
    if totals:
        new_state, new_decay = refs[:2]
        refs = refs[2:]
    if bit >= 2:
        new_before, new_before_decay = refs[:2]
        refs = refs[2:]
    (other,) = refs
    upper = ((lax.axis_index("seq") >> bit) & 1) == 1
    received_decays(recv, part.quarter_tiles, other)
    decays = []
    for t in range(part.quarter_tiles):
        rows = slice(t * STATE, (t + 1) * STATE)
        mine, theirs = state[rows, :], recv[rows, :].astype(F32)
        d_mine, d_theirs = decay[t : t + 1, :], other[t : t + 1, :]
        early, late = jnp.where(upper, theirs, mine), jnp.where(upper, mine, theirs)
        total = jnp.where(upper, d_mine, d_theirs) * early + late
        send[rows, :] = total.astype(BF16)
        if totals:
            new_state[rows, :] = total
            new_decay[t : t + 1, :] = d_mine * d_theirs
        decays.append(d_mine * d_theirs)
        if bit >= 2:
            if carried:
                b, bd = before[rows, :], before_decay[t : t + 1, :]
                new_before[rows, :] = jnp.where(upper, b + bd * theirs, b)
                new_before_decay[t : t + 1, :] = jnp.where(upper, bd * d_theirs, bd)
            else:
                new_before[rows, :] = jnp.where(upper, theirs, 0.0)
                new_before_decay[t : t + 1, :] = jnp.where(upper, d_theirs, 1.0)
    if totals:
        put_decays(send, part.quarter_tiles, decays)


def to_planes(part, bit, carried, *refs):
    recv = refs[0]
    refs = refs[1:]
    if carried:
        before, before_decay = refs[:2]
        refs = refs[2:]
    own, own_decay, recv_pair, send, start, other = refs
    me = lax.axis_index("seq")
    upper = ((me >> bit) & 1) == 1
    y = ((me >> 1) & 1) == 1
    received_decays(recv_pair, part.quarter_tiles, other)
    for t in range(part.quarter_tiles):
        rows = slice(t * STATE, (t + 1) * STATE)
        theirs = recv[rows, :].astype(F32)
        if carried:
            b = before[rows, :]
            plane = jnp.where(upper, b + before_decay[t : t + 1, :] * theirs, b)
        else:
            plane = jnp.where(upper, theirs, 0.0)
        d = jnp.where(y, other[t : t + 1, :], own_decay[t : t + 1, :])
        grown = jnp.where(y, recv_pair[rows, :].astype(F32), own[rows, :])
        later = d * plane + grown
        send[rows, :] = jnp.where(y, plane, later).astype(BF16)
        start[rows, :] = jnp.where(y, later, plane)


def to_cores(part, start, recv_start, keep, keep_decay, recv, send, own, other):
    me = lax.axis_index("seq")
    first = (me & 1) == 0
    y = (me >> 1) & 1
    received_decays(recv, part.half_tiles, other)
    for side in range(2):
        for t in range(part.quarter_tiles):
            rows = slice(t * STATE, (t + 1) * STATE)
            at = (y if side == 0 else 1 - y) * part.quarter_tiles + t
            chip = start[rows, :] if side == 0 else recv_start[rows, :].astype(F32)
            d = jnp.where(first, keep_decay[pl.ds(at, 1), :], other[pl.ds(at, 1), :])
            grown = jnp.where(first, keep[tile_rows(at), :], recv[tile_rows(at), :].astype(F32))
            later = d * chip + grown
            send[tile_rows(at), :] = jnp.where(first, later, chip).astype(BF16)
            own[tile_rows(at), :] = jnp.where(first, chip, later).astype(BF16)


def inside(part, values_ref, keys_ref, reads_ref, both, both_t, carry_pair, row_pair, spread, gate, base, slope):
    row = lax.broadcasted_iota(jnp.int32, (SPAN, SPAN), 0)
    lane = lax.broadcasted_iota(jnp.int32, (SPAN, SPAN), 1)
    causal = row >= lane
    for j in range(part.groups):
        group = part.first + j
        cols = slice(j * GROUP_COLS, (j + 1) * GROUP_COLS)
        values = values_ref[:, cols]
        writes = keys_ref[:, j * STATE : (j + 1) * STATE]
        reads = reads_ref[:, group * STATE : (group + 1) * STATE]
        scores = dot(reads, writes, ((1,), (1,)))
        found = []
        for i in range(PER_GROUP):
            h = group * PER_GROUP + i
            gap = both[:, h : h + 1] - both_t[h : h + 1, :]
            weights = scores * jnp.exp(jnp.where(causal, gap, -jnp.inf)) * both_t[HEADS + h : HEADS + h + 1, :]
            found.append(dot(weights.astype(BF16), values[:, i * HEAD_DIM : (i + 1) * HEAD_DIM]))
        within = jnp.concatenate(found, axis=1)
        to_channels = spread[:, group * GROUP_COLS : (group + 1) * GROUP_COLS]
        skip = dot(row_pair[...], to_channels)[8:9, :]
        opened = silu(gate[:, group * GROUP_COLS : (group + 1) * GROUP_COLS].astype(F32))
        base[:, cols] = (within + skip * values.astype(F32)) * opened
        slope[:, cols] = dot(carry_pair[...], to_channels) * opened


def finish(part, mine, reads_ref, source, base, slope, gain, made):
    core = lax.axis_index("seq") & 1
    side = core if mine else 1 - core
    for j in range(part.half_groups):
        local = side * part.half_groups + j
        group = part.first + local
        cols = columns(local, GROUP_COLS)
        starts = jnp.concatenate(
            [source[(j * TILES + t) * STATE : (j * TILES + t + 1) * STATE, :] for t in range(TILES)], axis=1
        )
        gated = base[:, cols] + slope[:, cols] * dot(reads_ref[:, columns(group, STATE)], starts)
        mean = jnp.mean(gated * gated, axis=1, keepdims=True)
        normed = gated * lax.rsqrt(mean + 1e-5) * gain[:, columns(group, GROUP_COLS)]
        made[:, j * GROUP_COLS : (j + 1) * GROUP_COLS] = normed.astype(BF16)


def finish_last(part, others, *refs):
    count = len(others)
    arrays, out, made, sems = refs[:count], refs[-3], refs[-2], refs[-1]
    core = lax.axis_index("seq") & 1

    def copy_out(i, other, mine, array):
        group = other.first + (core if mine else 1 - core) * other.half_groups
        return pltpu.make_async_copy(
            array, out.at[:, pl.ds(pl.multiple_of(group * GROUP_COLS, GROUP_COLS), other.width // 2)], sems.at[i]
        )

    copies = [copy_out(i, *other, array) for i, (other, array) in enumerate(zip(others, arrays))]
    for copy in copies:
        copy.start()
    finish(part, False, *refs[count:-3], made)
    copies.append(copy_out(count, part, False, made))
    copies[-1].start()
    for copy in copies:
        copy.wait()


ORDER = (
    "I0", "I1", "R0", "A0", "A1", "W0", "B0", "W1", "B1", "C0", "C1", "S0", "S1",
    "H0", "H1", "E0", "F0", "E1", "F1",
)


def shards(mixer_input, gate_input, step_raw, conv_weight, conv_bias, step_bias, decay_log, skip_gain, norm_gain):
    devices = lax.axis_size("seq")
    bits = devices.bit_length() - 1
    parts = [Part(i) for i in range(len(SIZES))]

    def across(value, bit):
        flipped = 1 << bit if bit < 2 else (2 << bit) - 4
        return lax.ppermute(value, "seq", [(i, i ^ flipped) for i in range(devices)])

    padded = pltpu.VMEM((24, 512), F32)

    def decays_of(tiles):
        return vmem(decay_rows(tiles), LANES, F32)

    def decay_scratch(tiles):
        return [pltpu.VMEM((decay_rows(tiles), LANES), F32)]

    def rows_of(p):
        return [vmem(SPAN, p.width, BF16), vmem(SPAN, p.groups * STATE, BF16)]

    def half_send(p):
        return vmem(p.half_rows + extra_rows(p.half_tiles), LANES, BF16)

    def quarter_send(p):
        return vmem(p.quarter_rows + extra_rows(p.quarter_tiles), LANES, BF16)

    def quarter(p):
        return [vmem(p.quarter_rows, LANES, F32), decays_of(p.quarter_tiles)]

    halo = lax.ppermute(mixer_input[SPAN - 3 :], "seq", [(i, (i + 1) % devices) for i in range(devices)])
    held, weight, bias, both, both_t, tail_pair, carry_pair, row_pair, spread, *raw = call(
        functools.partial(prepare, parts),
        [
            vmem(SPAN, CONV_COLS, BF16),
            vmem(4, CONV_COLS, BF16),
            vmem(1, CONV_COLS, F32),
            vmem(SPAN, 2 * HEADS, F32),
            vmem(2 * HEADS, SPAN, F32),
            vmem(SPAN, 2 * HEADS, BF16),
            vmem(SPAN, 2 * HEADS, BF16),
            vmem(16, 2 * HEADS, BF16),
            vmem(2 * HEADS, INNER, BF16),
            *[shape for p in parts for shape in rows_of(p)],
        ],
        mixer_input, step_raw.T, step_bias[None, :], decay_log[None, :], skip_gain[None, :],
        conv_weight, conv_bias[None, :],
        hbm=range(7),
        cost=2.5,
        scratch=[
            pltpu.VMEM((HEADS, SPAN), BF16),
            pltpu.VMEM((24, HEADS), F32),
            pltpu.SemaphoreType.DMA((7 + 2 * len(parts),)),
        ],
    )
    gain = norm_gain[None, :]
    have = {}
    token = ()
    results = []
    for stage in ORDER:
        kind, p = stage[0], parts[int(stage[1:])]
        n = p.index
        get = lambda name: have[name, n]

        def put(**values):
            have.update({(name, n): value for name, value in values.items()})

        if kind == "R":
            (reads,) = call(
                convolve_reads, [vmem(SPAN, KEYS, BF16)], held, halo, weight, bias,
                after=token, cost=0.6, scratch=[padded],
            )
            token = (reads,)
        elif kind == "I":
            send, keep, keep_decay, values, keys = call(
                functools.partial(increments, p),
                [half_send(p), vmem(p.half_rows, LANES, F32), decays_of(p.half_tiles), *rows_of(p)],
                held, halo, weight, bias, *raw[2 * n : 2 * n + 2], tail_pair, row_pair, spread,
                after=token, cost=0.2 * p.groups,
                scratch=[
                    pltpu.VMEM((p.groups, SPAN, GROUP_COLS), BF16),
                    padded,
                    pltpu.VMEM((16, p.width), BF16),
                    pltpu.VMEM((16, p.groups * STATE), BF16),
                ],
            )
            put(values=values, keys=keys, kept=(keep, keep_decay, across(send, 0)))
            token = (keep_decay,)
        elif kind == "A":
            send, own, own_decay = call(
                functools.partial(join_cores, p), [quarter_send(p), *quarter(p)], *get("kept"),
                after=token, scratch=decay_scratch(p.half_tiles),
            )
            put(own=(own, own_decay, across(send, 1)), bit=1, carried=())
            have["state", n] = have["own", n]
            token = (own_decay,)
        elif kind in "BC":
            for bit in range(1, 2) if kind == "B" else range(2, bits - 1):
                totals, carried = bit + 1 < bits - 1, get("carried")
                outs = call(
                    functools.partial(join_pair, p, bit, bool(carried), totals),
                    [quarter_send(p) if totals else vmem(p.quarter_rows, LANES, BF16)] + quarter(p) * totals + quarter(p) * (bit >= 2),
                    *get("state"), *carried, after=token, scratch=decay_scratch(p.quarter_tiles),
                )
                recv = across(outs[0], bit + 1)
                put(
                    state=(*(outs[1:3] if totals else (None, None)), recv),
                    carried=tuple(outs[-2:]) if bit >= 2 else (),
                )
                token = (outs[-1],) if len(outs) > 1 else (outs[0],)
        elif kind == "S":
            send, start = call(
                functools.partial(to_planes, p, bits - 1, bool(get("carried"))),
                [vmem(p.quarter_rows, LANES, BF16), quarter(p)[0]],
                get("state")[2], *get("carried"), *get("own"),
                after=token, scratch=decay_scratch(p.quarter_tiles),
            )
            put(start=(start, across(send, 1)))
            token = (start,)
        elif kind == "H":
            send, own_start = call(
                functools.partial(to_cores, p), [vmem(p.half_rows, LANES, BF16)] * 2, *get("start"), *get("kept"),
                after=token, scratch=decay_scratch(p.half_tiles),
            )
            put(own_start=own_start, recv_start=across(send, 0))
            token = (own_start,)
        elif kind == "W":
            put(
                mixed=call(
                    functools.partial(inside, p), [vmem(SPAN, p.width, F32)] * 2,
                    get("values"), get("keys"), reads, both, both_t, carry_pair, row_pair, spread, gate_input,
                    after=token, cost=0.42 * p.groups,
                )
            )
            token = (get("mixed")[0],)
        elif kind in "EF" and len(results) < 2 * len(SIZES) - 1:
            name = "own_start" if kind == "E" else "recv_start"
            (made,) = call(
                functools.partial(finish, p, kind == "E"), [vmem(SPAN, p.width // 2, BF16)],
                reads, get(name), *get("mixed"), gain, after=token, cost=0.2 * p.half_groups,
            )
            results.append(((p, kind == "E"), made))
            token = (made,)
        else:
            (out,) = call(
                functools.partial(finish_last, p, [where for where, _ in results]),
                [((SPAN, INNER), BF16, pltpu.HBM)],
                *[made for _, made in results], reads, get("recv_start"), *get("mixed"), gain,
                after=token, cost=0.2 * p.half_groups,
                scratch=[pltpu.VMEM((SPAN, p.width // 2), BF16), pltpu.SemaphoreType.DMA((2 * len(SIZES),))],
            )
    return out


def solution(mesh):
    in_specs = (
        P(("groups", "seq"), None),
        P(("groups", "seq"), None),
        P(("groups", "seq"), None),
        P(),
        P(),
        P("groups"),
        P("groups"),
        P(),
        P(),
    )
    return jax.shard_map(
        shards, mesh=mesh, in_specs=in_specs, out_specs=P(("groups", "seq"), None), check_vma=False
    )
```

```python
import functools

import jax
import jax.numpy as jnp
from jax import lax
from jax.experimental import pallas as pl
from jax.experimental.pallas import tpu as pltpu
from jax.sharding import PartitionSpec as P

HEADS = 64
HEAD_DIM = 64
STATE = 128
GROUPS = 8
PER_GROUP = HEADS // GROUPS
GROUP_COLS = PER_GROUP * HEAD_DIM
INNER = HEADS * HEAD_DIM
KEYS = GROUPS * STATE
CONV_COLS = INNER + 2 * KEYS
SPAN = 128
LANES = 128
TILES = GROUP_COLS // LANES
SIZES = (4, 4)
F32 = jnp.float32
BF16 = jnp.bfloat16


class Part:
    def __init__(self, index):
        self.index = index
        self.first = sum(SIZES[:index])
        self.groups = SIZES[index]
        self.half_groups = self.groups // 2
        self.half_tiles = self.half_groups * TILES
        self.quarter_tiles = self.half_tiles // 2
        self.half_rows = self.half_tiles * STATE
        self.quarter_rows = self.quarter_tiles * STATE
        self.width = self.groups * GROUP_COLS
        self.spans = (
            (self.first * GROUP_COLS, self.width),
            (INNER + self.first * STATE, self.groups * STATE),
        )


VMEM_LIMIT = 24 * 1024 * 1024
FLOPS, BYTES = 1e9, 3e6


def extra_rows(tiles):
    return -(-2 * tiles // 16) * 16


def decay_rows(tiles):
    return -(-tiles // 8) * 8


def call(body, outs, *args, after=(), hbm=(), cost=0.1, scratch=()):
    count = len(args)
    args = [pltpu.with_memory_space_constraint(a, pltpu.HBM) if i in hbm else a for i, a in enumerate(args)]
    specs = [pl.BlockSpec(memory_space=pltpu.HBM if i in hbm else pltpu.VMEM) for i in range(count)]
    specs += [pl.BlockSpec(memory_space=pl.ANY) for _ in after]

    def kernel(*refs):
        body(*refs[:count], *refs[count + len(after) :])

    return pl.pallas_call(
        kernel,
        out_shape=[space(shape, kind) for shape, kind, space in outs],
        in_specs=specs,
        out_specs=[pl.BlockSpec(memory_space=space) for _, _, space in outs],
        scratch_shapes=list(scratch),
        compiler_params=pltpu.CompilerParams(vmem_limit_bytes=VMEM_LIMIT),
        cost_estimate=pl.CostEstimate(flops=int(cost * FLOPS), bytes_accessed=int(cost * BYTES), transcendentals=0),
    )(*args, *after)


def vmem(rows, cols, kind):
    return ((rows, cols), kind, pltpu.VMEM)


def dot(a, b, dims=((1,), (0,))):
    return lax.dot_general(a, b, (dims, ((), ())), preferred_element_type=F32)


def silu(v):
    return silu_of_twice(0.5 * v)


def pieces(v, count):
    found = []
    for _ in range(count):
        piece = v.astype(BF16)
        found.append(piece)
        v = v - piece.astype(F32)
    return found


def columns(group, width, start=0):
    return pl.ds(pl.multiple_of(start + group * width, LANES), width)


def silu_of_twice(half):
    return half + half * jnp.tanh(half)


def halved_taps(weight, bias, cols):
    return 0.5 * weight[:, cols].astype(F32), 0.5 * bias[:, cols]


def convolve_into(rows, padded, weight, bias, cols):
    taps, total = halved_taps(weight, bias, cols)
    for tap in range(4):
        total = total + taps[tap : tap + 1] * padded[5 + tap : 5 + tap + rows, :]
    return silu_of_twice(total).astype(BF16)


def accurate_log1p(u):
    w = 1.0 + u
    return jnp.where(w == 1.0, u, jnp.log(w) * (u / jnp.where(w == 1.0, 1.0, w - 1.0)))


def convolve_body(source, weight, bias, spans, outs):
    for (start, width), out in zip(spans, outs):
        block = min(width, 256)

        @pl.loop(0, width // block)
        def _(i, start=start, out=out, block=block):
            cols = columns(i, block, start)
            here = source[:, cols].astype(F32)
            taps, total = halved_taps(weight, bias, cols)
            total = total + taps[3:4] * here
            for back in range(1, 4):
                total = total + taps[3 - back : 4 - back] * pltpu.roll(here, back, 0)
            out[:, columns(i, block)] = silu_of_twice(total).astype(BF16)


def convolve_head(source, halo, weight, bias, padded, spans, outs):
    first = lax.axis_index("seq") == 0
    for (start, width), out in zip(spans, outs):
        block = min(width, 512)

        @pl.loop(0, width // block)
        def _(i, start=start, out=out, block=block):
            cols = columns(i, block, start)
            here = padded.at[:, 0:block]
            here[0:8, :] = jnp.zeros((8, block), F32)
            here[5:8, :] = jnp.where(first, 0.0, halo[:, cols].astype(F32))
            here[8:24, :] = source[0:16, cols].astype(F32)
            out[0:16, columns(i, block)] = convolve_into(16, here, weight, bias, cols)


def prepare(
    parts, x, raw_t, step_bias, decay_log, skip, weight_in, bias_in,
    held, weight, bias, both, both_t, tail_pair, carry_pair, row_pair, spread, *refs,
):
    *outs, raw_here, small, sems = refs
    spans = [span for part in parts for span in part.spans]
    copies = [
        pltpu.make_async_copy(raw_t, raw_here, sems.at[0]),
        pltpu.make_async_copy(step_bias, small.at[0:1], sems.at[1]),
        pltpu.make_async_copy(decay_log, small.at[8:9], sems.at[2]),
        pltpu.make_async_copy(skip, small.at[16:17], sems.at[3]),
        pltpu.make_async_copy(weight_in, weight, sems.at[4]),
        pltpu.make_async_copy(bias_in, bias, sems.at[5]),
    ]
    for i, (start, width) in enumerate(spans + [(INNER + KEYS, KEYS)]):
        cols = slice(start, start + width)
        copies.append(pltpu.make_async_copy(x.at[:, cols], held.at[:, cols], sems.at[6 + i]))
    for copy in copies:
        copy.start()
    channel = lax.broadcasted_iota(jnp.int32, (2 * HEADS, GROUP_COLS), 1)
    head = (lax.broadcasted_iota(jnp.int32, (2 * HEADS, GROUP_COLS), 0) & (HEADS - 1)) - channel // HEAD_DIM
    for group in range(GROUPS):
        spread[:, group * GROUP_COLS : (group + 1) * GROUP_COLS] = (head == group * PER_GROUP).astype(BF16)
    for copy in copies[:4]:
        copy.wait()
    raw = raw_here[...].astype(F32)
    raw = jnp.concatenate([raw, raw], axis=0).T[:, :HEADS] + small[0:1, :]
    sizes = jnp.maximum(raw, 0.0) + accurate_log1p(jnp.exp(-jnp.abs(raw)))
    log_decay = sizes * -jnp.exp(small[8:9, :])
    row = lax.broadcasted_iota(jnp.int32, (SPAN, SPAN), 0)
    lane = lax.broadcasted_iota(jnp.int32, (SPAN, SPAN), 1)
    lower = (row >= lane).astype(BF16)
    cumulative = sum(dot(lower, piece) for piece in pieces(log_decay, 3))
    total = cumulative[SPAN - 1 : SPAN, :]
    tail = jnp.exp(total - cumulative) * sizes
    joined = jnp.concatenate([cumulative, sizes], axis=1)
    both[...] = joined
    both_t[...] = joined.T
    tail_pair[...] = jnp.concatenate(pieces(tail, 2), axis=1)
    carry_pair[...] = jnp.concatenate(pieces(jnp.exp(cumulative), 2), axis=1)
    rows = jnp.concatenate(
        [jnp.broadcast_to(jnp.exp(total), (8, HEADS)), jnp.broadcast_to(small[16:17, :], (8, HEADS))], axis=0
    )
    row_pair[...] = jnp.concatenate(pieces(rows, 2), axis=1)
    for copy in copies[4:6]:
        copy.wait()
    for i, (span, out) in enumerate(zip(spans, outs)):
        copies[6 + i].wait()
        convolve_body(held, weight, bias, [span], [out])
    copies[-1].wait()


def convolve_reads(held, halo, weight, bias, reads, padded):
    spans = [(INNER + KEYS, KEYS)]
    convolve_body(held, weight, bias, spans, [reads])
    convolve_head(held, halo, weight, bias, padded, spans, [reads])


def put_decays(send, tiles, decays):
    high = [d.astype(BF16).astype(F32) for d in decays]
    low = [d - h for d, h in zip(decays, high)]
    rows = high + low
    spare = extra_rows(tiles) - len(rows)
    block = jnp.concatenate(rows + [jnp.zeros((spare, LANES), F32)] * (spare > 0), axis=0)
    send[tiles * STATE : tiles * STATE + extra_rows(tiles), :] = block.astype(BF16)


def increments(part, *refs):
    held, halo, weight, bias, raw_values, raw_keys = refs[:6]
    tail_pair, row_pair, spread, send, keep, keep_decay, values_ref, keys_ref = refs[6:14]
    scaled, padded, value_fix, key_fix = refs[14:]
    convolve_head(held, halo, weight, bias, padded, part.spans, (value_fix, key_fix))
    keys_ref[0:16, :] = key_fix[...]
    keys_ref[16:, :] = raw_keys[16:, :]
    core = lax.axis_index("seq") & 1
    targets = ((send, 1 - core), (keep, core))
    order = [(target, side * part.half_groups + j, j) for target, side in targets for j in range(part.half_groups)]
    for i, (_, local, _) in enumerate(order):
        cols = columns(local, GROUP_COLS)
        scale = dot(tail_pair[...], spread[:, columns(part.first + local, GROUP_COLS)])
        values = jnp.concatenate([value_fix[:, cols], raw_values[16:, cols]], axis=0)
        values_ref[:, cols] = values
        scaled[i] = (values.astype(F32) * scale).astype(BF16)
    for target, side in targets:
        decay = dot(
            row_pair[...],
            spread[:, columns((part.first + side * part.half_groups) // part.half_groups, part.width // 2)],
        )
        decays = [decay[0:1, t * LANES : (t + 1) * LANES] for t in range(part.half_tiles)]
        if target is send:
            put_decays(send, part.half_tiles, decays)
        else:
            for t, d in enumerate(decays):
                keep_decay[t : t + 1, :] = d
    for i, (target, local, j) in enumerate(order):
        grown = dot(keys_ref[:, columns(local, STATE)], scaled[i], ((0,), (0,)))
        for t in range(TILES):
            at = (j * TILES + t) * STATE
            target[at : at + STATE, :] = grown[:, t * LANES : (t + 1) * LANES].astype(target.dtype)


def tile_rows(t):
    return pl.ds(pl.multiple_of(t * STATE, STATE), STATE)


def received_decays(recv, tiles, scratch):
    rows = recv[tiles * STATE : tiles * STATE + extra_rows(tiles), :].astype(F32)
    scratch[0:tiles, :] = rows[0:tiles] + rows[tiles : 2 * tiles]


def join_cores(part, keep, keep_decay, recv, send, own, own_decay, other):
    me = lax.axis_index("seq")
    first = (me & 1) == 0
    y = (me >> 1) & 1
    received_decays(recv, part.half_tiles, other)

    def joined(t):
        mine, theirs = keep[tile_rows(t), :], recv[tile_rows(t), :].astype(F32)
        decay_mine, decay_theirs = keep_decay[pl.ds(t, 1), :], other[pl.ds(t, 1), :]
        early, late = jnp.where(first, mine, theirs), jnp.where(first, theirs, mine)
        return jnp.where(first, decay_theirs, decay_mine) * early + late, decay_mine * decay_theirs

    decays = []
    for t in range(part.quarter_tiles):
        state, decay = joined((1 - y) * part.quarter_tiles + t)
        send[t * STATE : (t + 1) * STATE, :] = state.astype(BF16)
        decays.append(decay)
    put_decays(send, part.quarter_tiles, decays)
    for t in range(part.quarter_tiles):
        state, decay = joined(y * part.quarter_tiles + t)
        own[t * STATE : (t + 1) * STATE, :] = state
        own_decay[t : t + 1, :] = decay


def join_pair(part, bit, carried, totals, *refs):
    state, decay, recv = refs[:3]
    refs = refs[3:]
    if carried:
        before, before_decay = refs[:2]
        refs = refs[2:]
    send = refs[0]
    refs = refs[1:]
    if totals:
        new_state, new_decay = refs[:2]
        refs = refs[2:]
    if bit >= 2:
        new_before, new_before_decay = refs[:2]
        refs = refs[2:]
    (other,) = refs
    upper = ((lax.axis_index("seq") >> bit) & 1) == 1
    received_decays(recv, part.quarter_tiles, other)
    decays = []
    for t in range(part.quarter_tiles):
        rows = slice(t * STATE, (t + 1) * STATE)
        mine, theirs = state[rows, :], recv[rows, :].astype(F32)
        d_mine, d_theirs = decay[t : t + 1, :], other[t : t + 1, :]
        early, late = jnp.where(upper, theirs, mine), jnp.where(upper, mine, theirs)
        total = jnp.where(upper, d_mine, d_theirs) * early + late
        send[rows, :] = total.astype(BF16)
        if totals:
            new_state[rows, :] = total
            new_decay[t : t + 1, :] = d_mine * d_theirs
        decays.append(d_mine * d_theirs)
        if bit >= 2:
            if carried:
                b, bd = before[rows, :], before_decay[t : t + 1, :]
                new_before[rows, :] = jnp.where(upper, b + bd * theirs, b)
                new_before_decay[t : t + 1, :] = jnp.where(upper, bd * d_theirs, bd)
            else:
                new_before[rows, :] = jnp.where(upper, theirs, 0.0)
                new_before_decay[t : t + 1, :] = jnp.where(upper, d_theirs, 1.0)
    if totals:
        put_decays(send, part.quarter_tiles, decays)


def to_planes(part, bit, carried, *refs):
    recv = refs[0]
    refs = refs[1:]
    if carried:
        before, before_decay = refs[:2]
        refs = refs[2:]
    own, own_decay, recv_pair, send, start, other = refs
    me = lax.axis_index("seq")
    upper = ((me >> bit) & 1) == 1
    y = ((me >> 1) & 1) == 1
    received_decays(recv_pair, part.quarter_tiles, other)
    for t in range(part.quarter_tiles):
        rows = slice(t * STATE, (t + 1) * STATE)
        theirs = recv[rows, :].astype(F32)
        if carried:
            b = before[rows, :]
            plane = jnp.where(upper, b + before_decay[t : t + 1, :] * theirs, b)
        else:
            plane = jnp.where(upper, theirs, 0.0)
        d = jnp.where(y, other[t : t + 1, :], own_decay[t : t + 1, :])
        grown = jnp.where(y, recv_pair[rows, :].astype(F32), own[rows, :])
        later = d * plane + grown
        send[rows, :] = jnp.where(y, plane, later).astype(BF16)
        start[rows, :] = jnp.where(y, later, plane)


def to_cores(part, start, recv_start, keep, keep_decay, recv, send, own, other):
    me = lax.axis_index("seq")
    first = (me & 1) == 0
    y = (me >> 1) & 1
    received_decays(recv, part.half_tiles, other)
    for side in range(2):
        for t in range(part.quarter_tiles):
            rows = slice(t * STATE, (t + 1) * STATE)
            at = (y if side == 0 else 1 - y) * part.quarter_tiles + t
            chip = start[rows, :] if side == 0 else recv_start[rows, :].astype(F32)
            d = jnp.where(first, keep_decay[pl.ds(at, 1), :], other[pl.ds(at, 1), :])
            grown = jnp.where(first, keep[tile_rows(at), :], recv[tile_rows(at), :].astype(F32))
            later = d * chip + grown
            send[tile_rows(at), :] = jnp.where(first, later, chip).astype(BF16)
            own[tile_rows(at), :] = jnp.where(first, chip, later).astype(BF16)


def inside(part, values_ref, keys_ref, reads_ref, both, both_t, carry_pair, row_pair, spread, gate, base, slope):
    row = lax.broadcasted_iota(jnp.int32, (SPAN, SPAN), 0)
    lane = lax.broadcasted_iota(jnp.int32, (SPAN, SPAN), 1)
    causal = row >= lane
    for j in range(part.groups):
        group = part.first + j
        cols = slice(j * GROUP_COLS, (j + 1) * GROUP_COLS)
        values = values_ref[:, cols]
        writes = keys_ref[:, j * STATE : (j + 1) * STATE]
        reads = reads_ref[:, group * STATE : (group + 1) * STATE]
        scores = dot(reads, writes, ((1,), (1,)))
        found = []
        for i in range(PER_GROUP):
            h = group * PER_GROUP + i
            gap = both[:, h : h + 1] - both_t[h : h + 1, :]
            weights = scores * jnp.exp(jnp.where(causal, gap, -jnp.inf)) * both_t[HEADS + h : HEADS + h + 1, :]
            found.append(dot(weights.astype(BF16), values[:, i * HEAD_DIM : (i + 1) * HEAD_DIM]))
        within = jnp.concatenate(found, axis=1)
        to_channels = spread[:, group * GROUP_COLS : (group + 1) * GROUP_COLS]
        skip = dot(row_pair[...], to_channels)[8:9, :]
        opened = silu(gate[:, group * GROUP_COLS : (group + 1) * GROUP_COLS].astype(F32))
        base[:, cols] = (within + skip * values.astype(F32)) * opened
        slope[:, cols] = dot(carry_pair[...], to_channels) * opened


def finish(part, mine, reads_ref, source, base, slope, gain, made):
    core = lax.axis_index("seq") & 1
    side = core if mine else 1 - core
    for j in range(part.half_groups):
        local = side * part.half_groups + j
        group = part.first + local
        cols = columns(local, GROUP_COLS)
        starts = jnp.concatenate(
            [source[(j * TILES + t) * STATE : (j * TILES + t + 1) * STATE, :] for t in range(TILES)], axis=1
        )
        gated = base[:, cols] + slope[:, cols] * dot(reads_ref[:, columns(group, STATE)], starts)
        mean = jnp.mean(gated * gated, axis=1, keepdims=True)
        normed = gated * lax.rsqrt(mean + 1e-5) * gain[:, columns(group, GROUP_COLS)]
        made[:, j * GROUP_COLS : (j + 1) * GROUP_COLS] = normed.astype(BF16)


def finish_last(part, others, *refs):
    count = len(others)
    arrays, out, made, sems = refs[:count], refs[-3], refs[-2], refs[-1]
    core = lax.axis_index("seq") & 1

    def copy_out(i, other, mine, array):
        group = other.first + (core if mine else 1 - core) * other.half_groups
        return pltpu.make_async_copy(
            array, out.at[:, pl.ds(pl.multiple_of(group * GROUP_COLS, GROUP_COLS), other.width // 2)], sems.at[i]
        )

    copies = [copy_out(i, *other, array) for i, (other, array) in enumerate(zip(others, arrays))]
    for copy in copies:
        copy.start()
    finish(part, False, *refs[count:-3], made)
    copies.append(copy_out(count, part, False, made))
    copies[-1].start()
    for copy in copies:
        copy.wait()


ORDER = (
    "I0", "I1", "A0", "A1", "B0", "R0", "W0", "B1", "C0", "C1", "W1", "S0", "S1",
    "H0", "H1", "E0", "F0", "E1", "F1",
)


def shards(mixer_input, gate_input, step_raw, conv_weight, conv_bias, step_bias, decay_log, skip_gain, norm_gain):
    devices = lax.axis_size("seq")
    bits = devices.bit_length() - 1
    parts = [Part(i) for i in range(len(SIZES))]

    def across(value, bit):
        flipped = 1 << bit if bit < 2 else (2 << bit) - 4
        return lax.ppermute(value, "seq", [(i, i ^ flipped) for i in range(devices)])

    padded = pltpu.VMEM((24, 512), F32)

    def decays_of(tiles):
        return vmem(decay_rows(tiles), LANES, F32)

    def decay_scratch(tiles):
        return [pltpu.VMEM((decay_rows(tiles), LANES), F32)]

    def rows_of(p):
        return [vmem(SPAN, p.width, BF16), vmem(SPAN, p.groups * STATE, BF16)]

    def half_send(p):
        return vmem(p.half_rows + extra_rows(p.half_tiles), LANES, BF16)

    def quarter_send(p):
        return vmem(p.quarter_rows + extra_rows(p.quarter_tiles), LANES, BF16)

    def quarter(p):
        return [vmem(p.quarter_rows, LANES, F32), decays_of(p.quarter_tiles)]

    halo = lax.ppermute(mixer_input[SPAN - 3 :], "seq", [(i, (i + 1) % devices) for i in range(devices)])
    held, weight, bias, both, both_t, tail_pair, carry_pair, row_pair, spread, *raw = call(
        functools.partial(prepare, parts),
        [
            vmem(SPAN, CONV_COLS, BF16),
            vmem(4, CONV_COLS, BF16),
            vmem(1, CONV_COLS, F32),
            vmem(SPAN, 2 * HEADS, F32),
            vmem(2 * HEADS, SPAN, F32),
            vmem(SPAN, 2 * HEADS, BF16),
            vmem(SPAN, 2 * HEADS, BF16),
            vmem(16, 2 * HEADS, BF16),
            vmem(2 * HEADS, INNER, BF16),
            *[shape for p in parts for shape in rows_of(p)],
        ],
        mixer_input, step_raw.T, step_bias[None, :], decay_log[None, :], skip_gain[None, :],
        conv_weight, conv_bias[None, :],
        hbm=range(7),
        cost=2.5,
        scratch=[
            pltpu.VMEM((HEADS, SPAN), BF16),
            pltpu.VMEM((24, HEADS), F32),
            pltpu.SemaphoreType.DMA((7 + 2 * len(parts),)),
        ],
    )
    gain = norm_gain[None, :]
    have = {}
    token = ()
    results = []
    for stage in ORDER:
        kind, p = stage[0], parts[int(stage[1:])]
        n = p.index
        get = lambda name: have[name, n]

        def put(**values):
            have.update({(name, n): value for name, value in values.items()})

        if kind == "R":
            (reads,) = call(
                convolve_reads, [vmem(SPAN, KEYS, BF16)], held, halo, weight, bias,
                after=token, cost=0.6, scratch=[padded],
            )
            token = (reads,)
        elif kind == "I":
            send, keep, keep_decay, values, keys = call(
                functools.partial(increments, p),
                [half_send(p), vmem(p.half_rows, LANES, F32), decays_of(p.half_tiles), *rows_of(p)],
                held, halo, weight, bias, *raw[2 * n : 2 * n + 2], tail_pair, row_pair, spread,
                after=token, cost=0.2 * p.groups,
                scratch=[
                    pltpu.VMEM((p.groups, SPAN, GROUP_COLS), BF16),
                    padded,
                    pltpu.VMEM((16, p.width), BF16),
                    pltpu.VMEM((16, p.groups * STATE), BF16),
                ],
            )
            put(values=values, keys=keys, kept=(keep, keep_decay, across(send, 0)))
            token = (keep_decay,)
        elif kind == "A":
            send, own, own_decay = call(
                functools.partial(join_cores, p), [quarter_send(p), *quarter(p)], *get("kept"),
                after=token, scratch=decay_scratch(p.half_tiles),
            )
            put(own=(own, own_decay, across(send, 1)), bit=1, carried=())
            have["state", n] = have["own", n]
            token = (own_decay,)
        elif kind in "BC":
            for bit in range(1, 2) if kind == "B" else range(2, bits - 1):
                totals, carried = bit + 1 < bits - 1, get("carried")
                outs = call(
                    functools.partial(join_pair, p, bit, bool(carried), totals),
                    [quarter_send(p) if totals else vmem(p.quarter_rows, LANES, BF16)] + quarter(p) * totals + quarter(p) * (bit >= 2),
                    *get("state"), *carried, after=token, scratch=decay_scratch(p.quarter_tiles),
                )
                recv = across(outs[0], bit + 1)
                put(
                    state=(*(outs[1:3] if totals else (None, None)), recv),
                    carried=tuple(outs[-2:]) if bit >= 2 else (),
                )
                token = (outs[-1],) if len(outs) > 1 else (outs[0],)
        elif kind == "S":
            send, start = call(
                functools.partial(to_planes, p, bits - 1, bool(get("carried"))),
                [vmem(p.quarter_rows, LANES, BF16), quarter(p)[0]],
                get("state")[2], *get("carried"), *get("own"),
                after=token, scratch=decay_scratch(p.quarter_tiles),
            )
            put(start=(start, across(send, 1)))
            token = (start,)
        elif kind == "H":
            send, own_start = call(
                functools.partial(to_cores, p), [vmem(p.half_rows, LANES, BF16)] * 2, *get("start"), *get("kept"),
                after=token, scratch=decay_scratch(p.half_tiles),
            )
            put(own_start=own_start, recv_start=across(send, 0))
            token = (own_start,)
        elif kind == "W":
            put(
                mixed=call(
                    functools.partial(inside, p), [vmem(SPAN, p.width, F32)] * 2,
                    get("values"), get("keys"), reads, both, both_t, carry_pair, row_pair, spread, gate_input,
                    after=token, cost=0.42 * p.groups,
                )
            )
            token = (get("mixed")[0],)
        elif kind in "EF" and len(results) < 2 * len(SIZES) - 1:
            name = "own_start" if kind == "E" else "recv_start"
            (made,) = call(
                functools.partial(finish, p, kind == "E"), [vmem(SPAN, p.width // 2, BF16)],
                reads, get(name), *get("mixed"), gain, after=token, cost=0.2 * p.half_groups,
            )
            results.append(((p, kind == "E"), made))
            token = (made,)
        else:
            (out,) = call(
                functools.partial(finish_last, p, [where for where, _ in results]),
                [((SPAN, INNER), BF16, pltpu.HBM)],
                *[made for _, made in results], reads, get("recv_start"), *get("mixed"), gain,
                after=token, cost=0.2 * p.half_groups,
                scratch=[pltpu.VMEM((SPAN, p.width // 2), BF16), pltpu.SemaphoreType.DMA((2 * len(SIZES),))],
            )
    return out


def solution(mesh):
    in_specs = (
        P(("groups", "seq"), None),
        P(("groups", "seq"), None),
        P(("groups", "seq"), None),
        P(),
        P(),
        P("groups"),
        P("groups"),
        P(),
        P(),
    )
    return jax.shard_map(
        shards, mesh=mesh, in_specs=in_specs, out_specs=P(("groups", "seq"), None), check_vma=False
    )
```

```python
import functools

import jax
import jax.numpy as jnp
from jax import lax
from jax.experimental import pallas as pl
from jax.experimental.pallas import tpu as pltpu
from jax.sharding import PartitionSpec as P

HEADS = 64
HEAD_DIM = 64
STATE = 128
GROUPS = 8
PER_GROUP = HEADS // GROUPS
GROUP_COLS = PER_GROUP * HEAD_DIM
INNER = HEADS * HEAD_DIM
KEYS = GROUPS * STATE
CONV_COLS = INNER + 2 * KEYS
SPAN = 128
LANES = 128
TILES = GROUP_COLS // LANES
SIZES = (4, 4)
F32 = jnp.float32
BF16 = jnp.bfloat16


class Part:
    def __init__(self, index):
        self.index = index
        self.first = sum(SIZES[:index])
        self.groups = SIZES[index]
        self.half_groups = self.groups // 2
        self.half_tiles = self.half_groups * TILES
        self.quarter_tiles = self.half_tiles // 2
        self.half_rows = self.half_tiles * STATE
        self.quarter_rows = self.quarter_tiles * STATE
        self.width = self.groups * GROUP_COLS
        self.spans = (
            (self.first * GROUP_COLS, self.width),
            (INNER + self.first * STATE, self.groups * STATE),
        )


VMEM_LIMIT = 24 * 1024 * 1024
FLOPS, BYTES = 1e9, 3e6


def extra_rows(tiles):
    return -(-2 * tiles // 16) * 16


def decay_rows(tiles):
    return -(-tiles // 8) * 8


def call(body, outs, *args, after=(), hbm=(), cost=0.1, scratch=()):
    count = len(args)
    args = [pltpu.with_memory_space_constraint(a, pltpu.HBM) if i in hbm else a for i, a in enumerate(args)]
    specs = [pl.BlockSpec(memory_space=pltpu.HBM if i in hbm else pltpu.VMEM) for i in range(count)]
    specs += [pl.BlockSpec(memory_space=pl.ANY) for _ in after]

    def kernel(*refs):
        body(*refs[:count], *refs[count + len(after) :])

    return pl.pallas_call(
        kernel,
        out_shape=[space(shape, kind) for shape, kind, space in outs],
        in_specs=specs,
        out_specs=[pl.BlockSpec(memory_space=space) for _, _, space in outs],
        scratch_shapes=list(scratch),
        compiler_params=pltpu.CompilerParams(vmem_limit_bytes=VMEM_LIMIT),
        cost_estimate=pl.CostEstimate(flops=int(cost * FLOPS), bytes_accessed=int(cost * BYTES), transcendentals=0),
    )(*args, *after)


def vmem(rows, cols, kind):
    return ((rows, cols), kind, pltpu.VMEM)


def dot(a, b, dims=((1,), (0,))):
    return lax.dot_general(a, b, (dims, ((), ())), preferred_element_type=F32)


def silu(v):
    return silu_of_twice(0.5 * v)


def pieces(v, count):
    found = []
    for _ in range(count):
        piece = v.astype(BF16)
        found.append(piece)
        v = v - piece.astype(F32)
    return found


def columns(group, width, start=0):
    return pl.ds(pl.multiple_of(start + group * width, LANES), width)


def silu_of_twice(half):
    return half + half * jnp.tanh(half)


def halved_taps(weight, bias, cols):
    return 0.5 * weight[:, cols].astype(F32), 0.5 * bias[:, cols]


def convolve_into(rows, padded, weight, bias, cols):
    taps, total = halved_taps(weight, bias, cols)
    for tap in range(4):
        total = total + taps[tap : tap + 1] * padded[5 + tap : 5 + tap + rows, :]
    return silu_of_twice(total).astype(BF16)


def accurate_log1p(u):
    w = 1.0 + u
    return jnp.where(w == 1.0, u, jnp.log(w) * (u / jnp.where(w == 1.0, 1.0, w - 1.0)))


def convolve_body(source, weight, bias, spans, outs):
    for (start, width), out in zip(spans, outs):
        block = min(width, 256)

        @pl.loop(0, width // block)
        def _(i, start=start, out=out, block=block):
            cols = columns(i, block, start)
            here = source[:, cols].astype(F32)
            taps, total = halved_taps(weight, bias, cols)
            total = total + taps[3:4] * here
            for back in range(1, 4):
                total = total + taps[3 - back : 4 - back] * pltpu.roll(here, back, 0)
            out[:, columns(i, block)] = silu_of_twice(total).astype(BF16)


def convolve_head(source, halo, weight, bias, padded, spans, outs):
    first = lax.axis_index("seq") == 0
    for (start, width), out in zip(spans, outs):
        block = min(width, 512)

        @pl.loop(0, width // block)
        def _(i, start=start, out=out, block=block):
            cols = columns(i, block, start)
            here = padded.at[:, 0:block]
            here[0:8, :] = jnp.zeros((8, block), F32)
            here[5:8, :] = jnp.where(first, 0.0, halo[:, cols].astype(F32))
            here[8:24, :] = source[0:16, cols].astype(F32)
            out[0:16, columns(i, block)] = convolve_into(16, here, weight, bias, cols)


def take_last_rows(x, out, rows, sems):
    copy = pltpu.make_async_copy(x.at[SPAN - 16 : SPAN, :], rows, sems.at[0])
    copy.start()
    copy.wait()
    out[...] = rows[...].astype(F32)[13:16, :].astype(BF16)


def prepare(
    parts, x, raw_t, step_bias, decay_log, skip, weight_in, bias_in,
    held, weight, bias, both, both_t, tail_pair, carry_pair, row_pair, spread, *refs,
):
    *outs, raw_here, small, sems = refs
    spans = [span for part in parts for span in part.spans]
    copies = [
        pltpu.make_async_copy(raw_t, raw_here, sems.at[0]),
        pltpu.make_async_copy(step_bias, small.at[0:1], sems.at[1]),
        pltpu.make_async_copy(decay_log, small.at[8:9], sems.at[2]),
        pltpu.make_async_copy(skip, small.at[16:17], sems.at[3]),
        pltpu.make_async_copy(weight_in, weight, sems.at[4]),
        pltpu.make_async_copy(bias_in, bias, sems.at[5]),
    ]
    for i, (start, width) in enumerate(spans + [(INNER + KEYS, KEYS)]):
        cols = slice(start, start + width)
        copies.append(pltpu.make_async_copy(x.at[:, cols], held.at[:, cols], sems.at[6 + i]))
    for copy in copies:
        copy.start()
    channel = lax.broadcasted_iota(jnp.int32, (2 * HEADS, GROUP_COLS), 1)
    head = (lax.broadcasted_iota(jnp.int32, (2 * HEADS, GROUP_COLS), 0) & (HEADS - 1)) - channel // HEAD_DIM
    for group in range(GROUPS):
        spread[:, group * GROUP_COLS : (group + 1) * GROUP_COLS] = (head == group * PER_GROUP).astype(BF16)
    for copy in copies[:4]:
        copy.wait()
    raw = raw_here[...].astype(F32)
    raw = jnp.concatenate([raw, raw], axis=0).T[:, :HEADS] + small[0:1, :]
    sizes = jnp.maximum(raw, 0.0) + accurate_log1p(jnp.exp(-jnp.abs(raw)))
    log_decay = sizes * -jnp.exp(small[8:9, :])
    row = lax.broadcasted_iota(jnp.int32, (SPAN, SPAN), 0)
    lane = lax.broadcasted_iota(jnp.int32, (SPAN, SPAN), 1)
    lower = (row >= lane).astype(BF16)
    cumulative = sum(dot(lower, piece) for piece in pieces(log_decay, 3))
    total = cumulative[SPAN - 1 : SPAN, :]
    tail = jnp.exp(total - cumulative) * sizes
    joined = jnp.concatenate([cumulative, sizes], axis=1)
    both[...] = joined
    both_t[...] = joined.T
    tail_pair[...] = jnp.concatenate(pieces(tail, 2), axis=1)
    carry_pair[...] = jnp.concatenate(pieces(jnp.exp(cumulative), 2), axis=1)
    rows = jnp.concatenate(
        [jnp.broadcast_to(jnp.exp(total), (8, HEADS)), jnp.broadcast_to(small[16:17, :], (8, HEADS))], axis=0
    )
    row_pair[...] = jnp.concatenate(pieces(rows, 2), axis=1)
    for copy in copies[4:6]:
        copy.wait()
    for i, (span, out) in enumerate(zip(spans, outs)):
        copies[6 + i].wait()
        convolve_body(held, weight, bias, [span], [out])
    copies[-1].wait()


def convolve_reads(held, halo, weight, bias, reads, padded):
    spans = [(INNER + KEYS, KEYS)]
    convolve_body(held, weight, bias, spans, [reads])
    convolve_head(held, halo, weight, bias, padded, spans, [reads])


def put_decays(send, tiles, decays):
    high = [d.astype(BF16).astype(F32) for d in decays]
    low = [d - h for d, h in zip(decays, high)]
    rows = high + low
    spare = extra_rows(tiles) - len(rows)
    block = jnp.concatenate(rows + [jnp.zeros((spare, LANES), F32)] * (spare > 0), axis=0)
    send[tiles * STATE : tiles * STATE + extra_rows(tiles), :] = block.astype(BF16)


def increments(part, *refs):
    held, halo, weight, bias, raw_values, raw_keys = refs[:6]
    tail_pair, row_pair, spread, send, keep, keep_decay, values_ref, keys_ref = refs[6:14]
    scaled, padded, value_fix, key_fix = refs[14:]
    convolve_head(held, halo, weight, bias, padded, part.spans, (value_fix, key_fix))
    keys_ref[0:16, :] = key_fix[...]
    keys_ref[16:, :] = raw_keys[16:, :]
    core = lax.axis_index("seq") & 1
    targets = ((send, 1 - core), (keep, core))
    order = [(target, side * part.half_groups + j, j) for target, side in targets for j in range(part.half_groups)]
    for i, (_, local, _) in enumerate(order):
        cols = columns(local, GROUP_COLS)
        scale = dot(tail_pair[...], spread[:, columns(part.first + local, GROUP_COLS)])
        values = jnp.concatenate([value_fix[:, cols], raw_values[16:, cols]], axis=0)
        values_ref[:, cols] = values
        scaled[i] = (values.astype(F32) * scale).astype(BF16)
    for target, side in targets:
        decay = dot(
            row_pair[...],
            spread[:, columns((part.first + side * part.half_groups) // part.half_groups, part.width // 2)],
        )
        decays = [decay[0:1, t * LANES : (t + 1) * LANES] for t in range(part.half_tiles)]
        if target is send:
            put_decays(send, part.half_tiles, decays)
        else:
            for t, d in enumerate(decays):
                keep_decay[t : t + 1, :] = d
    for i, (target, local, j) in enumerate(order):
        grown = dot(keys_ref[:, columns(local, STATE)], scaled[i], ((0,), (0,)))
        for t in range(TILES):
            at = (j * TILES + t) * STATE
            target[at : at + STATE, :] = grown[:, t * LANES : (t + 1) * LANES].astype(target.dtype)


def tile_rows(t):
    return pl.ds(pl.multiple_of(t * STATE, STATE), STATE)


def received_decays(recv, tiles, scratch):
    rows = recv[tiles * STATE : tiles * STATE + extra_rows(tiles), :].astype(F32)
    scratch[0:tiles, :] = rows[0:tiles] + rows[tiles : 2 * tiles]


def join_cores(part, keep, keep_decay, recv, send, own, own_decay, other):
    me = lax.axis_index("seq")
    first = (me & 1) == 0
    y = (me >> 1) & 1
    received_decays(recv, part.half_tiles, other)

    def joined(t):
        mine, theirs = keep[tile_rows(t), :], recv[tile_rows(t), :].astype(F32)
        decay_mine, decay_theirs = keep_decay[pl.ds(t, 1), :], other[pl.ds(t, 1), :]
        early, late = jnp.where(first, mine, theirs), jnp.where(first, theirs, mine)
        return jnp.where(first, decay_theirs, decay_mine) * early + late, decay_mine * decay_theirs

    decays = []
    for t in range(part.quarter_tiles):
        state, decay = joined((1 - y) * part.quarter_tiles + t)
        send[t * STATE : (t + 1) * STATE, :] = state.astype(BF16)
        decays.append(decay)
    put_decays(send, part.quarter_tiles, decays)
    for t in range(part.quarter_tiles):
        state, decay = joined(y * part.quarter_tiles + t)
        own[t * STATE : (t + 1) * STATE, :] = state
        own_decay[t : t + 1, :] = decay


def join_pair(part, bit, carried, totals, *refs):
    state, decay, recv = refs[:3]
    refs = refs[3:]
    if carried:
        before, before_decay = refs[:2]
        refs = refs[2:]
    send = refs[0]
    refs = refs[1:]
    if totals:
        new_state, new_decay = refs[:2]
        refs = refs[2:]
    if bit >= 2:
        new_before, new_before_decay = refs[:2]
        refs = refs[2:]
    (other,) = refs
    upper = ((lax.axis_index("seq") >> bit) & 1) == 1
    received_decays(recv, part.quarter_tiles, other)
    decays = []
    for t in range(part.quarter_tiles):
        rows = slice(t * STATE, (t + 1) * STATE)
        mine, theirs = state[rows, :], recv[rows, :].astype(F32)
        d_mine, d_theirs = decay[t : t + 1, :], other[t : t + 1, :]
        early, late = jnp.where(upper, theirs, mine), jnp.where(upper, mine, theirs)
        total = jnp.where(upper, d_mine, d_theirs) * early + late
        send[rows, :] = total.astype(BF16)
        if totals:
            new_state[rows, :] = total
            new_decay[t : t + 1, :] = d_mine * d_theirs
        decays.append(d_mine * d_theirs)
        if bit >= 2:
            if carried:
                b, bd = before[rows, :], before_decay[t : t + 1, :]
                new_before[rows, :] = jnp.where(upper, b + bd * theirs, b)
                new_before_decay[t : t + 1, :] = jnp.where(upper, bd * d_theirs, bd)
            else:
                new_before[rows, :] = jnp.where(upper, theirs, 0.0)
                new_before_decay[t : t + 1, :] = jnp.where(upper, d_theirs, 1.0)
    if totals:
        put_decays(send, part.quarter_tiles, decays)


def to_planes(part, bit, carried, *refs):
    recv = refs[0]
    refs = refs[1:]
    if carried:
        before, before_decay = refs[:2]
        refs = refs[2:]
    own, own_decay, recv_pair, send, start, other = refs
    me = lax.axis_index("seq")
    upper = ((me >> bit) & 1) == 1
    y = ((me >> 1) & 1) == 1
    received_decays(recv_pair, part.quarter_tiles, other)
    for t in range(part.quarter_tiles):
        rows = slice(t * STATE, (t + 1) * STATE)
        theirs = recv[rows, :].astype(F32)
        if carried:
            b = before[rows, :]
            plane = jnp.where(upper, b + before_decay[t : t + 1, :] * theirs, b)
        else:
            plane = jnp.where(upper, theirs, 0.0)
        d = jnp.where(y, other[t : t + 1, :], own_decay[t : t + 1, :])
        grown = jnp.where(y, recv_pair[rows, :].astype(F32), own[rows, :])
        later = d * plane + grown
        send[rows, :] = jnp.where(y, plane, later).astype(BF16)
        start[rows, :] = jnp.where(y, later, plane)


def to_cores(part, start, recv_start, keep, keep_decay, recv, send, own, other):
    me = lax.axis_index("seq")
    first = (me & 1) == 0
    y = (me >> 1) & 1
    received_decays(recv, part.half_tiles, other)
    for side in range(2):
        for t in range(part.quarter_tiles):
            rows = slice(t * STATE, (t + 1) * STATE)
            at = (y if side == 0 else 1 - y) * part.quarter_tiles + t
            chip = start[rows, :] if side == 0 else recv_start[rows, :].astype(F32)
            d = jnp.where(first, keep_decay[pl.ds(at, 1), :], other[pl.ds(at, 1), :])
            grown = jnp.where(first, keep[tile_rows(at), :], recv[tile_rows(at), :].astype(F32))
            later = d * chip + grown
            send[tile_rows(at), :] = jnp.where(first, later, chip).astype(BF16)
            own[tile_rows(at), :] = jnp.where(first, chip, later).astype(BF16)


def inside(part, values_ref, keys_ref, reads_ref, both, both_t, carry_pair, row_pair, spread, gate, base, slope):
    row = lax.broadcasted_iota(jnp.int32, (SPAN, SPAN), 0)
    lane = lax.broadcasted_iota(jnp.int32, (SPAN, SPAN), 1)
    causal = row >= lane
    for j in range(part.groups):
        group = part.first + j
        cols = slice(j * GROUP_COLS, (j + 1) * GROUP_COLS)
        values = values_ref[:, cols]
        writes = keys_ref[:, j * STATE : (j + 1) * STATE]
        reads = reads_ref[:, group * STATE : (group + 1) * STATE]
        scores = dot(reads, writes, ((1,), (1,)))
        found = []
        for i in range(PER_GROUP):
            h = group * PER_GROUP + i
            gap = both[:, h : h + 1] - both_t[h : h + 1, :]
            weights = scores * jnp.exp(jnp.where(causal, gap, -jnp.inf)) * both_t[HEADS + h : HEADS + h + 1, :]
            found.append(dot(weights.astype(BF16), values[:, i * HEAD_DIM : (i + 1) * HEAD_DIM]))
        within = jnp.concatenate(found, axis=1)
        to_channels = spread[:, group * GROUP_COLS : (group + 1) * GROUP_COLS]
        skip = dot(row_pair[...], to_channels)[8:9, :]
        opened = silu(gate[:, group * GROUP_COLS : (group + 1) * GROUP_COLS].astype(F32))
        base[:, cols] = (within + skip * values.astype(F32)) * opened
        slope[:, cols] = dot(carry_pair[...], to_channels) * opened


def finish(part, mine, reads_ref, source, base, slope, gain, made):
    core = lax.axis_index("seq") & 1
    side = core if mine else 1 - core
    for j in range(part.half_groups):
        local = side * part.half_groups + j
        group = part.first + local
        cols = columns(local, GROUP_COLS)
        starts = jnp.concatenate(
            [source[(j * TILES + t) * STATE : (j * TILES + t + 1) * STATE, :] for t in range(TILES)], axis=1
        )
        gated = base[:, cols] + slope[:, cols] * dot(reads_ref[:, columns(group, STATE)], starts)
        mean = jnp.mean(gated * gated, axis=1, keepdims=True)
        normed = gated * lax.rsqrt(mean + 1e-5) * gain[:, columns(group, GROUP_COLS)]
        made[:, j * GROUP_COLS : (j + 1) * GROUP_COLS] = normed.astype(BF16)


def finish_last(part, others, *refs):
    count = len(others)
    arrays, out, made, sems = refs[:count], refs[-3], refs[-2], refs[-1]
    core = lax.axis_index("seq") & 1

    def copy_out(i, other, mine, array):
        group = other.first + (core if mine else 1 - core) * other.half_groups
        return pltpu.make_async_copy(
            array, out.at[:, pl.ds(pl.multiple_of(group * GROUP_COLS, GROUP_COLS), other.width // 2)], sems.at[i]
        )

    copies = [copy_out(i, *other, array) for i, (other, array) in enumerate(zip(others, arrays))]
    for copy in copies:
        copy.start()
    finish(part, False, *refs[count:-3], made)
    copies.append(copy_out(count, part, False, made))
    copies[-1].start()
    for copy in copies:
        copy.wait()


ORDER = (
    "I0", "I1", "A0", "A1", "B0", "R0", "W0", "B1", "C0", "C1", "W1", "S0", "S1",
    "H0", "H1", "E0", "F0", "E1", "F1",
)


def shards(mixer_input, gate_input, step_raw, conv_weight, conv_bias, step_bias, decay_log, skip_gain, norm_gain):
    devices = lax.axis_size("seq")
    bits = devices.bit_length() - 1
    parts = [Part(i) for i in range(len(SIZES))]

    def across(value, bit):
        flipped = 1 << bit if bit < 2 else (2 << bit) - 4
        return lax.ppermute(value, "seq", [(i, i ^ flipped) for i in range(devices)])

    padded = pltpu.VMEM((24, 512), F32)

    def decays_of(tiles):
        return vmem(decay_rows(tiles), LANES, F32)

    def decay_scratch(tiles):
        return [pltpu.VMEM((decay_rows(tiles), LANES), F32)]

    def rows_of(p):
        return [vmem(SPAN, p.width, BF16), vmem(SPAN, p.groups * STATE, BF16)]

    def half_send(p):
        return vmem(p.half_rows + extra_rows(p.half_tiles), LANES, BF16)

    def quarter_send(p):
        return vmem(p.quarter_rows + extra_rows(p.quarter_tiles), LANES, BF16)

    def quarter(p):
        return [vmem(p.quarter_rows, LANES, F32), decays_of(p.quarter_tiles)]

    (last_rows,) = call(
        take_last_rows, [vmem(3, CONV_COLS, BF16)], mixer_input, hbm=(0,),
        scratch=[pltpu.VMEM((16, CONV_COLS), BF16), pltpu.SemaphoreType.DMA((1,))],
    )
    halo = lax.ppermute(last_rows, "seq", [(i, (i + 1) % devices) for i in range(devices)])
    held, weight, bias, both, both_t, tail_pair, carry_pair, row_pair, spread, *raw = call(
        functools.partial(prepare, parts),
        [
            vmem(SPAN, CONV_COLS, BF16),
            vmem(4, CONV_COLS, BF16),
            vmem(1, CONV_COLS, F32),
            vmem(SPAN, 2 * HEADS, F32),
            vmem(2 * HEADS, SPAN, F32),
            vmem(SPAN, 2 * HEADS, BF16),
            vmem(SPAN, 2 * HEADS, BF16),
            vmem(16, 2 * HEADS, BF16),
            vmem(2 * HEADS, INNER, BF16),
            *[shape for p in parts for shape in rows_of(p)],
        ],
        mixer_input, step_raw.T, step_bias[None, :], decay_log[None, :], skip_gain[None, :],
        conv_weight, conv_bias[None, :],
        hbm=range(7),
        cost=2.5,
        scratch=[
            pltpu.VMEM((HEADS, SPAN), BF16),
            pltpu.VMEM((24, HEADS), F32),
            pltpu.SemaphoreType.DMA((7 + 2 * len(parts),)),
        ],
    )
    gain = norm_gain[None, :]
    have = {}
    token = ()
    results = []
    for stage in ORDER:
        kind, p = stage[0], parts[int(stage[1:])]
        n = p.index
        get = lambda name: have[name, n]

        def put(**values):
            have.update({(name, n): value for name, value in values.items()})

        if kind == "R":
            (reads,) = call(
                convolve_reads, [vmem(SPAN, KEYS, BF16)], held, halo, weight, bias,
                after=token, cost=0.6, scratch=[padded],
            )
            token = (reads,)
        elif kind == "I":
            send, keep, keep_decay, values, keys = call(
                functools.partial(increments, p),
                [half_send(p), vmem(p.half_rows, LANES, F32), decays_of(p.half_tiles), *rows_of(p)],
                held, halo, weight, bias, *raw[2 * n : 2 * n + 2], tail_pair, row_pair, spread,
                after=token, cost=0.2 * p.groups,
                scratch=[
                    pltpu.VMEM((p.groups, SPAN, GROUP_COLS), BF16),
                    padded,
                    pltpu.VMEM((16, p.width), BF16),
                    pltpu.VMEM((16, p.groups * STATE), BF16),
                ],
            )
            put(values=values, keys=keys, kept=(keep, keep_decay, across(send, 0)))
            token = (keep_decay,)
        elif kind == "A":
            send, own, own_decay = call(
                functools.partial(join_cores, p), [quarter_send(p), *quarter(p)], *get("kept"),
                after=token, scratch=decay_scratch(p.half_tiles),
            )
            put(own=(own, own_decay, across(send, 1)), bit=1, carried=())
            have["state", n] = have["own", n]
            token = (own_decay,)
        elif kind in "BC":
            for bit in range(1, 2) if kind == "B" else range(2, bits - 1):
                totals, carried = bit + 1 < bits - 1, get("carried")
                outs = call(
                    functools.partial(join_pair, p, bit, bool(carried), totals),
                    [quarter_send(p) if totals else vmem(p.quarter_rows, LANES, BF16)] + quarter(p) * totals + quarter(p) * (bit >= 2),
                    *get("state"), *carried, after=token, scratch=decay_scratch(p.quarter_tiles),
                )
                recv = across(outs[0], bit + 1)
                put(
                    state=(*(outs[1:3] if totals else (None, None)), recv),
                    carried=tuple(outs[-2:]) if bit >= 2 else (),
                )
                token = (outs[-1],) if len(outs) > 1 else (outs[0],)
        elif kind == "S":
            send, start = call(
                functools.partial(to_planes, p, bits - 1, bool(get("carried"))),
                [vmem(p.quarter_rows, LANES, BF16), quarter(p)[0]],
                get("state")[2], *get("carried"), *get("own"),
                after=token, scratch=decay_scratch(p.quarter_tiles),
            )
            put(start=(start, across(send, 1)))
            token = (start,)
        elif kind == "H":
            send, own_start = call(
                functools.partial(to_cores, p), [vmem(p.half_rows, LANES, BF16)] * 2, *get("start"), *get("kept"),
                after=token, scratch=decay_scratch(p.half_tiles),
            )
            put(own_start=own_start, recv_start=across(send, 0))
            token = (own_start,)
        elif kind == "W":
            put(
                mixed=call(
                    functools.partial(inside, p), [vmem(SPAN, p.width, F32)] * 2,
                    get("values"), get("keys"), reads, both, both_t, carry_pair, row_pair, spread, gate_input,
                    after=token, cost=0.42 * p.groups,
                )
            )
            token = (get("mixed")[0],)
        elif kind in "EF" and len(results) < 2 * len(SIZES) - 1:
            name = "own_start" if kind == "E" else "recv_start"
            (made,) = call(
                functools.partial(finish, p, kind == "E"), [vmem(SPAN, p.width // 2, BF16)],
                reads, get(name), *get("mixed"), gain, after=token, cost=0.2 * p.half_groups,
            )
            results.append(((p, kind == "E"), made))
            token = (made,)
        else:
            (out,) = call(
                functools.partial(finish_last, p, [where for where, _ in results]),
                [((SPAN, INNER), BF16, pltpu.HBM)],
                *[made for _, made in results], reads, get("recv_start"), *get("mixed"), gain,
                after=token, cost=0.2 * p.half_groups,
                scratch=[pltpu.VMEM((SPAN, p.width // 2), BF16), pltpu.SemaphoreType.DMA((2 * len(SIZES),))],
            )
    return out


def solution(mesh):
    in_specs = (
        P(("groups", "seq"), None),
        P(("groups", "seq"), None),
        P(("groups", "seq"), None),
        P(),
        P(),
        P("groups"),
        P("groups"),
        P(),
        P(),
    )
    return jax.shard_map(
        shards, mesh=mesh, in_specs=in_specs, out_specs=P(("groups", "seq"), None), check_vma=False
    )
```

```python
import functools

import jax
import jax.numpy as jnp
from jax import lax
from jax.experimental import pallas as pl
from jax.experimental.pallas import tpu as pltpu
from jax.sharding import PartitionSpec as P

HEADS = 64
HEAD_DIM = 64
STATE = 128
GROUPS = 8
PER_GROUP = HEADS // GROUPS
GROUP_COLS = PER_GROUP * HEAD_DIM
INNER = HEADS * HEAD_DIM
KEYS = GROUPS * STATE
CONV_COLS = INNER + 2 * KEYS
SPAN = 128
LANES = 128
TILES = GROUP_COLS // LANES
SIZES = (4, 4)
F32 = jnp.float32
BF16 = jnp.bfloat16


class Part:
    def __init__(self, index):
        self.index = index
        self.first = sum(SIZES[:index])
        self.groups = SIZES[index]
        self.half_groups = self.groups // 2
        self.half_tiles = self.half_groups * TILES
        self.quarter_tiles = self.half_tiles // 2
        self.half_rows = self.half_tiles * STATE
        self.quarter_rows = self.quarter_tiles * STATE
        self.width = self.groups * GROUP_COLS
        self.spans = (
            (self.first * GROUP_COLS, self.width),
            (INNER + self.first * STATE, self.groups * STATE),
        )


VMEM_LIMIT = 24 * 1024 * 1024
FLOPS, BYTES = 1e9, 3e6


def extra_rows(tiles):
    return -(-2 * tiles // 16) * 16


def decay_rows(tiles):
    return -(-tiles // 8) * 8


def call(body, outs, *args, after=(), hbm=(), cost=0.1, scratch=()):
    count = len(args)
    args = [pltpu.with_memory_space_constraint(a, pltpu.HBM) if i in hbm else a for i, a in enumerate(args)]
    specs = [pl.BlockSpec(memory_space=pltpu.HBM if i in hbm else pltpu.VMEM) for i in range(count)]
    specs += [pl.BlockSpec(memory_space=pl.ANY) for _ in after]

    def kernel(*refs):
        body(*refs[:count], *refs[count + len(after) :])

    return pl.pallas_call(
        kernel,
        out_shape=[space(shape, kind) for shape, kind, space in outs],
        in_specs=specs,
        out_specs=[pl.BlockSpec(memory_space=space) for _, _, space in outs],
        scratch_shapes=list(scratch),
        compiler_params=pltpu.CompilerParams(vmem_limit_bytes=VMEM_LIMIT),
        cost_estimate=pl.CostEstimate(flops=int(cost * FLOPS), bytes_accessed=int(cost * BYTES), transcendentals=0),
    )(*args, *after)


def vmem(rows, cols, kind):
    return ((rows, cols), kind, pltpu.VMEM)


def dot(a, b, dims=((1,), (0,))):
    return lax.dot_general(a, b, (dims, ((), ())), preferred_element_type=F32)


def silu(v):
    return silu_of_twice(0.5 * v)


def pieces(v, count):
    found = []
    for _ in range(count):
        piece = v.astype(BF16)
        found.append(piece)
        v = v - piece.astype(F32)
    return found


def columns(group, width, start=0):
    return pl.ds(pl.multiple_of(start + group * width, LANES), width)


def silu_of_twice(half):
    return half + half * jnp.tanh(half)


def halved_taps(weight, bias, cols):
    return 0.5 * weight[:, cols].astype(F32), 0.5 * bias[:, cols]


def convolve_into(rows, padded, weight, bias, cols):
    taps, total = halved_taps(weight, bias, cols)
    for tap in range(4):
        total = total + taps[tap : tap + 1] * padded[5 + tap : 5 + tap + rows, :]
    return silu_of_twice(total).astype(BF16)


def accurate_log1p(u):
    w = 1.0 + u
    return jnp.where(w == 1.0, u, jnp.log(w) * (u / jnp.where(w == 1.0, 1.0, w - 1.0)))


def convolve_body(source, weight, bias, spans, outs):
    for (start, width), out in zip(spans, outs):
        for i in range(width // LANES):
            cols = slice(start + i * LANES, start + (i + 1) * LANES)
            here = source[:, cols].astype(F32)
            taps, total = halved_taps(weight, bias, cols)
            total = total + taps[3:4] * here
            for back in range(1, 4):
                total = total + taps[3 - back : 4 - back] * pltpu.roll(here, back, 0)
            out[:, i * LANES : (i + 1) * LANES] = silu_of_twice(total).astype(BF16)


def convolve_head(source, halo, weight, bias, padded, spans, outs):
    first = lax.axis_index("seq") == 0
    for (start, width), out in zip(spans, outs):
        block = min(width, 512)

        @pl.loop(0, width // block)
        def _(i, start=start, out=out, block=block):
            cols = columns(i, block, start)
            here = padded.at[:, 0:block]
            here[0:8, :] = jnp.zeros((8, block), F32)
            here[5:8, :] = jnp.where(first, 0.0, halo[:, cols].astype(F32))
            here[8:24, :] = source[0:16, cols].astype(F32)
            out[0:16, columns(i, block)] = convolve_into(16, here, weight, bias, cols)


def prepare(
    parts, x, raw_t, step_bias, decay_log, skip, weight_in, bias_in,
    held, weight, bias, both, both_t, tail_pair, carry_pair, row_pair, spread, *refs,
):
    *outs, raw_here, small, sems = refs
    spans = [span for part in parts for span in part.spans]
    copies = [
        pltpu.make_async_copy(raw_t, raw_here, sems.at[0]),
        pltpu.make_async_copy(step_bias, small.at[0:1], sems.at[1]),
        pltpu.make_async_copy(decay_log, small.at[8:9], sems.at[2]),
        pltpu.make_async_copy(skip, small.at[16:17], sems.at[3]),
        pltpu.make_async_copy(weight_in, weight, sems.at[4]),
        pltpu.make_async_copy(bias_in, bias, sems.at[5]),
    ]
    for i, (start, width) in enumerate(spans + [(INNER + KEYS, KEYS)]):
        cols = slice(start, start + width)
        copies.append(pltpu.make_async_copy(x.at[:, cols], held.at[:, cols], sems.at[6 + i]))
    for copy in copies:
        copy.start()
    channel = lax.broadcasted_iota(jnp.int32, (2 * HEADS, GROUP_COLS), 1)
    head = (lax.broadcasted_iota(jnp.int32, (2 * HEADS, GROUP_COLS), 0) & (HEADS - 1)) - channel // HEAD_DIM
    for group in range(GROUPS):
        spread[:, group * GROUP_COLS : (group + 1) * GROUP_COLS] = (head == group * PER_GROUP).astype(BF16)
    for copy in copies[:4]:
        copy.wait()
    raw = raw_here[...].astype(F32)
    raw = jnp.concatenate([raw, raw], axis=0).T[:, :HEADS] + small[0:1, :]
    sizes = jnp.maximum(raw, 0.0) + accurate_log1p(jnp.exp(-jnp.abs(raw)))
    log_decay = sizes * -jnp.exp(small[8:9, :])
    row = lax.broadcasted_iota(jnp.int32, (SPAN, SPAN), 0)
    lane = lax.broadcasted_iota(jnp.int32, (SPAN, SPAN), 1)
    lower = (row >= lane).astype(BF16)
    cumulative = sum(dot(lower, piece) for piece in pieces(log_decay, 3))
    total = cumulative[SPAN - 1 : SPAN, :]
    tail = jnp.exp(total - cumulative) * sizes
    joined = jnp.concatenate([cumulative, sizes], axis=1)
    both[...] = joined
    both_t[...] = joined.T
    tail_pair[...] = jnp.concatenate(pieces(tail, 2), axis=1)
    carry_pair[...] = jnp.concatenate(pieces(jnp.exp(cumulative), 2), axis=1)
    rows = jnp.concatenate(
        [jnp.broadcast_to(jnp.exp(total), (8, HEADS)), jnp.broadcast_to(small[16:17, :], (8, HEADS))], axis=0
    )
    row_pair[...] = jnp.concatenate(pieces(rows, 2), axis=1)
    for copy in copies[4:6]:
        copy.wait()
    for i, (span, out) in enumerate(zip(spans, outs)):
        copies[6 + i].wait()
        convolve_body(held, weight, bias, [span], [out])
    copies[-1].wait()


def convolve_reads(held, halo, weight, bias, reads, padded):
    spans = [(INNER + KEYS, KEYS)]
    convolve_body(held, weight, bias, spans, [reads])
    convolve_head(held, halo, weight, bias, padded, spans, [reads])


def put_decays(send, tiles, decays):
    high = [d.astype(BF16).astype(F32) for d in decays]
    low = [d - h for d, h in zip(decays, high)]
    rows = high + low
    spare = extra_rows(tiles) - len(rows)
    block = jnp.concatenate(rows + [jnp.zeros((spare, LANES), F32)] * (spare > 0), axis=0)
    send[tiles * STATE : tiles * STATE + extra_rows(tiles), :] = block.astype(BF16)


def increments(part, *refs):
    held, halo, weight, bias, raw_values, raw_keys = refs[:6]
    tail_pair, row_pair, spread, send, keep, keep_decay, values_ref, keys_ref = refs[6:14]
    scaled, padded, value_fix, key_fix = refs[14:]
    convolve_head(held, halo, weight, bias, padded, part.spans, (value_fix, key_fix))
    keys_ref[0:16, :] = key_fix[...]
    keys_ref[16:, :] = raw_keys[16:, :]
    core = lax.axis_index("seq") & 1
    targets = ((send, 1 - core), (keep, core))
    order = [(target, side * part.half_groups + j, j) for target, side in targets for j in range(part.half_groups)]
    for i, (_, local, _) in enumerate(order):
        cols = columns(local, GROUP_COLS)
        scale = dot(tail_pair[...], spread[:, columns(part.first + local, GROUP_COLS)])
        values = jnp.concatenate([value_fix[:, cols], raw_values[16:, cols]], axis=0)
        values_ref[:, cols] = values
        scaled[i] = (values.astype(F32) * scale).astype(BF16)
    for target, side in targets:
        decay = dot(
            row_pair[...],
            spread[:, columns((part.first + side * part.half_groups) // part.half_groups, part.width // 2)],
        )
        decays = [decay[0:1, t * LANES : (t + 1) * LANES] for t in range(part.half_tiles)]
        if target is send:
            put_decays(send, part.half_tiles, decays)
        else:
            for t, d in enumerate(decays):
                keep_decay[t : t + 1, :] = d
    for i, (target, local, j) in enumerate(order):
        grown = dot(keys_ref[:, columns(local, STATE)], scaled[i], ((0,), (0,)))
        for t in range(TILES):
            at = (j * TILES + t) * STATE
            target[at : at + STATE, :] = grown[:, t * LANES : (t + 1) * LANES].astype(target.dtype)


def tile_rows(t):
    return pl.ds(pl.multiple_of(t * STATE, STATE), STATE)


def received_decays(recv, tiles, scratch):
    rows = recv[tiles * STATE : tiles * STATE + extra_rows(tiles), :].astype(F32)
    scratch[0:tiles, :] = rows[0:tiles] + rows[tiles : 2 * tiles]


def join_cores(part, keep, keep_decay, recv, send, own, own_decay, other):
    me = lax.axis_index("seq")
    first = (me & 1) == 0
    y = (me >> 1) & 1
    received_decays(recv, part.half_tiles, other)

    def joined(t):
        mine, theirs = keep[tile_rows(t), :], recv[tile_rows(t), :].astype(F32)
        decay_mine, decay_theirs = keep_decay[pl.ds(t, 1), :], other[pl.ds(t, 1), :]
        early, late = jnp.where(first, mine, theirs), jnp.where(first, theirs, mine)
        return jnp.where(first, decay_theirs, decay_mine) * early + late, decay_mine * decay_theirs

    decays = []
    for t in range(part.quarter_tiles):
        state, decay = joined((1 - y) * part.quarter_tiles + t)
        send[t * STATE : (t + 1) * STATE, :] = state.astype(BF16)
        decays.append(decay)
    put_decays(send, part.quarter_tiles, decays)
    for t in range(part.quarter_tiles):
        state, decay = joined(y * part.quarter_tiles + t)
        own[t * STATE : (t + 1) * STATE, :] = state
        own_decay[t : t + 1, :] = decay


def join_pair(part, bit, carried, totals, *refs):
    state, decay, recv = refs[:3]
    refs = refs[3:]
    if carried:
        before, before_decay = refs[:2]
        refs = refs[2:]
    send = refs[0]
    refs = refs[1:]
    if totals:
        new_state, new_decay = refs[:2]
        refs = refs[2:]
    if bit >= 2:
        new_before, new_before_decay = refs[:2]
        refs = refs[2:]
    (other,) = refs
    upper = ((lax.axis_index("seq") >> bit) & 1) == 1
    received_decays(recv, part.quarter_tiles, other)
    decays = []
    for t in range(part.quarter_tiles):
        rows = slice(t * STATE, (t + 1) * STATE)
        mine, theirs = state[rows, :], recv[rows, :].astype(F32)
        d_mine, d_theirs = decay[t : t + 1, :], other[t : t + 1, :]
        early, late = jnp.where(upper, theirs, mine), jnp.where(upper, mine, theirs)
        total = jnp.where(upper, d_mine, d_theirs) * early + late
        send[rows, :] = total.astype(BF16)
        if totals:
            new_state[rows, :] = total
            new_decay[t : t + 1, :] = d_mine * d_theirs
        decays.append(d_mine * d_theirs)
        if bit >= 2:
            if carried:
                b, bd = before[rows, :], before_decay[t : t + 1, :]
                new_before[rows, :] = jnp.where(upper, b + bd * theirs, b)
                new_before_decay[t : t + 1, :] = jnp.where(upper, bd * d_theirs, bd)
            else:
                new_before[rows, :] = jnp.where(upper, theirs, 0.0)
                new_before_decay[t : t + 1, :] = jnp.where(upper, d_theirs, 1.0)
    if totals:
        put_decays(send, part.quarter_tiles, decays)


def to_planes(part, bit, carried, *refs):
    recv = refs[0]
    refs = refs[1:]
    if carried:
        before, before_decay = refs[:2]
        refs = refs[2:]
    own, own_decay, recv_pair, send, start, other = refs
    me = lax.axis_index("seq")
    upper = ((me >> bit) & 1) == 1
    y = ((me >> 1) & 1) == 1
    received_decays(recv_pair, part.quarter_tiles, other)
    for t in range(part.quarter_tiles):
        rows = slice(t * STATE, (t + 1) * STATE)
        theirs = recv[rows, :].astype(F32)
        if carried:
            b = before[rows, :]
            plane = jnp.where(upper, b + before_decay[t : t + 1, :] * theirs, b)
        else:
            plane = jnp.where(upper, theirs, 0.0)
        d = jnp.where(y, other[t : t + 1, :], own_decay[t : t + 1, :])
        grown = jnp.where(y, recv_pair[rows, :].astype(F32), own[rows, :])
        later = d * plane + grown
        send[rows, :] = jnp.where(y, plane, later).astype(BF16)
        start[rows, :] = jnp.where(y, later, plane)


def to_cores(part, start, recv_start, keep, keep_decay, recv, send, own, other):
    me = lax.axis_index("seq")
    first = (me & 1) == 0
    y = (me >> 1) & 1
    received_decays(recv, part.half_tiles, other)
    for side in range(2):
        for t in range(part.quarter_tiles):
            rows = slice(t * STATE, (t + 1) * STATE)
            at = (y if side == 0 else 1 - y) * part.quarter_tiles + t
            chip = start[rows, :] if side == 0 else recv_start[rows, :].astype(F32)
            d = jnp.where(first, keep_decay[pl.ds(at, 1), :], other[pl.ds(at, 1), :])
            grown = jnp.where(first, keep[tile_rows(at), :], recv[tile_rows(at), :].astype(F32))
            later = d * chip + grown
            send[tile_rows(at), :] = jnp.where(first, later, chip).astype(BF16)
            own[tile_rows(at), :] = jnp.where(first, chip, later).astype(BF16)


def inside(part, values_ref, keys_ref, reads_ref, both, both_t, carry_pair, row_pair, spread, gate, base, slope):
    row = lax.broadcasted_iota(jnp.int32, (SPAN, SPAN), 0)
    lane = lax.broadcasted_iota(jnp.int32, (SPAN, SPAN), 1)
    causal = row >= lane
    for j in range(part.groups):
        group = part.first + j
        cols = slice(j * GROUP_COLS, (j + 1) * GROUP_COLS)
        values = values_ref[:, cols]
        writes = keys_ref[:, j * STATE : (j + 1) * STATE]
        reads = reads_ref[:, group * STATE : (group + 1) * STATE]
        scores = dot(reads, writes, ((1,), (1,)))
        found = []
        for i in range(PER_GROUP):
            h = group * PER_GROUP + i
            gap = both[:, h : h + 1] - both_t[h : h + 1, :]
            weights = scores * jnp.exp(jnp.where(causal, gap, -jnp.inf)) * both_t[HEADS + h : HEADS + h + 1, :]
            found.append(dot(weights.astype(BF16), values[:, i * HEAD_DIM : (i + 1) * HEAD_DIM]))
        within = jnp.concatenate(found, axis=1)
        to_channels = spread[:, group * GROUP_COLS : (group + 1) * GROUP_COLS]
        skip = dot(row_pair[...], to_channels)[8:9, :]
        opened = silu(gate[:, group * GROUP_COLS : (group + 1) * GROUP_COLS].astype(F32))
        base[:, cols] = (within + skip * values.astype(F32)) * opened
        slope[:, cols] = dot(carry_pair[...], to_channels) * opened


def finish(part, mine, reads_ref, source, base, slope, gain, made):
    core = lax.axis_index("seq") & 1
    side = core if mine else 1 - core
    for j in range(part.half_groups):
        local = side * part.half_groups + j
        group = part.first + local
        cols = columns(local, GROUP_COLS)
        starts = jnp.concatenate(
            [source[(j * TILES + t) * STATE : (j * TILES + t + 1) * STATE, :] for t in range(TILES)], axis=1
        )
        gated = base[:, cols] + slope[:, cols] * dot(reads_ref[:, columns(group, STATE)], starts)
        mean = jnp.mean(gated * gated, axis=1, keepdims=True)
        normed = gated * lax.rsqrt(mean + 1e-5) * gain[:, columns(group, GROUP_COLS)]
        made[:, j * GROUP_COLS : (j + 1) * GROUP_COLS] = normed.astype(BF16)


def finish_last(part, others, *refs):
    count = len(others)
    arrays, out, made, sems = refs[:count], refs[-3], refs[-2], refs[-1]
    core = lax.axis_index("seq") & 1

    def copy_out(i, other, mine, array):
        group = other.first + (core if mine else 1 - core) * other.half_groups
        return pltpu.make_async_copy(
            array, out.at[:, pl.ds(pl.multiple_of(group * GROUP_COLS, GROUP_COLS), other.width // 2)], sems.at[i]
        )

    copies = [copy_out(i, *other, array) for i, (other, array) in enumerate(zip(others, arrays))]
    for copy in copies:
        copy.start()
    finish(part, False, *refs[count:-3], made)
    copies.append(copy_out(count, part, False, made))
    copies[-1].start()
    for copy in copies:
        copy.wait()


ORDER = (
    "I0", "I1", "A0", "A1", "B0", "R0", "W0", "B1", "C0", "C1", "W1", "S0", "S1",
    "H0", "H1", "E0", "F0", "E1", "F1",
)


def shards(mixer_input, gate_input, step_raw, conv_weight, conv_bias, step_bias, decay_log, skip_gain, norm_gain):
    devices = lax.axis_size("seq")
    bits = devices.bit_length() - 1
    parts = [Part(i) for i in range(len(SIZES))]

    def across(value, bit):
        flipped = 1 << bit if bit < 2 else (2 << bit) - 4
        return lax.ppermute(value, "seq", [(i, i ^ flipped) for i in range(devices)])

    padded = pltpu.VMEM((24, 512), F32)

    def decays_of(tiles):
        return vmem(decay_rows(tiles), LANES, F32)

    def decay_scratch(tiles):
        return [pltpu.VMEM((decay_rows(tiles), LANES), F32)]

    def rows_of(p):
        return [vmem(SPAN, p.width, BF16), vmem(SPAN, p.groups * STATE, BF16)]

    def half_send(p):
        return vmem(p.half_rows + extra_rows(p.half_tiles), LANES, BF16)

    def quarter_send(p):
        return vmem(p.quarter_rows + extra_rows(p.quarter_tiles), LANES, BF16)

    def quarter(p):
        return [vmem(p.quarter_rows, LANES, F32), decays_of(p.quarter_tiles)]

    halo = lax.ppermute(mixer_input[SPAN - 3 :], "seq", [(i, (i + 1) % devices) for i in range(devices)])
    held, weight, bias, both, both_t, tail_pair, carry_pair, row_pair, spread, *raw = call(
        functools.partial(prepare, parts),
        [
            vmem(SPAN, CONV_COLS, BF16),
            vmem(4, CONV_COLS, BF16),
            vmem(1, CONV_COLS, F32),
            vmem(SPAN, 2 * HEADS, F32),
            vmem(2 * HEADS, SPAN, F32),
            vmem(SPAN, 2 * HEADS, BF16),
            vmem(SPAN, 2 * HEADS, BF16),
            vmem(16, 2 * HEADS, BF16),
            vmem(2 * HEADS, INNER, BF16),
            *[shape for p in parts for shape in rows_of(p)],
        ],
        mixer_input, step_raw.T, step_bias[None, :], decay_log[None, :], skip_gain[None, :],
        conv_weight, conv_bias[None, :],
        hbm=range(7),
        cost=2.5,
        scratch=[
            pltpu.VMEM((HEADS, SPAN), BF16),
            pltpu.VMEM((24, HEADS), F32),
            pltpu.SemaphoreType.DMA((7 + 2 * len(parts),)),
        ],
    )
    gain = norm_gain[None, :]
    have = {}
    token = ()
    results = []
    for stage in ORDER:
        kind, p = stage[0], parts[int(stage[1:])]
        n = p.index
        get = lambda name: have[name, n]

        def put(**values):
            have.update({(name, n): value for name, value in values.items()})

        if kind == "R":
            (reads,) = call(
                convolve_reads, [vmem(SPAN, KEYS, BF16)], held, halo, weight, bias,
                after=token, cost=0.6, scratch=[padded],
            )
            token = (reads,)
        elif kind == "I":
            send, keep, keep_decay, values, keys = call(
                functools.partial(increments, p),
                [half_send(p), vmem(p.half_rows, LANES, F32), decays_of(p.half_tiles), *rows_of(p)],
                held, halo, weight, bias, *raw[2 * n : 2 * n + 2], tail_pair, row_pair, spread,
                after=token, cost=0.2 * p.groups,
                scratch=[
                    pltpu.VMEM((p.groups, SPAN, GROUP_COLS), BF16),
                    padded,
                    pltpu.VMEM((16, p.width), BF16),
                    pltpu.VMEM((16, p.groups * STATE), BF16),
                ],
            )
            put(values=values, keys=keys, kept=(keep, keep_decay, across(send, 0)))
            token = (keep_decay,)
        elif kind == "A":
            send, own, own_decay = call(
                functools.partial(join_cores, p), [quarter_send(p), *quarter(p)], *get("kept"),
                after=token, scratch=decay_scratch(p.half_tiles),
            )
            put(own=(own, own_decay, across(send, 1)), bit=1, carried=())
            have["state", n] = have["own", n]
            token = (own_decay,)
        elif kind in "BC":
            for bit in range(1, 2) if kind == "B" else range(2, bits - 1):
                totals, carried = bit + 1 < bits - 1, get("carried")
                outs = call(
                    functools.partial(join_pair, p, bit, bool(carried), totals),
                    [quarter_send(p) if totals else vmem(p.quarter_rows, LANES, BF16)] + quarter(p) * totals + quarter(p) * (bit >= 2),
                    *get("state"), *carried, after=token, scratch=decay_scratch(p.quarter_tiles),
                )
                recv = across(outs[0], bit + 1)
                put(
                    state=(*(outs[1:3] if totals else (None, None)), recv),
                    carried=tuple(outs[-2:]) if bit >= 2 else (),
                )
                token = (outs[-1],) if len(outs) > 1 else (outs[0],)
        elif kind == "S":
            send, start = call(
                functools.partial(to_planes, p, bits - 1, bool(get("carried"))),
                [vmem(p.quarter_rows, LANES, BF16), quarter(p)[0]],
                get("state")[2], *get("carried"), *get("own"),
                after=token, scratch=decay_scratch(p.quarter_tiles),
            )
            put(start=(start, across(send, 1)))
            token = (start,)
        elif kind == "H":
            send, own_start = call(
                functools.partial(to_cores, p), [vmem(p.half_rows, LANES, BF16)] * 2, *get("start"), *get("kept"),
                after=token, scratch=decay_scratch(p.half_tiles),
            )
            put(own_start=own_start, recv_start=across(send, 0))
            token = (own_start,)
        elif kind == "W":
            put(
                mixed=call(
                    functools.partial(inside, p), [vmem(SPAN, p.width, F32)] * 2,
                    get("values"), get("keys"), reads, both, both_t, carry_pair, row_pair, spread, gate_input,
                    after=token, cost=0.42 * p.groups,
                )
            )
            token = (get("mixed")[0],)
        elif kind in "EF" and len(results) < 2 * len(SIZES) - 1:
            name = "own_start" if kind == "E" else "recv_start"
            (made,) = call(
                functools.partial(finish, p, kind == "E"), [vmem(SPAN, p.width // 2, BF16)],
                reads, get(name), *get("mixed"), gain, after=token, cost=0.2 * p.half_groups,
            )
            results.append(((p, kind == "E"), made))
            token = (made,)
        else:
            (out,) = call(
                functools.partial(finish_last, p, [where for where, _ in results]),
                [((SPAN, INNER), BF16, pltpu.HBM)],
                *[made for _, made in results], reads, get("recv_start"), *get("mixed"), gain,
                after=token, cost=0.2 * p.half_groups,
                scratch=[pltpu.VMEM((SPAN, p.width // 2), BF16), pltpu.SemaphoreType.DMA((2 * len(SIZES),))],
            )
    return out


def solution(mesh):
    in_specs = (
        P(("groups", "seq"), None),
        P(("groups", "seq"), None),
        P(("groups", "seq"), None),
        P(),
        P(),
        P("groups"),
        P("groups"),
        P(),
        P(),
    )
    return jax.shard_map(
        shards, mesh=mesh, in_specs=in_specs, out_specs=P(("groups", "seq"), None), check_vma=False
    )
```
